32 devices in a mesh: dp: 8 (over z, x), mp: 4 (over y, core).
Axes of the slice: x: 2, y: 2, z: 4, core: 2. Of those that a mesh axis runs over, the one named last changes fastest.
Arguments:
- inputs: bfloat16 [24576, 512], P(('dp', 'mp')), may hold values from -6 to 6
- gate_weight: bfloat16 [2, 3, 512, 1024], P(None, None, 'dp', 'mp'), may hold values from -0.25 to 0.25
- gate_bias: bfloat16 [2, 3, 1024], P(None, None, ('mp', 'dp')), may hold values from -9 to 4, as said below
- out_weight: bfloat16 [2, 1024, 512], P(None, 'mp', 'dp'), may hold values from -0.1875 to 0.1875
- norm_gain_one: bfloat16 [2, 512], P(None, ('dp', 'mp')), may hold values from 0.5 to 1.5
- norm_gain_two: bfloat16 [2, 512], P(None, ('dp', 'mp')), may hold values from 0.5 to 1.5
- up_weight: bfloat16 [2, 512, 2048], P(None, ('dp', 'mp')), may hold values from -0.25 to 0.25
- down_weight: bfloat16 [2, 2048, 512], P(None, ('dp', 'mp')), may hold values from -0.125 to 0.125
- cotangent: bfloat16 [24576, 512], P(('dp', 'mp')), may hold values from -6 to 6
Outputs:
- output: bfloat16 [24576, 512], P(('dp', 'mp'))
- input_grad: float32 [24576, 512], P(('dp', 'mp'))
- gate_weight_grad: float32 [2, 3, 512, 1024], P(None, None, 'dp', 'mp')
- gate_bias_grad: float32 [2, 3, 1024], P(None, None, ('mp', 'dp'))
- out_weight_grad: float32 [2, 1024, 512], P(None, 'mp', 'dp')
- gain_one_grad: float32 [2, 512], P(None, ('dp', 'mp'))
- gain_two_grad: float32 [2, 512], P(None, ('dp', 'mp'))
- up_weight_grad: float32 [2, 512, 2048], P(None, ('dp', 'mp'))
- down_weight_grad: float32 [2, 2048, 512], P(None, ('dp', 'mp'))
The draws below stay inside these ranges and needn't reach their ends.
Inputs may be any that keep to these rules, and one draw needn't show every extreme that they name: `gate_bias`: along the second dimension: forget, input and candidate biases.
All inputs are finite; a program needn't handle non-finite values.
Results may differ from the reference program's by a relative error of at most 0.017.
Values may be sent and summed in bfloat16 or wider, within the bound.
A program may use at most 192 MiB of HBM per device.

```python
import jax
import jax.numpy as jnp
from jax import lax

D = 512
FF = 1024
FF2 = 2048
LENGTH = 1024
LAYERS = 2
TOKENS = 24576


def draw_gate_bias(key, part):
    key = jax.random.fold_in(key, 7)
    key_forget, key_input, key_cand = jax.random.split(key, 3)
    shape = (LAYERS, 1, FF)
    forget = jax.random.uniform(key_forget, shape, jnp.float32, 0.0, 3.0)
    keeper = jax.random.uniform(key_input, shape, jnp.float32, -9.0, 0.0)
    cand = jnp.clip(1.5 * jax.random.normal(key_cand, shape, jnp.float32), -4.0, 4.0)
    return jnp.concatenate([forget, keeper, cand], axis=1).astype(jnp.bfloat16)


def shard_levels(key, shape, cuts, low, top_value):
    def one(axis_at, parts):
        heights = jax.random.uniform(jax.random.fold_in(jax.random.fold_in(key, 6), axis_at), (parts,), jnp.float32, low / len(cuts), top_value / len(cuts))
        return jnp.repeat(jnp.exp(heights), shape[axis_at] // parts).reshape((-1,) + (1,) * (len(shape) - axis_at - 1))

    level = one(*cuts[0])
    for cut in cuts[1:]:
        level = level * one(*cut)
    return level


def normal_values(own_key, dims, deviation, limit, cuts=(), kind=jnp.bfloat16):
    array = jax.random.normal(own_key, dims, jnp.float32) * deviation
    if len(cuts) > 0:
        array = shard_levels(own_key, dims, cuts, -0.22, 0.18) * array
    return jnp.clip(array, min=-limit, max=limit).astype(kind)


def setup_inputs(seed: int = 0) -> dict:
    arg_keys = jax.random.split(jax.random.key(seed), 10)
    inputs = normal_values(arg_keys[0], (TOKENS, D), 1.0, 6.0, ((0, 32),))
    gate_weight = normal_values(arg_keys[1], (LAYERS, 3, D, FF), D ** -0.5, 0.25, ((2, 8), (3, 4)))
    gate_bias = draw_gate_bias(jax.random.fold_in(arg_keys[9], 71), 0)
    out_weight = normal_values(arg_keys[3], (LAYERS, FF, D), FF ** -0.5, 0.1875, ((1, 4), (2, 8)))
    norm_gain_one = jnp.clip(1.0 + 0.1 * jax.random.normal(arg_keys[4], (LAYERS, D), jnp.float32), 0.5, 1.5).astype(jnp.bfloat16)
    norm_gain_two = jnp.clip(1.0 + 0.1 * jax.random.normal(arg_keys[5], (LAYERS, D), jnp.float32), 0.5, 1.5).astype(jnp.bfloat16)
    up_weight = normal_values(arg_keys[6], (LAYERS, D, FF2), D ** -0.5, 0.25, ((1, 32),))
    down_weight = normal_values(arg_keys[7], (LAYERS, FF2, D), FF2 ** -0.5, 0.125, ((1, 32),))
    cotangent = normal_values(arg_keys[8], (TOKENS, D), 1.0, 6.0, ((0, 32),))
    return dict(inputs=inputs, gate_weight=gate_weight, gate_bias=gate_bias, out_weight=out_weight, norm_gain_one=norm_gain_one, norm_gain_two=norm_gain_two, up_weight=up_weight, down_weight=down_weight, cotangent=cotangent)


@jax.custom_vjp
def low(v):
    return lax.optimization_barrier(v.astype(jnp.bfloat16)).astype(jnp.float32)

@jax.custom_vjp
def low_back(v):
    return v

def low_keep(v):
    return (low(v), None)

def low_pass(kept, grad):
    return (grad,)

def back_keep(v):
    return (v, None)

def back_low(kept, grad):
    return (low(grad),)
low.defvjp(low_keep, low_pass)
low_back.defvjp(back_keep, back_low)
eps = 1e-06

def rms_scale(values, gain):
    return values * lax.rsqrt(lax.optimization_barrier(jnp.mean(values * values, axis=-1, keepdims=True)) + eps) * gain

def link(earlier, later):
    return (earlier[0] * later[0], later[0] * earlier[1] + later[1])

def gate_terms(pre_forget, pre_input, pre_cand, starts):
    sig_forget = jax.nn.sigmoid(pre_forget)
    sig_input = jax.nn.sigmoid(pre_input)
    total = sig_forget + sig_input
    decay = jnp.where(starts, 0.0, sig_forget / total)
    return (decay, sig_input / total * pre_cand)

def block(stream, gates, biases, out_w, gain_first, gain_second, up_w, down_w, starts):
    highest = lax.Precision.HIGHEST
    normed = low(rms_scale(stream, gain_first))
    pre_list = [low_back(jnp.dot(normed, gates[index], precision=highest) + biases[index]) for index in range(3)]
    decay, drive = gate_terms(pre_list[0], pre_list[1], pre_list[2], starts)
    width = decay.shape[1]
    decay = decay.reshape(-1, LENGTH, width)
    drive = drive.reshape(-1, LENGTH, width)
    products, states = lax.associative_scan(link, (decay, drive), axis=1)
    hidden = low(states.reshape(-1, width))
    mixed = stream + low_back(jnp.dot(hidden, out_w, precision=highest))
    second = low(rms_scale(mixed, gain_second))
    up_acts = low_back(jnp.dot(second, up_w, precision=highest))
    activated = low(jax.nn.gelu(up_acts))
    return mixed + low_back(jnp.dot(activated, down_w, precision=highest))

def reference(inputs, gate_weight, gate_bias, out_weight, norm_gain_one, norm_gain_two, up_weight, down_weight, cotangent):
    starts = (jnp.arange(TOKENS, dtype=jnp.int32) % LENGTH == 0)[:, None]
    params = tuple((item.astype(jnp.float32) for item in (gate_weight, gate_bias, out_weight, norm_gain_one, norm_gain_two, up_weight, down_weight)))

    def forward(stream, gates, biases, out_w, gain_a, gain_b, up_w, down_w):
        for layer_no in range(LAYERS):
            stream = block(stream, gates[layer_no], biases[layer_no], out_w[layer_no], gain_a[layer_no], gain_b[layer_no], up_w[layer_no], down_w[layer_no], starts)
        return stream
    result, backward = jax.vjp(forward, inputs.astype(jnp.float32), *params)
    grads = backward(cotangent.astype(jnp.float32))
    return (result.astype(jnp.bfloat16), grads[0], grads[1], grads[2], grads[3], grads[4], grads[5], grads[6], grads[7])
```

```python
from functools import partial

import jax
import jax.numpy as jnp
from jax import lax
from jax.experimental import pallas as pl
from jax.experimental.pallas import tpu as pltpu
from jax.sharding import PartitionSpec as P

LENGTH = 1024


eps = 1e-06


def cut_along(x, dim, size):
    shape = x.shape
    blocks = x.reshape(*shape[:dim], size, shape[dim] // size, *shape[dim + 1 :])
    return jnp.moveaxis(blocks, dim, 0)


def sum_at_owner(x, axis, dim):
    size = lax.axis_size(axis)
    blocks = lax.all_to_all(cut_along(x, dim, size), axis, 0, 0, tiled=True)
    return jnp.sum(blocks.astype(jnp.float32), axis=0)


def rms_scale(values, gain):
    return values * lax.rsqrt(jnp.mean(values * values, axis=-1, keepdims=True) + eps) * gain


def link(earlier, later):
    return (earlier[0] * later[0], later[0] * earlier[1] + later[1])


def gate_terms(pre_acts, starts):
    sig_forget = jax.nn.sigmoid(pre_acts[0])
    sig_input = jax.nn.sigmoid(pre_acts[1])
    total = sig_forget + sig_input
    decay = jnp.where(starts, 0.0, sig_forget / total)
    return (decay, sig_input / total * pre_acts[2])


def dot_plain(left, right):
    return jnp.dot(left, right, preferred_element_type=jnp.float32)


def dot_first(left, right):
    return lax.dot_general(
        left, right, (((0,), (0,)), ((), ())), preferred_element_type=jnp.float32
    )


def dot_last(left, right):
    return lax.dot_general(
        left, right, (((1,), (1,)), ((), ())), preferred_element_type=jnp.float32
    )


ALL = slice(None)
MESH = pl.DeviceIdType.MESH
BF = jnp.bfloat16
F32 = jnp.float32
SHIFT = 0.25
LOG_SHIFT = -1.3862943611198906
TOP = 87.0
GELU_A = 0.7978845608028654
GELU_B = 0.044715
ROWS = 256


def place():
    dp = lax.axis_index("dp")
    mp = lax.axis_index("mp")
    return (lax.div(dp, 2), lax.rem(dp, 2), lax.div(mp, 2), lax.rem(mp, 2))


def device(z, x, y, c):
    return (z * 2 + x, y * 2 + c)


def greet():
    z, x, y, c = place()
    partners = [device(lax.rem(z + k, 4), x, y, c) for k in (1, 2, 3)]
    partners += [device(z, 1 - x, y, c), device(z, x, 1 - y, c)]
    partners += [device(z, x, y, 1 - c), device(z, x, 1 - y, 1 - c)]
    barrier = pltpu.get_barrier_semaphore()
    for partner in partners:
        pl.semaphore_signal(barrier, inc=1, device_id=partner, device_id_type=MESH)
    pl.semaphore_wait(barrier, len(partners))


class Gather:
    def __init__(self, bufs, send, recv):
        self.bufs = bufs
        self.send = send
        self.recv = recv
        self.at = place()
        self.sent = []

    def view(self, item, z, x, y, c, h):
        kind, l = item
        w4, up, dn, vec = self.bufs
        if kind == "vec":
            return vec.at[z, x, y, c, h]
        if kind == "gate":
            return w4.at[l, y, c, pl.ds(0, 3), z, x, h]
        if kind == "out":
            return w4.at[l, y, c, 3, z, x, h]
        if kind == "up":
            return up.at[l, h, z, x, y, c]
        return dn.at[l, z, x, y, c, h]

    def go(self, n, slot, ref, target):
        cp = pltpu.make_async_remote_copy(
            src_ref=ref,
            dst_ref=ref,
            send_sem=self.send.at[n, slot],
            recv_sem=self.recv.at[n, slot],
            device_id=target,
            device_id_type=MESH,
        )
        cp.start()
        self.sent.append(cp)

    def landed(self, n, slot, ref, source):
        pltpu.make_async_remote_copy(
            src_ref=ref,
            dst_ref=ref,
            send_sem=self.send.at[n, slot],
            recv_sem=self.recv.at[n, slot],
            device_id=source,
            device_id_type=MESH,
        ).wait_recv()

    def stage(self, step, n, item):
        z, x, y, c = self.at
        v = lambda *where: self.view(item, *where)
        to_x = device(z, 1 - x, y, c)
        to_y = device(z, x, 1 - y, c)
        to_c = device(z, x, y, 1 - c)
        if step == 0:
            for k in (1, 2, 3):
                self.go(n, k - 1, v(z, x, y, c, ALL), device(lax.rem(z + k, 4), x, y, c))
        elif step == 1:
            for k in (1, 2, 3):
                source = lax.rem(z + 4 - k, 4)
                self.landed(n, k - 1, v(source, x, y, c, ALL), device(source, x, y, c))
            self.go(n, 3, v(ALL, x, y, c, 0), to_x)
            self.go(n, 4, v(ALL, x, y, c, 1), to_y)
            self.go(n, 7, v(ALL, x, y, c, ALL), to_c)
        elif step == 2:
            self.landed(n, 3, v(ALL, 1 - x, y, c, 0), to_x)
            self.go(n, 5, v(ALL, ALL, y, c, 0), to_y)
            self.landed(n, 4, v(ALL, x, 1 - y, c, 1), to_y)
            self.go(n, 6, v(ALL, x, ALL, c, 1), to_x)
            self.go(n, 8, v(ALL, 1 - x, y, c, 0), to_c)
            self.go(n, 9, v(ALL, x, 1 - y, c, 1), to_c)
        elif step == 3:
            self.landed(n, 5, v(ALL, ALL, 1 - y, c, 0), to_y)
            self.go(n, 10, v(ALL, ALL, 1 - y, c, 0), to_c)
            self.landed(n, 6, v(ALL, 1 - x, ALL, c, 1), to_x)
            self.go(n, 11, v(ALL, 1 - x, ALL, c, 1), to_c)
        else:
            self.landed(n, 7, v(ALL, x, y, 1 - c, ALL), to_c)
            self.landed(n, 8, v(ALL, 1 - x, y, 1 - c, 0), to_c)
            self.landed(n, 9, v(ALL, x, 1 - y, 1 - c, 1), to_c)
            self.landed(n, 10, v(ALL, ALL, 1 - y, 1 - c, 0), to_c)
            self.landed(n, 11, v(ALL, 1 - x, ALL, 1 - c, 1), to_c)

    def finish(self):
        for cp in self.sent:
            cp.wait_send()


def dot(a, b):
    return jnp.dot(a, b, preferred_element_type=F32)


def dot_nt(a, b):
    return lax.dot_general(a, b, (((1,), (1,)), ((), ())), preferred_element_type=F32)


def dot_tn(a, b):
    return lax.dot_general(a, b, (((0,), (0,)), ((), ())), preferred_element_type=F32)


def spread(vec, l, first, size, total, per_mp):
    rows = vec[:, :, :, :, l].reshape(256, 128).astype(BF)
    j = lax.broadcasted_iota(jnp.int32, (128, total), 0)
    d = lax.broadcasted_iota(jnp.int32, (128, total), 1)
    pick = jnp.where(j == first + lax.rem(d, size), 1.0, 0.0).astype(BF)
    wide = dot(rows, pick)
    r = lax.div(lax.broadcasted_iota(jnp.int32, (256, total), 0), 8)
    d = lax.broadcasted_iota(jnp.int32, (256, total), 1)
    if per_mp:
        owner = lax.div(lax.rem(d, total // 4), size) * 4 + lax.div(d, total // 4)
    else:
        owner = lax.div(d, size)
    return jnp.sum(jnp.where(r == owner, wide, 0.0), axis=0, keepdims=True)


def combine(a, b, row, sign):
    for s in (1, 2, 4):
        keep = (row >= s) if sign > 0 else (row < 8 - s)
        by = s if sign > 0 else 8 - s
        am = jnp.where(keep, a, 0.0)
        b = b + am * pltpu.roll(b, by, 0)
        if s < 4:
            a = jnp.where(keep, a * pltpu.roll(a, by, 0), a)
        else:
            a = jnp.where(keep, a * pltpu.roll(a, by, 0), a)
    return a, b


def fwd_kernel(
    x_in, gate_in, out_in, up_in, down_in, vec_in,
    out_hbm, w4_hbm, up_hbm, dn_hbm, gain_hbm, stream_hbm, mixed_hbm, keep_hbm, q_hbm, hid_hbm, ff_hbm,
    w4, up, dn, vec, normed, stream, mixed, acc, keep, drive, c3, hid, ff, bias, gain, c_out, c_in,
    ag_send, ag_recv, own_sem, spill_sem, carry_send, carry_recv,
):
    z, x, y, c = place()
    mp = y * 2 + c
    rows_all = normed.shape[0]
    chunks = rows_all // ROWS
    fill = []

    def local(src, dst, sem):
        cp = pltpu.make_async_copy(src, dst, sem)
        cp.start()
        return cp

    own = {}
    n_own = 0

    def add_own(key, src, dst):
        nonlocal n_own
        own.setdefault(key, []).append(local(src, dst, own_sem.at[n_own]))
        n_own += 1

    add_own(("vec", 0), vec_in, vec.at[z, x, y, c])
    for l in range(2):
        add_own(("gate", l), gate_in.at[l], w4.at[l, y, c, pl.ds(0, 3), z, x])
        add_own(("out", l), out_in.at[l], w4.at[l, y, c, pl.ds(3, 1), z, x])
        for h in range(2):
            add_own(("up", l), up_in.at[l, :, pl.ds(h * 1024, 1024)], up.at[l, h, z, x, y, c])
        add_own(("down", l), down_in.at[l], dn.at[l, z, x, y, c])
    x_copy = local(x_in, normed, own_sem.at[n_own])
    greet()
    gather = Gather((w4, up, dn, vec), ag_send, ag_recv)
    items = [
        [("vec", 0), ("gate", 0)], [("out", 0)], [("up", 0)], [("down", 0)],
        [("gate", 1)], [("out", 1)], [("up", 1)], [("down", 1)],
    ]
    number = {}
    for group in items:
        for item in group:
            number[item] = len(number)

    def tick(t):
        for step in (0, 4, 3, 2, 1):
            if 0 <= t - step < len(items):
                for item in items[t - step]:
                    if step == 0:
                        for cp in own[item]:
                            cp.wait()
                    gather.stage(step, number[item], item)

    n_spill = 0
    spills = {}

    def spill(key, src, dst):
        nonlocal n_spill
        spills[key] = local(src, dst, spill_sem.at[n_spill])
        n_spill += 1

    def settle(key):
        if key in spills:
            spills.pop(key).wait()

    def rms(src, dst, g):
        @pl.loop(0, chunks)
        def _(i):
            r = pl.ds(pl.multiple_of(i * ROWS, ROWS), ROWS)
            v = src[r, :]
            scale = lax.rsqrt(jnp.mean(v * v, axis=-1, keepdims=True) + eps)
            dst[r, :] = (v * scale * g).astype(BF)

    def gate_panel(l, p):
        w = [w4[l, p // 2, p % 2, k].reshape(512, 256) for k in range(3)]
        bs = [bias[l, k : k + 1, p * 256 : (p + 1) * 256] for k in range(3)]

        @pl.loop(0, chunks)
        def _(i):
            r = pl.ds(pl.multiple_of(i * ROWS, ROWS), ROWS)
            n = normed[r, :]
            f, inp, cand = [dot(n, w[k]) + bs[k] for k in range(3)]
            e_f = jnp.exp(jnp.minimum(-f, TOP) + LOG_SHIFT)
            e_i = jnp.exp(jnp.minimum(-inp, TOP) + LOG_SHIFT)
            a_f = e_f + SHIFT
            a_i = e_i + SHIFT
            total = a_f + a_i
            inv = pl.reciprocal(total, approx=True)
            inv = inv * (2.0 - total * inv)
            share = a_f * inv
            decay = a_i * inv
            keep[p, r, :] = share
            drive[p, r, :] = share * cand
            c3[p, 0, r, :] = (decay * (e_f * inv)).astype(BF)
            c3[p, 1, r, :] = (share * (e_i * inv)).astype(BF)
            c3[p, 2, r, :] = cand.astype(BF)

    row = lax.broadcasted_iota(jnp.int32, (8, 256), 0)

    def scan(lo, hi, carry):
        def body(g, carry):
            r = pl.ds(pl.multiple_of(g * 16, 16), 16)
            after = []
            for p in range(4):
                s_prev = carry[p]
                share = keep[p, r, :]
                b16 = drive[p, r, :]
                states = []
                before = []
                for half in range(2):
                    part = slice(half * 8, half * 8 + 8)
                    a, b = combine(1.0 - share[part], b16[part], row, 1)
                    last = jnp.broadcast_to(s_prev[7:8, :], (8, 256))
                    s = b + a * last
                    before.append(jnp.where(row == 0, last, pltpu.roll(s, 1, 0)))
                    states.append(s)
                    s_prev = s
                after.append(s_prev)
                s16 = jnp.concatenate(states, axis=0)
                gap = jnp.concatenate(before, axis=0) - c3[p, 2, r, :].astype(F32)
                hid[p, r, :] = s16.astype(BF)
                c3[p, 0, r, :] = (gap * c3[p, 0, r, :].astype(F32)).astype(BF)
                c3[p, 1, r, :] = (-gap * c3[p, 1, r, :].astype(F32)).astype(BF)
            return tuple(after)

        return lax.fori_loop(lo, hi, body, carry)

    start_row = jnp.minimum(lax.rem(mp * (LENGTH - rows_all), LENGTH), rows_all)
    start = lax.div(start_row, 16)
    groups = rows_all // 16

    def carry_copy(l, to_y, to_c):
        return pltpu.make_async_remote_copy(
            src_ref=c_out.at[l],
            dst_ref=c_in.at[l],
            send_sem=carry_send.at[l],
            recv_sem=carry_recv.at[l],
            device_id=device(z, x, to_y, to_c),
            device_id_type=MESH,
        )

    def scan_tail(l):
        zero = jnp.zeros((8, 256), F32)
        end = scan(start, groups, (zero,) * 4)
        for p in range(4):
            c_out[l, :, p * 256 : (p + 1) * 256] = end[p]
        after = jnp.minimum(mp + 1, 3)

        @pl.when(mp < 3)
        def _():
            carry_copy(l, lax.div(after, 2), lax.rem(after, 2)).start()

    def scan_head(l):
        before = jnp.maximum(mp - 1, 0)

        @pl.when(mp > 0)
        def _():
            carry_copy(l, lax.div(before, 2), lax.rem(before, 2)).wait_recv()
            scan(0, start, tuple(c_in[l, :, p * 256 : (p + 1) * 256] for p in range(4)))

        after = jnp.minimum(mp + 1, 3)

        @pl.when(mp < 3)
        def _():
            carry_copy(l, lax.div(after, 2), lax.rem(after, 2)).wait_send()

    def project(l):
        g = gain[l, 1:2, :]
        w = [w4[l, p // 2, p % 2, 3].reshape(512, 256) for p in range(4)]

        @pl.loop(0, chunks)
        def _(i):
            r = pl.ds(pl.multiple_of(i * ROWS, ROWS), ROWS)
            v = stream[r, :]
            for p in range(4):
                v = v + dot_nt(hid[p, r, :], w[p])
            mixed[r, :] = v
            scale = lax.rsqrt(jnp.mean(v * v, axis=-1, keepdims=True) + eps)
            normed[r, :] = (v * scale * g).astype(BF)

    def feed(l, q):
        w_up = up[l, q // 2].reshape(512, 1024)[:, (q % 2) * 512 : (q % 2) * 512 + 512]
        w_down = dn[l, q].reshape(512, 512)

        @pl.loop(0, chunks)
        def _(i):
            r = pl.ds(pl.multiple_of(i * ROWS, ROWS), ROWS)
            u = dot(normed[r, :], w_up)
            sq = u * u
            t = jnp.tanh(u * (GELU_A + (GELU_A * GELU_B) * sq))
            gate = 0.5 + 0.5 * t
            act = (u * gate).astype(BF)
            slope = gate + (0.5 * u) * (1.0 - t * t) * (GELU_A + (3.0 * GELU_A * GELU_B) * sq)
            for half in range(2):
                side = slice(half * 256, half * 256 + 256)
                ff[q, half, r, :] = slope[:, side].astype(BF)
                ff[q, 2 + half, r, :] = act[:, side]
            base = mixed[r, :] if q == 0 else stream[r, :]
            stream[r, :] = base + dot(act, w_down)

    for t in range(5):
        tick(t)
    for l in range(2):
        gain[l, 0:1, :] = spread(vec, l, 0, 16, 512, False)
        gain[l, 1:2, :] = spread(vec, l, 16, 16, 512, False)
        for k in range(3):
            bias[l, k : k + 1, :] = spread(vec, l, 32 + 32 * k, 32, 1024, True)
    x_copy.wait()

    @pl.loop(0, chunks)
    def _(i):
        r = pl.ds(pl.multiple_of(i * ROWS, ROWS), ROWS)
        stream[r, :] = normed[r, :].astype(F32)

    def save_weights(kinds, l):
        if "w4" in kinds:
            spill(("w4", l), w4.at[l], w4_hbm.at[l])
        if "up" in kinds:
            spill(("up", l), up.at[l], up_hbm.at[l])
        if "dn" in kinds:
            spill(("dn", l), dn.at[l], dn_hbm.at[l])

    spill("gain", gain, gain_hbm)
    for l in range(2):
        settle("ff")
        rms(stream, normed, gain[l, 0:1, :])
        if l == 1:
            settle(("keep", 0))
            settle(("q", 0))
            spill("stream", stream, stream_hbm)
        gate_panel(l, 0)
        gate_panel(l, 1)
        tick(5 + 4 * l)
        save_weights(("w4",), l)
        gate_panel(l, 2)
        gate_panel(l, 3)
        settle(("hid", 0))
        scan_tail(l)
        spill(("keep", l), keep, keep_hbm.at[l])
        tick(6 + 4 * l)
        scan_head(l)
        spill(("q", l), c3.at[:, pl.ds(0, 2)], q_hbm.at[l])
        spill(("hid", l), hid, hid_hbm.at[l])
        settle(("mixed", 0))
        project(l)
        spill(("mixed", l), mixed, mixed_hbm.at[l])
        tick(7 + 4 * l)
        save_weights(("up", "dn"), l)
        settle("stream")
        for q in range(4):
            settle(("ff", 0, q))
            feed(l, q)
            spill(("ff", l, q), ff.at[q], ff_hbm.at[l, q])
        if l == 0:
            tick(8)

    @pl.loop(0, chunks)
    def _(i):
        r = pl.ds(pl.multiple_of(i * ROWS, ROWS), ROWS)
        normed[r, :] = stream[r, :].astype(BF)

    spill("result", normed, out_hbm)
    for key in list(spills):
        settle(key)
    gather.finish()


def forward(x, gate_weight, gate_bias, out_weight, gain_one, gain_two, up_weight, down_weight):
    rows = x.shape[0]
    any_space = pl.BlockSpec(memory_space=pl.ANY)
    packed = jnp.concatenate([gain_one, gain_two, gate_bias.reshape(2, 96)], axis=1).astype(F32)
    vec = jnp.pad(packed[:, None, :], ((0, 0), (0, 7), (0, 0)))
    args = (
        x,
        gate_weight.reshape(2, 3, 2, 32, 256),
        out_weight.transpose(0, 2, 1).reshape(2, 1, 2, 32, 256),
        up_weight,
        down_weight.reshape(2, 2, 32, 512),
        vec,
    )
    s = jax.ShapeDtypeStruct
    w4 = (2, 2, 2, 4, 4, 2, 2, 32, 256)
    up = (2, 2, 4, 2, 2, 2, 16, 1024)
    dn = (2, 4, 2, 2, 2, 2, 32, 512)
    dma = pltpu.SemaphoreType.DMA
    return pl.pallas_call(
        fwd_kernel,
        name="forward",
        out_shape=(
            s((rows, 512), BF), s(w4, BF), s(up, BF), s(dn, BF), s((2, 8, 512), F32), s((rows, 512), F32),
            s((2, rows, 512), F32), s((2, 4, rows, 256), F32), s((2, 4, 2, rows, 256), BF),
            s((2, 4, rows, 256), BF), s((2, 4, 4, rows, 256), BF),
        ),
        in_specs=[any_space] * len(args),
        out_specs=(any_space,) * 11,
        scratch_shapes=[
            pltpu.VMEM(w4, BF), pltpu.VMEM(up, BF), pltpu.VMEM(dn, BF), pltpu.VMEM((4, 2, 2, 2, 2, 8, 128), F32),
            pltpu.VMEM((rows, 512), BF), pltpu.VMEM((rows, 512), F32), pltpu.VMEM((rows, 512), F32), pltpu.VMEM((8, 128), F32),
            pltpu.VMEM((4, rows, 256), F32), pltpu.VMEM((4, rows, 256), F32), pltpu.VMEM((4, 3, rows, 256), BF),
            pltpu.VMEM((4, rows, 256), BF), pltpu.VMEM((4, 4, rows, 256), BF),
            pltpu.VMEM((2, 8, 1024), F32), pltpu.VMEM((2, 8, 512), F32),
            pltpu.VMEM((2, 8, 1024), F32), pltpu.VMEM((2, 8, 1024), F32),
            dma((9, 12)), dma((9, 12)), dma((12,)), dma((32,)), dma((2,)), dma((2,)),
        ],
        compiler_params=pltpu.CompilerParams(
            collective_id=0, has_side_effects=True, vmem_limit_bytes=62 * 2**20
        ),
    )(*args)


class Scatter:
    def __init__(self, grads, landing, finals, send, recv):
        self.grads = grads
        self.landing = landing
        self.finals = finals
        self.send = send
        self.recv = recv
        self.at = place()
        self.sent = {}
        self.done = {}

    def own(self, item, z, x, y, c, h):
        kind, l = item
        w4, up, dn, vec = self.grads
        if kind == "vec":
            return vec.at[z, x, y, c, h]
        if kind == "gate":
            return w4.at[y, c, pl.ds(0, 3), z, x, h]
        if kind == "out":
            return w4.at[y, c, pl.ds(3, 1), z, x, h]
        if kind == "up":
            return up.at[h, z, x, y, c]
        return dn.at[z, x, y, c, h]

    def land(self, item, stage, *more):
        kind, l = item
        ref = self.landing[{"vec": 3, "gate": 0, "out": 0, "up": 1, "down": 2}[kind]][stage]
        if kind == "vec":
            return ref.at[more] if more else ref
        if kind in ("gate", "out"):
            k = pl.ds(0, 3) if kind == "gate" else pl.ds(3, 1)
            if stage in (0, 2):
                return ref.at[l, :, k]
            if stage == 1:
                return ref.at[l, k]
            return ref.at[(l, *more, k)]
        return ref.at[(l, *more)]

    def copy(self, n, slot, src, dst, target):
        return pltpu.make_async_remote_copy(
            src_ref=src,
            dst_ref=dst,
            send_sem=self.send.at[n, slot],
            recv_sem=self.recv.at[n, slot],
            device_id=target,
            device_id_type=MESH,
        )

    def go(self, n, slot, src, dst, target):
        cp = self.copy(n, slot, src, dst, target)
        cp.start()
        self.sent.setdefault(n, []).append(cp)

    def landed(self, n, slot, dst, source):
        self.copy(n, slot, dst, dst, source).wait_recv()

    def add(self, item, stage):
        kind, l = item
        z, x, y, c = self.at
        w4, up, dn, vec = self.grads
        lw, lu, ld, lv = self.landing
        ks = (0, 3) if kind == "gate" else (3, 1)
        if stage == 0:
            if kind in ("gate", "out"):

                @pl.loop(0, 8 * ks[1])
                def _(i):
                    yy, kz = lax.div(i, 4 * ks[1]), lax.rem(i, 4 * ks[1])
                    k, zz = ks[0] + lax.div(kz, 4), lax.rem(kz, 4)
                    w4[yy, c, k, zz] += lw[0][l, yy, k, zz]
            elif kind == "up":

                @pl.loop(0, 8)
                def _(i):
                    h, zz = lax.div(i, 4), lax.rem(i, 4)
                    for xx in range(2):
                        for yy in range(2):
                            up[h, zz, xx, yy, c] += lu[0][l, h, zz, xx, yy]
            elif kind == "down":

                @pl.loop(0, 4)
                def _(zz):
                    for xx in range(2):
                        for yy in range(2):
                            dn[zz, xx, yy, c] += ld[0][l, zz, xx, yy]
            else:
                vec[:, :, :, c] += lv[0][...]
        elif stage == 1:
            if kind in ("gate", "out"):

                @pl.loop(0, 4 * ks[1])
                def _(i):
                    k, zz = ks[0] + lax.div(i, 4), lax.rem(i, 4)
                    for xx in range(2):
                        w4[y, c, k, zz, xx, 0] += lw[1][l, k, zz, xx]
            elif kind == "up":

                @pl.loop(0, 4)
                def _(zz):
                    for xx in range(2):
                        up[0, zz, xx, y, c] += lu[1][l, zz, xx]
            elif kind == "down":

                @pl.loop(0, 4)
                def _(zz):
                    for xx in range(2):
                        dn[zz, xx, y, c, 0] += ld[1][l, zz, xx]
            else:
                vec[:, :, y, c, 0] += lv[1][...]
        elif stage == 2:
            if kind in ("gate", "out"):

                @pl.loop(0, 4 * ks[1])
                def _(i):
                    k, zz = ks[0] + lax.div(i, 4), lax.rem(i, 4)
                    for yy in range(2):
                        w4[yy, c, k, zz, x, 1] += lw[2][l, yy, k, zz]
            elif kind == "up":

                @pl.loop(0, 4)
                def _(zz):
                    for yy in range(2):
                        up[1, zz, x, yy, c] += lu[2][l, zz, yy]
            elif kind == "down":

                @pl.loop(0, 4)
                def _(zz):
                    for yy in range(2):
                        dn[zz, x, yy, c, 1] += ld[2][l, zz, yy]
            else:
                vec[:, x, :, c, 1] += lv[2][...]
        elif stage == 3:
            if kind in ("gate", "out"):

                @pl.loop(ks[0], ks[0] + ks[1])
                def _(k):
                    for zz in range(4):
                        for h in range(2):
                            w4[y, c, k, zz, x, h] += lw[3][l, h, k, zz]
            elif kind == "up":
                for zz in range(4):
                    for h in range(2):
                        up[h, zz, x, y, c] += lu[3][l, h, zz]
            elif kind == "down":
                for zz in range(4):
                    for h in range(2):
                        dn[zz, x, y, c, h] += ld[3][l, h, zz]
            else:
                for h in range(2):
                    vec[:, x, y, c, h] += lv[3][h]
        else:
            fw, fu, fd, fv = self.finals
            wide = lambda first, rest: sum([r.astype(F32) for r in rest], first.astype(F32))
            if kind in ("gate", "out"):

                @pl.loop(ks[0], ks[0] + ks[1])
                def _(k):
                    fw[l, k] = wide(w4[y, c, k, z, x], [lw[4][l, j, k] for j in range(3)])
            elif kind == "up":
                for h in range(2):
                    fu[l, h] = wide(up[h, z, x, y, c], [lu[4][l, j, h] for j in range(3)])
            elif kind == "down":
                fd[l] = wide(dn[z, x, y, c], [ld[4][l, j] for j in range(3)])
            else:
                fv[...] = wide(vec[z, x, y, c], [lv[4][j] for j in range(3)])

    def stage(self, step, n, item):
        z, x, y, c = self.at
        v = lambda *where: self.own(item, *where)
        to_x = device(z, 1 - x, y, c)
        to_y = device(z, x, 1 - y, c)
        to_c = device(z, x, y, 1 - c)
        land = lambda *w: self.land(item, *w)
        if step == 0:
            self.go(n, 0, v(ALL, ALL, ALL, 1 - c, ALL), land(0), to_c)
        elif step == 1:
            self.landed(n, 0, land(0), to_c)
            self.add(item, 0)
            self.go(n, 1, v(ALL, ALL, 1 - y, c, 0), land(1), to_y)
            self.go(n, 2, v(ALL, 1 - x, ALL, c, 1), land(2), to_x)
        elif step == 2:
            self.landed(n, 1, land(1), to_y)
            self.add(item, 1)
            self.go(n, 3, v(ALL, 1 - x, y, c, 0), land(3, 0), to_x)
            self.landed(n, 2, land(2), to_x)
            self.add(item, 2)
            self.go(n, 4, v(ALL, x, 1 - y, c, 1), land(3, 1), to_y)
        elif step == 3:
            self.landed(n, 3, land(3, 0), to_x)
            self.landed(n, 4, land(3, 1), to_y)
            self.add(item, 3)
            for k in (1, 2, 3):
                there = lax.rem(z + k, 4)
                self.go(n, 4 + k, v(there, x, y, c, ALL), land(4, k - 1), device(there, x, y, c))
        else:
            for k in (1, 2, 3):
                source = lax.rem(z + 4 - k, 4)
                self.landed(n, 4 + k, land(4, k - 1), device(source, x, y, c))
            self.add(item, 4)

    def settle(self, n):
        for cp in self.sent.pop(n, []):
            cp.wait_send()


def spread_back(g, first, size, total, per_mp):
    r = lax.div(lax.broadcasted_iota(jnp.int32, (256, total), 0), 8)
    d = lax.broadcasted_iota(jnp.int32, (256, total), 1)
    if per_mp:
        owner = lax.div(lax.rem(d, total // 4), size) * 4 + lax.div(d, total // 4)
    else:
        owner = lax.div(d, size)
    rows = jnp.where(r == owner, g, 0.0)
    d = lax.broadcasted_iota(jnp.int32, (total, 128), 0)
    j = lax.broadcasted_iota(jnp.int32, (total, 128), 1)
    pick = jnp.where(j == first + lax.rem(d, size), 1.0, 0.0).astype(BF)
    high = rows.astype(BF)
    rest = rows - high.astype(F32)
    middle = rest.astype(BF)
    low = (rest - middle.astype(F32)).astype(BF)
    return dot(high, pick) + dot(middle, pick) + dot(low, pick)


def bwd_kernel(
    ct_in, x_in, w4_in, up_in, dn_in, gain_in, stream_in, mixed_in, keep_in, q_in, hid_in, ff_in,
    grad_hbm, gate_hbm, up_hbm, down_hbm, vec_hbm,
    w4, up, dn, gain, keep, pre, mixed, stream, ff, grad, acc, low, low_t, act_t, up_low, sg, c_out, c_in,
    gains, biases, g_w4, g_up, g_dn, g_vec,
    lw0, lw1, lw2, lw3, lw4, lu0, lu1, lu2, lu3, lu4, ld0, ld1, ld2, ld3, ld4, lv0, lv1, lv2, lv3, lv4,
    f_w4, f_up, f_dn, f_vec,
    rs_send, rs_recv, load_sem, save_sem, carry_send, carry_recv,
):
    z, x, y, c = place()
    mp = y * 2 + c
    rows_all = low.shape[0]
    chunks = rows_all // ROWS
    loads = {}
    n_load = 0
    saves = []

    def load(key, src, dst):
        nonlocal n_load
        cp = pltpu.make_async_copy(src, dst, load_sem.at[n_load])
        cp.start()
        loads[key] = cp
        n_load += 1

    def ready(key):
        loads.pop(key).wait()

    def save(src, dst):
        cp = pltpu.make_async_copy(src, dst, save_sem.at[len(saves)])
        cp.start()
        saves.append(cp)

    def load_feed(l):
        load("dn", dn_in.at[l], dn)
        load("up", up_in.at[l], up)

    def load_chunk(l, q):
        load(("ff", q), ff_in.at[l, q], ff.at[q % 2])

    load("ct", ct_in, low)
    load("gain", gain_in, gain)
    load("mixed", mixed_in.at[1], mixed)
    load_feed(1)
    load_chunk(1, 0)
    load_chunk(1, 1)
    load("w4", w4_in.at[1], w4)
    load("keep", keep_in.at[1], keep)
    load("q", q_in.at[1], pre.at[:, pl.ds(0, 2)])
    load("stream", stream_in, stream)
    greet()
    landing = (
        (lw0, lw1, lw2, lw3, lw4), (lu0, lu1, lu2, lu3, lu4), (ld0, ld1, ld2, ld3, ld4), (lv0, lv1, lv2, lv3, lv4),
    )
    scatter = Scatter((g_w4, g_up, g_dn, g_vec), landing, (f_w4, f_up, f_dn, f_vec), rs_send, rs_recv)
    number = {}
    for item in (
        ("down", 1), ("up", 1), ("out", 1), ("gate", 1), ("down", 0), ("up", 0), ("out", 0), ("gate", 0), ("vec", 0),
    ):
        number[item] = len(number)
    stage_of = {item: 0 for item in number}

    def push(*kinds):
        for item in kinds:
            step = stage_of[item]
            scatter.stage(step, number[item], item)
            stage_of[item] = step + 1
            if step == 4:
                kind, l = item
                if kind == "gate":
                    save(f_w4.at[l, pl.ds(0, 3)], gate_hbm.at[l, pl.ds(0, 3)])
                elif kind == "out":
                    save(f_w4.at[l, pl.ds(3, 1)], gate_hbm.at[l, pl.ds(3, 1)])
                elif kind == "up":
                    for h in range(2):
                        save(f_up.at[l, h], up_hbm.at[l, :, pl.ds(h * 1024, 1024)])
                elif kind == "down":
                    save(f_dn.at[l], down_hbm.at[l])
                else:
                    save(f_vec, vec_hbm)

    def each(fn):
        @pl.loop(0, chunks)
        def _(i):
            fn(i, pl.ds(pl.multiple_of(i * ROWS, ROWS), ROWS))

    def rms_t(src, dst_t, g):
        def part(i, r):
            v = src[r, :]
            scale = lax.rsqrt(jnp.mean(v * v, axis=-1, keepdims=True) + eps)
            dst_t[:, r] = (v * scale * g).astype(BF).T

        each(part)

    def feed(l, q):
        slot = q % 2
        w_down = dn[q].reshape(512, 512)
        w_up = up[q // 2].reshape(512, 1024)[:, (q % 2) * 512 : (q % 2) * 512 + 512]

        def part(i, r):
            act_grad = dot_nt(low[r, :], w_down)
            slope = jnp.concatenate([ff[slot, 0, r, :], ff[slot, 1, r, :]], axis=1).astype(F32)
            u = (act_grad * slope).astype(BF)
            up_low[r, :] = u
            back = dot_nt(u, w_up)
            acc[r, :] = back if q == 0 else acc[r, :] + back

        each(part)
        for half in range(2):
            g = dot_tn(ff[slot, 2 + half], low[...]).astype(BF)
            g_dn[q, half] = g.reshape(2, 2, 2, 32, 512)
            g = dot(act_t[half * 256 : half * 256 + 256, :], up_low[...]).astype(BF)
            g_up[q // 2, half * 2 : half * 2 + 2, :, :, :, :, (q % 2) * 512 : (q % 2) * 512 + 512] = g.reshape(
                2, 2, 2, 2, 16, 512
            )

    def rms_back(l, which, src, values_t):
        g = gain[l, which : which + 1, :]
        gains[l, which : which + 1, :] = jnp.zeros((1, 512), F32)

        def part(i, r):
            v = src[r, :]
            scale = lax.rsqrt(jnp.mean(v * v, axis=-1, keepdims=True) + eps)
            u = v * scale
            d = acc[r, :]
            gains[l, which : which + 1, :] += jnp.sum(d * u, axis=0, keepdims=True)
            dg = d * g
            new = grad[r, :] + scale * (dg - u * jnp.mean(dg * u, axis=-1, keepdims=True))
            grad[r, :] = new
            new = new.astype(BF)
            low[r, :] = new
            if values_t is not None:
                values_t[:, r] = new.T

        each(part)

    def states_back(l, p):
        w = w4[p // 2, p % 2, 3].reshape(512, 256)

        def part(i, r):
            sg[p, r, :] = dot(low[r, :], w)

        each(part)
        g = dot(low_t[...], ff[0, p]).astype(BF)
        g_w4[p // 2, p % 2, 3] = g.reshape(4, 2, 2, 32, 256)

    row = lax.broadcasted_iota(jnp.int32, (8, 256), 0)

    def scan(lo, hi, carry):
        def body(n, carry):
            r = pl.ds(pl.multiple_of((hi - 1 - n + lo) * 16, 16), 16)
            after = []
            for p in range(4):
                v_next = carry[p]
                share = keep[p, r, :]
                s16 = sg[p, r, :]
                decay = 1.0 - share
                adjoint = [None, None]
                for half in (1, 0):
                    part = slice(half * 8, half * 8 + 8)
                    s8 = s16[part]
                    a, b = combine(decay[part], decay[part] * s8, row, -1)
                    first = jnp.broadcast_to(v_next[0:1, :], (8, 256))
                    v = b + a * first
                    adjoint[half] = s8 + jnp.where(row == 7, first, pltpu.roll(v, 7, 0))
                    v_next = v
                after.append(v_next)
                adj = jnp.concatenate(adjoint, axis=0)
                pre[p, 0, r, :] = (adj * pre[p, 0, r, :].astype(F32)).astype(BF)
                pre[p, 1, r, :] = (adj * pre[p, 1, r, :].astype(F32)).astype(BF)
                pre[p, 2, r, :] = (adj * share).astype(BF)
            return tuple(after)

        return lax.fori_loop(lo, hi, body, carry)

    start_row = jnp.minimum(lax.rem(mp * (LENGTH - rows_all), LENGTH), rows_all)
    start = lax.div(start_row, 16)
    groups = rows_all // 16

    def carry_copy(l, to_y, to_c):
        return pltpu.make_async_remote_copy(
            src_ref=c_out.at[l],
            dst_ref=c_in.at[l],
            send_sem=carry_send.at[l],
            recv_sem=carry_recv.at[l],
            device_id=device(z, x, to_y, to_c),
            device_id_type=MESH,
        )

    def scan_head(l):
        zero = jnp.zeros((8, 256), F32)
        end = scan(0, start, (zero,) * 4)
        for p in range(4):
            c_out[l, :, p * 256 : (p + 1) * 256] = end[p]
        before = jnp.maximum(mp - 1, 0)

        @pl.when(mp > 0)
        def _():
            carry_copy(l, lax.div(before, 2), lax.rem(before, 2)).start()

    def scan_tail(l):
        after = jnp.minimum(mp + 1, 3)

        @pl.when(mp < 3)
        def _():
            carry_copy(l, lax.div(after, 2), lax.rem(after, 2)).wait_recv()
            scan(start, groups, tuple(c_in[l, :, p * 256 : (p + 1) * 256] for p in range(4)))

        before = jnp.maximum(mp - 1, 0)

        @pl.when(mp > 0)
        def _():
            carry_copy(l, lax.div(before, 2), lax.rem(before, 2)).wait_send()

    def gate_back(l, p):
        w = [w4[p // 2, p % 2, k].reshape(512, 256) for k in range(3)]

        def part(i, r):
            back = dot_nt(pre[p, 0, r, :], w[0]) + dot_nt(pre[p, 1, r, :], w[1]) + dot_nt(pre[p, 2, r, :], w[2])
            acc[r, :] = back if p == 0 else acc[r, :] + back

        each(part)
        ones = jnp.ones((8, rows_all), BF)
        for k in range(3):
            values = pre[p, k]
            g_w4[p // 2, p % 2, k] = dot(act_t[...], values).astype(BF).reshape(4, 2, 2, 32, 256)
            biases[l, k : k + 1, p * 256 : (p + 1) * 256] = dot(ones, values)[0:1, :]

    ready("ct")

    def widen(i, r):
        grad[r, :] = low[r, :].astype(F32)

    each(widen)
    ready("gain")
    for l in (1, 0):
        down, upw, out, gate = [(kind, l) for kind in ("down", "up", "out", "gate")]
        late = lambda *kinds: push(*[(kind, 1) for kind in kinds]) if l == 0 else None
        ready("mixed")
        rms_t(mixed, act_t, gain[l, 1:2, :])
        if l == 0:
            scatter.settle(number[("down", 1)])
            scatter.settle(number[("up", 1)])
        ready("dn")
        ready("up")
        for q in range(4):
            ready(("ff", q))
            feed(l, q)
            if q < 2:
                load_chunk(l, q + 2)
            elif q == 2:
                load("hid", hid_in.at[l], ff.at[0])
            if q == 0:
                late("gate")
            elif q == 1:
                late("gate")
            elif q == 2:
                late("gate")
        push(down, upw)
        rms_back(l, 1, mixed, low_t)
        if l == 1:
            load_feed(0)
            load("mixed", mixed_in.at[0], mixed)
        if l == 1:
            ready("stream")
            load("x", x_in, up_low)
        rms_t(stream, act_t, gain[l, 0:1, :])
        late("gate")
        push(down, upw)
        if l == 0:
            scatter.settle(number[("out", 1)])
            scatter.settle(number[("gate", 1)])
        ready("w4")
        ready("hid")
        for p in range(4):
            states_back(l, p)
        push(out, down, upw)
        if l == 1:
            load_chunk(0, 0)
        ready("keep")
        ready("q")
        scan_head(l)
        push(out, down, upw)
        scan_tail(l)
        push(out, down, upw)
        for p in range(4):
            gate_back(l, p)
            if p == 1:
                push(out)
        push(gate)
        if l == 1:
            load_chunk(0, 1)
            load("w4", w4_in.at[0], w4)
            load("keep", keep_in.at[0], keep)
            load("q", q_in.at[0], pre.at[:, pl.ds(0, 2)])
        rms_back(l, 0, stream, None)
        if l == 1:
            ready("x")

            def widen_x(i, r):
                stream[r, :] = up_low[r, :].astype(F32)

            each(widen_x)
        push(out)
        rows = spread_back(gains[l, 0:1, :], 0, 16, 512, False) + spread_back(gains[l, 1:2, :], 16, 16, 512, False)
        for k in range(3):
            rows = rows + spread_back(biases[l, k : k + 1, :], 32 + 32 * k, 32, 1024, True)
        g_vec[:, :, :, :, l] = rows.reshape(4, 2, 2, 2, 8, 128)
    save(grad, grad_hbm)
    vec_item = ("vec", 0)
    gate = ("gate", 0)
    for step in range(5):
        push(vec_item)
        if step < 4:
            push(gate)
    for n in range(len(number)):
        scatter.settle(n)
    for cp in saves:
        cp.wait()


def backward(cotangent, x, kept):
    w4_all, up_all, dn_all, gain, stream, mixed, keep, q, hid, ff = kept
    rows = x.shape[0]
    any_space = pl.BlockSpec(memory_space=pl.ANY)
    s = jax.ShapeDtypeStruct
    dma = pltpu.SemaphoreType.DMA
    v = pltpu.VMEM
    args = (cotangent, x, w4_all, up_all, dn_all, gain, stream, mixed, keep, q, hid, ff)
    grad, gates, up, down, vec = pl.pallas_call(
        bwd_kernel,
        name="backward",
        out_shape=(
            s((rows, 512), F32), s((2, 4, 2, 32, 256), F32), s((2, 16, 2048), F32), s((2, 2, 32, 512), F32), s((2, 8, 128), F32),
        ),
        in_specs=[any_space] * len(args),
        out_specs=(any_space,) * 5,
        scratch_shapes=[
            v((2, 2, 4, 4, 2, 2, 32, 256), BF), v((2, 4, 2, 2, 2, 16, 1024), BF), v((4, 2, 2, 2, 2, 32, 512), BF),
            v((2, 8, 512), F32), v((4, rows, 256), F32), v((4, 3, rows, 256), BF), v((rows, 512), F32), v((rows, 512), F32),
            v((2, 4, rows, 256), BF), v((rows, 512), F32), v((rows, 512), F32), v((rows, 512), BF), v((512, rows), BF),
            v((512, rows), BF), v((rows, 512), BF), v((4, rows, 256), F32), v((2, 8, 1024), F32), v((2, 8, 1024), F32),
            v((2, 8, 512), F32), v((2, 8, 1024), F32),
            v((2, 2, 4, 4, 2, 2, 32, 256), BF), v((2, 4, 2, 2, 2, 16, 1024), BF), v((4, 2, 2, 2, 2, 32, 512), BF),
            v((4, 2, 2, 2, 2, 8, 128), F32),
            v((2, 2, 4, 4, 2, 2, 32, 256), BF), v((2, 4, 4, 2, 32, 256), BF), v((2, 2, 4, 4, 32, 256), BF),
            v((2, 2, 4, 4, 32, 256), BF), v((2, 3, 4, 2, 32, 256), BF),
            v((2, 2, 4, 2, 2, 16, 1024), BF), v((2, 4, 2, 16, 1024), BF), v((2, 4, 2, 16, 1024), BF),
            v((2, 2, 4, 16, 1024), BF), v((2, 3, 2, 16, 1024), BF),
            v((2, 4, 2, 2, 2, 32, 512), BF), v((2, 4, 2, 32, 512), BF), v((2, 4, 2, 32, 512), BF),
            v((2, 2, 4, 32, 512), BF), v((2, 3, 2, 32, 512), BF),
            v((4, 2, 2, 2, 8, 128), F32), v((4, 2, 8, 128), F32), v((4, 2, 8, 128), F32), v((2, 4, 8, 128), F32),
            v((3, 2, 8, 128), F32),
            v((2, 4, 2, 32, 256), F32), v((2, 2, 16, 1024), F32), v((2, 2, 32, 512), F32), v((2, 8, 128), F32),
            dma((9, 8)), dma((9, 8)), dma((32,)), dma((16,)), dma((2,)), dma((2,)),
        ],
        compiler_params=pltpu.CompilerParams(
            collective_id=1, has_side_effects=True, vmem_limit_bytes=63 * 2**20
        ),
    )(*args)
    gates = gates.reshape(2, 4, 64, 256)
    vec = vec[:, 0, :]
    return (
        grad,
        gates[:, :3],
        vec[:, 32:].reshape(2, 3, 32),
        gates[:, 3].transpose(0, 2, 1),
        vec[:, :16],
        vec[:, 16:32],
        up,
        down.reshape(2, 64, 512),
    )


def fits(inputs, gate_weight, gate_bias, out_weight, gain_one, gain_two, up_weight, down_weight):
    rows = inputs.shape[0]
    shapes = (gate_weight.shape, gate_bias.shape, out_weight.shape, gain_one.shape, up_weight.shape, down_weight.shape)
    planned = ((2, 3, 64, 256), (2, 3, 32), (2, 256, 64), (2, 16), (2, 16, 2048), (2, 64, 512))
    axes = (lax.axis_size("dp"), lax.axis_size("mp"))
    return axes == (8, 4) and shapes == planned and rows == 768 and 4 * rows == 3 * LENGTH


def general_body(
    inputs,
    gate_weight,
    gate_bias,
    out_weight,
    norm_gain_one,
    norm_gain_two,
    up_weight,
    down_weight,
    cotangent,
):
    own_rows = inputs.shape[0]
    group = own_rows * lax.axis_size("mp")
    starts = (jnp.arange(group, dtype=jnp.int32) % LENGTH == 0)[:, None]
    layer_count = gate_weight.shape[0]
    width = gate_weight.shape[3]
    stream = inputs.astype(jnp.float32)
    saved = []
    held = []
    for layer_no in range(layer_count):
        gates_full, bias_full, out_full = (
            lax.all_gather(gate_weight[layer_no], "dp", axis=1, tiled=True),
            lax.all_gather(gate_bias[layer_no], "dp", axis=1, tiled=True),
            lax.all_gather(out_weight[layer_no], "dp", axis=1, tiled=True),
        )
        up_full, down_full, gain_first, gain_second = (
            lax.all_gather(up_weight[layer_no], ("dp", "mp"), axis=0, tiled=True),
            lax.all_gather(down_weight[layer_no], ("dp", "mp"), axis=0, tiled=True),
            lax.all_gather(norm_gain_one[layer_no], ("dp", "mp"), axis=0, tiled=True),
            lax.all_gather(norm_gain_two[layer_no], ("dp", "mp"), axis=0, tiled=True),
        )
        gain_first = gain_first.astype(jnp.float32)
        gain_second = gain_second.astype(jnp.float32)
        normed = rms_scale(stream, gain_first).astype(jnp.bfloat16)
        normed_all = lax.all_gather(normed, "mp", axis=0, tiled=True)
        pre_acts = (
            jnp.einsum("td,kdf->ktf", normed_all, gates_full, preferred_element_type=jnp.float32)
            + bias_full.astype(jnp.float32)[:, None, :]
        )
        decay, drive = gate_terms(pre_acts, starts)
        products, states = lax.associative_scan(link, (decay, drive), axis=0)
        hidden = states.astype(jnp.bfloat16)
        mixed = stream + lax.psum_scatter(
            dot_plain(hidden, out_full).astype(jnp.bfloat16), "mp", scatter_dimension=0, tiled=True
        ).astype(jnp.float32)
        second = rms_scale(mixed, gain_second).astype(jnp.bfloat16)
        up_acts = dot_plain(second, up_full)
        activated = jax.nn.gelu(up_acts).astype(jnp.bfloat16)
        saved.append(
            {
                "stream": stream,
                "gain_first": gain_first,
                "gain_second": gain_second,
                "normed": normed_all,
                "pre": pre_acts,
                "decay": decay,
                "states": states,
                "hidden": hidden,
                "mixed": mixed,
                "second": second,
                "up_acts": up_acts,
                "activated": activated,
            }
        )
        held.append((gates_full, out_full, up_full, down_full))
        stream = mixed + dot_plain(activated, down_full)
    grad = cotangent.astype(jnp.float32)
    gate_parts = []
    mlp_parts = []
    for layer_no in reversed(range(layer_count)):
        kept = saved[layer_no]
        gates_full, out_full, up_full, down_full = held[layer_no]
        grad_low = grad.astype(jnp.bfloat16)
        act_grad = dot_last(grad_low, down_full)
        down_grad = dot_first(kept["activated"], grad_low)
        unused_gelu, gelu_back = jax.vjp(jax.nn.gelu, kept["up_acts"])
        up_low = gelu_back(act_grad)[0].astype(jnp.bfloat16)
        up_grad = dot_first(kept["second"], up_low)
        second_grad = dot_last(up_low, up_full)
        unused_norm, norm_back = jax.vjp(rms_scale, kept["mixed"], kept["gain_second"])
        mixed_part, gain_two_grad = norm_back(second_grad)
        mixed_grad = grad + mixed_part
        mixed_low = mixed_grad.astype(jnp.bfloat16)
        mixed_all = lax.all_gather(mixed_low, "mp", axis=0, tiled=True)
        state_grad = dot_last(mixed_all, out_full)
        out_grad = dot_first(kept["hidden"], mixed_all)
        decay = kept["decay"]
        shifted = jnp.concatenate([decay[1:], jnp.ones((1, width), jnp.float32)], axis=0)
        back_products, back_partial = lax.associative_scan(
            link, (shifted[::-1], state_grad[::-1]), axis=0
        )
        adjoint = back_partial[::-1]
        previous = jnp.concatenate(
            [jnp.zeros((1, width), jnp.float32), kept["states"][:-1]], axis=0
        )
        unused_gate, gate_back = jax.vjp(partial(gate_terms, starts=starts), kept["pre"])
        pre_low = gate_back((adjoint * previous, adjoint))[0].astype(jnp.bfloat16)
        bias_grad = jnp.sum(pre_low.astype(jnp.float32), axis=1)
        gate_grad = jnp.einsum(
            "td,ktf->kdf", kept["normed"], pre_low, preferred_element_type=jnp.float32
        )
        normed_part = jnp.einsum(
            "ktf,kdf->td", pre_low, gates_full, preferred_element_type=jnp.float32
        )
        normed_grad = lax.psum_scatter(
            normed_part.astype(jnp.bfloat16), "mp", scatter_dimension=0, tiled=True
        ).astype(jnp.float32)
        unused_first, first_back = jax.vjp(rms_scale, kept["stream"], kept["gain_first"])
        stream_part, gain_one_grad = first_back(normed_grad)
        grad = mixed_grad + stream_part
        gate_parts.append(
            (
                sum_at_owner(gate_grad.astype(jnp.bfloat16), "dp", 1),
                sum_at_owner(bias_grad.astype(jnp.bfloat16), "dp", 1),
                sum_at_owner(out_grad.astype(jnp.bfloat16), "dp", 1),
            )
        )
        mlp_parts.append(
            (
                lax.psum_scatter(up_grad, ("dp", "mp"), scatter_dimension=0, tiled=True),
                lax.psum_scatter(down_grad, ("dp", "mp"), scatter_dimension=0, tiled=True),
                lax.psum_scatter(gain_one_grad, ("dp", "mp"), scatter_dimension=0, tiled=True),
                lax.psum_scatter(gain_two_grad, ("dp", "mp"), scatter_dimension=0, tiled=True),
            )
        )
    gate_parts = gate_parts[::-1]
    mlp_parts = mlp_parts[::-1]
    gate_stack = tuple((jnp.stack([entry[member] for entry in gate_parts]) for member in range(3)))
    mlp_stack = tuple((jnp.stack([entry[member] for entry in mlp_parts]) for member in range(4)))
    return (
        stream.astype(jnp.bfloat16),
        grad,
        gate_stack[0],
        gate_stack[1],
        gate_stack[2],
        mlp_stack[2],
        mlp_stack[3],
        mlp_stack[0],
        mlp_stack[1],
    )


def body(inputs, gate_weight, gate_bias, out_weight, gain_one, gain_two, up_weight, down_weight, cotangent):
    shards = (gate_weight, gate_bias, out_weight, gain_one, gain_two, up_weight, down_weight)
    if not fits(inputs, *shards):
        return general_body(inputs, *shards, cotangent)
    out, *kept = forward(inputs, *shards)
    grad, gates, biases, out_grad, gain_a, gain_b, up, down = backward(cotangent, inputs, kept)
    return (out, grad, gates, biases, out_grad, gain_a, gain_b, up, down)


def solution(mesh):
    placed = (
        P(("dp", "mp"), None),
        P(None, None, "dp", "mp"),
        P(None, None, ("mp", "dp")),
        P(None, "mp", "dp"),
        P(None, ("dp", "mp")),
        P(None, ("dp", "mp")),
        P(None, ("dp", "mp"), None),
        P(None, ("dp", "mp"), None),
        P(("dp", "mp"), None),
    )
    return jax.shard_map(
        body,
        mesh=mesh,
        in_specs=placed,
        out_specs=(
            P(("dp", "mp"), None),
            P(("dp", "mp"), None),
            P(None, None, "dp", "mp"),
            P(None, None, ("mp", "dp")),
            P(None, "mp", "dp"),
            P(None, ("dp", "mp")),
            P(None, ("dp", "mp")),
            P(None, ("dp", "mp"), None),
            P(None, ("dp", "mp"), None),
        ),
        check_vma=False,
    )
```

```python
from functools import partial

import jax
import jax.numpy as jnp
from jax import lax
from jax.experimental import pallas as pl
from jax.experimental.pallas import tpu as pltpu
from jax.sharding import PartitionSpec as P

LENGTH = 1024


eps = 1e-06


def cut_along(x, dim, size):
    shape = x.shape
    blocks = x.reshape(*shape[:dim], size, shape[dim] // size, *shape[dim + 1 :])
    return jnp.moveaxis(blocks, dim, 0)


def sum_at_owner(x, axis, dim):
    size = lax.axis_size(axis)
    blocks = lax.all_to_all(cut_along(x, dim, size), axis, 0, 0, tiled=True)
    return jnp.sum(blocks.astype(jnp.float32), axis=0)


def rms_scale(values, gain):
    return values * lax.rsqrt(jnp.mean(values * values, axis=-1, keepdims=True) + eps) * gain


def link(earlier, later):
    return (earlier[0] * later[0], later[0] * earlier[1] + later[1])


def gate_terms(pre_acts, starts):
    sig_forget = jax.nn.sigmoid(pre_acts[0])
    sig_input = jax.nn.sigmoid(pre_acts[1])
    total = sig_forget + sig_input
    decay = jnp.where(starts, 0.0, sig_forget / total)
    return (decay, sig_input / total * pre_acts[2])


def dot_plain(left, right):
    return jnp.dot(left, right, preferred_element_type=jnp.float32)


def dot_first(left, right):
    return lax.dot_general(
        left, right, (((0,), (0,)), ((), ())), preferred_element_type=jnp.float32
    )


def dot_last(left, right):
    return lax.dot_general(
        left, right, (((1,), (1,)), ((), ())), preferred_element_type=jnp.float32
    )


ALL = slice(None)
MESH = pl.DeviceIdType.MESH
BF = jnp.bfloat16
F32 = jnp.float32
SHIFT = 0.25
LOG_SHIFT = -1.3862943611198906
TOP = 87.0
GELU_A = 0.7978845608028654
GELU_B = 0.044715
ROWS = 256
STEPS = ROWS // 8


def first_of(mp, rows):
    return lax.div(jnp.minimum(lax.rem(mp * (LENGTH - rows), LENGTH), rows), ROWS)


def place():
    dp = lax.axis_index("dp")
    mp = lax.axis_index("mp")
    return (lax.div(dp, 2), lax.rem(dp, 2), lax.div(mp, 2), lax.rem(mp, 2))


def device(z, x, y, c):
    return (z * 2 + x, y * 2 + c)


def greet():
    z, x, y, c = place()
    partners = [device(lax.rem(z + k, 4), x, y, c) for k in (1, 2, 3)]
    partners += [device(z, 1 - x, y, c), device(z, x, 1 - y, c)]
    partners += [device(z, x, y, 1 - c), device(z, x, 1 - y, 1 - c)]
    barrier = pltpu.get_barrier_semaphore()
    for partner in partners:
        pl.semaphore_signal(barrier, inc=1, device_id=partner, device_id_type=MESH)
    pl.semaphore_wait(barrier, len(partners))


class Gather:
    def __init__(self, bufs, own, items, send, recv):
        self.bufs = bufs
        self.own = own
        self.items = items
        self.send = send
        self.recv = recv
        self.at = place()
        self.sent = []
        self.ticks = 0

    def view(self, item, z, x, y, c, h):
        kind, l, part = item
        w4, up, dn, vec = self.bufs
        if kind == "vec":
            return vec.at[z, x, y, c, h]
        if kind == "gate":
            return w4.at[l, y, c, part, z, x, h]
        if kind == "up":
            return up.at[l, part, h, z, x, y, c]
        return dn.at[l, z, x, y, c, part, h]

    def go(self, n, slot, ref, target):
        cp = pltpu.make_async_remote_copy(
            src_ref=ref,
            dst_ref=ref,
            send_sem=self.send.at[n, slot],
            recv_sem=self.recv.at[n, slot],
            device_id=target,
            device_id_type=MESH,
        )
        cp.start()
        self.sent.append(cp)

    def landed(self, n, slot, ref, source):
        pltpu.make_async_remote_copy(
            src_ref=ref,
            dst_ref=ref,
            send_sem=self.send.at[n, slot],
            recv_sem=self.recv.at[n, slot],
            device_id=source,
            device_id_type=MESH,
        ).wait_recv()

    def stage(self, step, n, item):
        z, x, y, c = self.at
        v = lambda *where: self.view(item, *where)
        to_x = device(z, 1 - x, y, c)
        to_y = device(z, x, 1 - y, c)
        to_c = device(z, x, y, 1 - c)
        if step == 0:
            for cp in self.own.pop(item):
                cp.wait()
            for k in (1, 2, 3):
                self.go(n, k - 1, v(z, x, y, c, ALL), device(lax.rem(z + k, 4), x, y, c))
        elif step == 1:
            for k in (1, 2, 3):
                source = lax.rem(z + 4 - k, 4)
                self.landed(n, k - 1, v(source, x, y, c, ALL), device(source, x, y, c))
            self.go(n, 3, v(ALL, x, y, c, 0), to_x)
            self.go(n, 4, v(ALL, x, y, c, 1), to_y)
            self.go(n, 7, v(ALL, x, y, c, ALL), to_c)
        elif step == 2:
            self.landed(n, 3, v(ALL, 1 - x, y, c, 0), to_x)
            self.go(n, 5, v(ALL, ALL, y, c, 0), to_y)
            self.landed(n, 4, v(ALL, x, 1 - y, c, 1), to_y)
            self.go(n, 6, v(ALL, x, ALL, c, 1), to_x)
            self.go(n, 8, v(ALL, 1 - x, y, c, 0), to_c)
            self.go(n, 9, v(ALL, x, 1 - y, c, 1), to_c)
        elif step == 3:
            self.landed(n, 5, v(ALL, ALL, 1 - y, c, 0), to_y)
            self.go(n, 10, v(ALL, ALL, 1 - y, c, 0), to_c)
            self.landed(n, 6, v(ALL, 1 - x, ALL, c, 1), to_x)
            self.go(n, 11, v(ALL, 1 - x, ALL, c, 1), to_c)
        else:
            self.landed(n, 7, v(ALL, x, y, 1 - c, ALL), to_c)
            self.landed(n, 8, v(ALL, 1 - x, y, 1 - c, 0), to_c)
            self.landed(n, 9, v(ALL, x, 1 - y, 1 - c, 1), to_c)
            self.landed(n, 10, v(ALL, ALL, 1 - y, 1 - c, 0), to_c)
            self.landed(n, 11, v(ALL, 1 - x, ALL, 1 - c, 1), to_c)

    def tick(self):
        t = self.ticks
        self.ticks += 1
        for step in range(5):
            if 0 <= t - step < len(self.items):
                self.stage(step, t - step, self.items[t - step])

    def have(self, item):
        while self.ticks < self.items.index(item) + 5:
            self.tick()

    def finish(self):
        for cp in self.sent:
            cp.wait_send()


def dot(a, b):
    return jnp.dot(a, b, preferred_element_type=F32)


def dot_nt(a, b):
    return lax.dot_general(a, b, (((1,), (1,)), ((), ())), preferred_element_type=F32)


def dot_tn(a, b):
    return lax.dot_general(a, b, (((0,), (0,)), ((), ())), preferred_element_type=F32)


def spread(vec, l, first, size, total, per_mp):
    rows = vec[:, :, :, :, l].reshape(256, 128).astype(BF)
    j = lax.broadcasted_iota(jnp.int32, (128, total), 0)
    d = lax.broadcasted_iota(jnp.int32, (128, total), 1)
    pick = jnp.where(j == first + lax.rem(d, size), 1.0, 0.0).astype(BF)
    wide = dot(rows, pick)
    r = lax.div(lax.broadcasted_iota(jnp.int32, (256, total), 0), 8)
    d = lax.broadcasted_iota(jnp.int32, (256, total), 1)
    if per_mp:
        owner = lax.div(lax.rem(d, total // 4), size) * 4 + lax.div(d, total // 4)
    else:
        owner = lax.div(d, size)
    return jnp.sum(jnp.where(r == owner, wide, 0.0), axis=0, keepdims=True)


def combine(a, b, row, sign):
    for s in (1, 2, 4):
        keep = (row >= s) if sign > 0 else (row < 8 - s)
        by = s if sign > 0 else 8 - s
        am = jnp.where(keep, a, 0.0)
        b = b + am * pltpu.roll(b, by, 0)
        if s < 4:
            a = jnp.where(keep, a * pltpu.roll(a, by, 0), a)
        else:
            a = jnp.where(keep, a * pltpu.roll(a, by, 0), a)
    return a, b


def into_steps(v, turn, i):
    for n in range(4):
        turn[n, pl.ds(i * ROWS, ROWS), :] = v[:, n * 128 : n * 128 + 128]
    parts = []
    for n in range(4):
        rows = [turn[n, pl.ds(i * ROWS + j, 8, stride=STEPS), :] for j in range(STEPS)]
        parts.append(jnp.concatenate(rows, axis=0))
    return jnp.concatenate(parts, axis=1)


def unturn(v, turn, i):
    for n in range(4):
        for j in range(STEPS):
            turn[n, pl.ds(i * ROWS + j, 8, stride=STEPS), :] = v[j * 8 : j * 8 + 8, n * 128 : n * 128 + 128]
    return jnp.concatenate([turn[n, pl.ds(i * ROWS, ROWS), :] for n in range(4)], axis=1)


def fwd_kernel(
    x_in, gate_in, out_in, up_in, down_in, vec_in,
    out_hbm, w4_hbm, up_hbm, dn_hbm, gain_hbm, stream_hbm, mixed_hbm, keep_hbm, q_hbm, hid_hbm, ff_hbm,
    w4, up, dn, vec, normed, stream, mixed, turn, ends, enter, keep, states, c3, hid, ff, bias, gain, c_out, c_in,
    ag_send, ag_recv, own_sem, spill_sem, carry_send, carry_recv,
):
    z, x, y, c = place()
    mp = y * 2 + c
    rows_all = normed.shape[0]
    chunks = rows_all // ROWS
    fill = []

    def local(src, dst, sem):
        cp = pltpu.make_async_copy(src, dst, sem)
        cp.start()
        return cp

    own = {}
    n_own = 0

    def add_own(key, src, dst):
        nonlocal n_own
        own.setdefault(key, []).append(local(src, dst, own_sem.at[n_own]))
        n_own += 1

    x_copy = local(x_in, normed, own_sem.at[48])
    add_own(("vec", 0, 0), vec_in, vec.at[z, x, y, c])
    for l in range(2):
        for k in range(3):
            add_own(("gate", l, k), gate_in.at[l, k], w4.at[l, y, c, k, z, x])
        add_own(("gate", l, 3), out_in.at[l], w4.at[l, y, c, 3, z, x])
        for pair in range(2):
            for h in range(2):
                columns = pl.ds((pair * 2 + h) * 512, 512)
                add_own(("up", l, pair), up_in.at[l, :, columns], up.at[l, pair, h, z, x, y, c])
            add_own(("down", l, pair), down_in.at[l, pair], dn.at[l, z, x, y, c, pair])
    greet()
    items = [("vec", 0, 0)]
    for l in range(2):
        items += [("gate", l, k) for k in range(4)]
        items += [(kind, l, pair) for kind in ("up", "down") for pair in range(2)]
    gather = Gather((w4, up, dn, vec), own, items, ag_send, ag_recv)
    tick, have = gather.tick, gather.have

    n_spill = 0
    spills = {}

    def spill(key, src, dst):
        nonlocal n_spill
        spills[key] = local(src, dst, spill_sem.at[n_spill])
        n_spill += 1

    def settle(key):
        if key in spills:
            spills.pop(key).wait()


    def rms(src, dst, g):
        @pl.loop(0, chunks)
        def _(i):
            r = pl.ds(pl.multiple_of(i * ROWS, ROWS), ROWS)
            v = src[r, :]
            scale = lax.rsqrt(jnp.mean(v * v, axis=-1, keepdims=True) + eps)
            dst[r, :] = (v * scale * g).astype(BF)

    def gate_panel(l, p):
        w = [w4[l, p // 2, p % 2, k].reshape(512, 256) for k in range(3)]
        bs = [bias[l, k : k + 1, p * 256 : (p + 1) * 256] for k in range(3)]

        @pl.loop(0, chunks)
        def _(i):
            r = pl.ds(pl.multiple_of(i * ROWS, ROWS), ROWS)
            n = normed[r, :]
            f, inp, cand = [dot(n, w[k]) + bs[k] for k in range(3)]
            e_f = jnp.exp(jnp.minimum(-f, TOP) + LOG_SHIFT)
            e_i = jnp.exp(jnp.minimum(-inp, TOP) + LOG_SHIFT)
            a_f = e_f + SHIFT
            a_i = e_i + SHIFT
            total = a_f + a_i
            inv = pl.reciprocal(total, approx=True)
            inv = inv * (2.0 - total * inv)
            share = a_f * inv
            decay = a_i * inv
            drive = share * cand
            keep[p, r, :] = share
            c3[p, 0, r, :] = (decay * (e_f * inv)).astype(BF)
            c3[p, 1, r, :] = (share * (e_i * inv)).astype(BF)
            c3[p, 2, r, :] = cand.astype(BF)
            s = drive[0:8]
            a = decay[0:8]
            local_states = [s]
            for j in range(1, STEPS):
                t = slice(j * 8, j * 8 + 8)
                s = decay[t] * s + drive[t]
                a = a * decay[t]
                local_states.append(s)
            states[p, r, :] = jnp.concatenate(local_states, axis=0)
            columns = slice(p * 256, p * 256 + 256)
            ends[0, i, :, columns] = a
            ends[1, i, :, columns] = s

    row = lax.broadcasted_iota(jnp.int32, (8, 1024), 0)
    first_chunk = first_of(mp, rows_all)

    def carries(entering):
        for i in range(chunks):
            c0 = jnp.where(first_chunk == i, 0.0, entering)
            a, s = combine(ends[0, i], ends[1, i], row, 1)
            enter[i] = jnp.where(row == 0, c0, pltpu.roll(a, 1, 0) * c0 + pltpu.roll(s, 1, 0))
            entering = jnp.broadcast_to(a[7:8] * c0[7:8] + s[7:8], (8, 1024))
        return entering

    def carry_copy(l, there):
        return pltpu.make_async_remote_copy(
            src_ref=c_out.at[l],
            dst_ref=c_in.at[l],
            send_sem=carry_send.at[l],
            recv_sem=carry_recv.at[l],
            device_id=device(z, x, lax.div(there, 2), lax.rem(there, 2)),
            device_id_type=MESH,
        )

    def carry_out(l):
        c_out[l] = carries(jnp.zeros((8, 1024), F32))

        @pl.when(mp < 3)
        def _():
            carry_copy(l, jnp.minimum(mp + 1, 3)).start()

    def carry_into(l):
        @pl.when(mp > 0)
        def _():
            carry_copy(l, jnp.maximum(mp - 1, 0)).wait_recv()
            carries(c_in[l])

        @pl.when(mp < 3)
        def _():
            carry_copy(l, jnp.minimum(mp + 1, 3)).wait_send()

    def project(l):
        g = gain[l, 1:2, :]
        w = [w4[l, p // 2, p % 2, 3].reshape(512, 256) for p in range(4)]

        @pl.loop(0, chunks)
        def _(i):
            r = pl.ds(pl.multiple_of(i * ROWS, ROWS), ROWS)
            v = stream[r, :]
            for p in range(4):
                share = keep[p, r, :]
                s_local = states[p, r, :]
                cand = c3[p, 2, r, :].astype(F32)
                enters = enter[i, :, p * 256 : p * 256 + 256]
                before = enters
                weight = enters
                now, gap = [], []
                for j in range(STEPS):
                    t = slice(j * 8, j * 8 + 8)
                    weight = weight - share[t] * weight
                    s = s_local[t] + weight
                    gap.append(before - cand[t])
                    now.append(s)
                    before = s
                gap = jnp.concatenate(gap, axis=0)
                h = jnp.concatenate(now, axis=0).astype(BF)
                hid[p, r, :] = h
                c3[p, 0, r, :] = (gap * c3[p, 0, r, :].astype(F32)).astype(BF)
                c3[p, 1, r, :] = (-gap * c3[p, 1, r, :].astype(F32)).astype(BF)
                v = v + dot_nt(h, w[p])
            mixed[r, :] = v
            scale = lax.rsqrt(jnp.mean(v * v, axis=-1, keepdims=True) + eps)
            normed[r, :] = (v * scale * g).astype(BF)

    def feed_up(l, q):
        w_up = up[l, q // 2, q % 2].reshape(512, 512)

        @pl.loop(0, chunks)
        def _(i):
            r = pl.ds(pl.multiple_of(i * ROWS, ROWS), ROWS)
            u = dot(normed[r, :], w_up)
            sq = u * u
            t = jnp.tanh(u * (GELU_A + (GELU_A * GELU_B) * sq))
            gate = 0.5 + 0.5 * t
            act = (u * gate).astype(BF)
            slope = gate + (0.5 * u) * (1.0 - t * t) * (GELU_A + (3.0 * GELU_A * GELU_B) * sq)
            for half in range(2):
                side = slice(half * 256, half * 256 + 256)
                ff[q, half, r, :] = slope[:, side].astype(BF)
                ff[q, 2 + half, r, :] = act[:, side]

    def feed_down(l):
        w_down = [dn[l, q].reshape(512, 512) for q in range(4)]

        @pl.loop(0, chunks)
        def _(i):
            r = pl.ds(pl.multiple_of(i * ROWS, ROWS), ROWS)
            v = mixed[r, :]
            for q in range(4):
                for half in range(2):
                    v = v + dot(ff[q, 2 + half, r, :], w_down[q][half * 256 : half * 256 + 256, :])
            if l == 0:
                stream[r, :] = v
            else:
                normed[r, :] = unturn(v, turn, i).astype(BF)

    have(("vec", 0, 0))
    for l in range(2):
        gain[l, 0:1, :] = spread(vec, l, 0, 16, 512, False)
        gain[l, 1:2, :] = spread(vec, l, 16, 16, 512, False)
        for k in range(3):
            bias[l, k : k + 1, :] = spread(vec, l, 32 + 32 * k, 32, 1024, True)
        tick()
    x_copy.wait()

    @pl.loop(0, chunks)
    def _(i):
        r = pl.ds(pl.multiple_of(i * ROWS, ROWS), ROWS)
        stream[r, :] = into_steps(normed[r, :].astype(F32), turn, i)

    spill("gain", gain, gain_hbm)
    for l in range(2):
        rms(stream, normed, gain[l, 0:1, :])
        settle(("keep", 0))
        settle(("q", 0))
        spill(("stream", l), stream, stream_hbm.at[l])
        have(("gate", l, 2))
        for p in range(4):
            gate_panel(l, p)
            if p % 2 == 1:
                tick()
        spill(("keep", l), keep, keep_hbm.at[l])
        carry_out(l)
        tick()
        settle(("hid", 0))
        settle(("mixed", 0))
        have(("gate", l, 3))
        carry_into(l)
        project(l)
        spill(("q", l), c3.at[:, pl.ds(0, 2)], q_hbm.at[l])
        spill(("hid", l), hid, hid_hbm.at[l])
        spill(("w4", l), w4.at[l], w4_hbm.at[l])
        spill(("mixed", l), mixed, mixed_hbm.at[l])
        for q in range(4):
            settle(("ff", 0, q))
            have(("up", l, q // 2))
            feed_up(l, q)
            spill(("ff", l, q), ff.at[q], ff_hbm.at[l, q])
            if q % 2 == 1:
                tick()
        spill(("up", l), up.at[l], up_hbm.at[l])
        have(("down", l, 1))
        settle(("stream", l))
        feed_down(l)
        spill(("dn", l), dn.at[l], dn_hbm.at[l])
    spill("result", normed, out_hbm)
    for key in list(spills):
        settle(key)
    gather.finish()


def forward(x, gate_weight, gate_bias, out_weight, gain_one, gain_two, up_weight, down_weight):
    rows = x.shape[0]
    any_space = pl.BlockSpec(memory_space=pl.ANY)
    packed = jnp.concatenate([gain_one, gain_two, gate_bias.reshape(2, 96)], axis=1).astype(F32)
    vec = jnp.pad(packed[:, None, :], ((0, 0), (0, 7), (0, 0)))
    args = (
        x,
        gate_weight.reshape(2, 3, 2, 32, 256),
        out_weight.transpose(0, 2, 1).reshape(2, 2, 32, 256),
        up_weight,
        down_weight.reshape(2, 2, 2, 16, 512),
        vec,
    )
    s = jax.ShapeDtypeStruct
    w4 = (2, 2, 2, 4, 4, 2, 2, 32, 256)
    up = (2, 2, 2, 4, 2, 2, 2, 16, 512)
    dn = (2, 4, 2, 2, 2, 2, 2, 16, 512)
    dma = pltpu.SemaphoreType.DMA
    return pl.pallas_call(
        fwd_kernel,
        name="forward",
        out_shape=(
            s((rows, 512), BF), s(w4, BF), s(up, BF), s(dn, BF), s((2, 8, 512), F32), s((2, rows, 512), F32),
            s((2, rows, 512), F32), s((2, 4, rows, 256), F32), s((2, 4, 2, rows, 256), BF),
            s((2, 4, rows, 256), BF), s((2, 4, 4, rows, 256), BF),
        ),
        in_specs=[any_space] * len(args),
        out_specs=(any_space,) * 11,
        scratch_shapes=[
            pltpu.VMEM(w4, BF), pltpu.VMEM(up, BF), pltpu.VMEM(dn, BF), pltpu.VMEM((4, 2, 2, 2, 2, 8, 128), F32),
            pltpu.VMEM((rows, 512), BF), pltpu.VMEM((rows, 512), F32), pltpu.VMEM((rows, 512), F32), pltpu.VMEM((4, rows, 128), F32),
            pltpu.VMEM((2, 3, 8, 1024), F32), pltpu.VMEM((3, 8, 1024), F32),
            pltpu.VMEM((4, rows, 256), F32), pltpu.VMEM((4, rows, 256), F32), pltpu.VMEM((4, 3, rows, 256), BF),
            pltpu.VMEM((4, rows, 256), BF), pltpu.VMEM((4, 4, rows, 256), BF),
            pltpu.VMEM((2, 8, 1024), F32), pltpu.VMEM((2, 8, 512), F32),
            pltpu.VMEM((2, 8, 1024), F32), pltpu.VMEM((2, 8, 1024), F32),
            dma((17, 12)), dma((17, 12)), dma((49,)), dma((32,)), dma((2,)), dma((2,)),
        ],
        compiler_params=pltpu.CompilerParams(
            collective_id=0, has_side_effects=True, vmem_limit_bytes=62 * 2**20
        ),
    )(*args)


class Scatter:
    def __init__(self, grads, landing, send, recv, give):
        self.grads = grads
        self.landing = landing
        self.send = send
        self.recv = recv
        self.give = give
        self.at = place()
        self.sent = {}
        self.queue = []
        self.active = []
        self.count = 0

    def own(self, item, z, x, y, c, h):
        kind, l, part = item
        w4, up, dn, vec = self.grads
        if kind == "vec":
            return vec.at[z, x, y, c, h]
        if kind == "gate":
            return w4.at[y, c, part, z, x, h]
        if kind == "up":
            return up.at[part, h, z, x, y, c]
        return dn.at[z, x, y, c, part, h]

    def land(self, item, stage, *where):
        kind, l, part = item
        ref = self.landing[("gate", "up", "down", "vec").index(kind)][stage]
        where = where if kind == "vec" else (l, part, *where)
        return ref.at[where] if where else ref

    def copy(self, n, slot, src, dst, target):
        return pltpu.make_async_remote_copy(
            src_ref=src,
            dst_ref=dst,
            send_sem=self.send.at[n, slot],
            recv_sem=self.recv.at[n, slot],
            device_id=target,
            device_id_type=MESH,
        )

    def go(self, n, slot, src, dst, target):
        cp = self.copy(n, slot, src, dst, target)
        cp.start()
        self.sent[n].append(cp)

    def landed(self, n, slot, dst, source):
        self.copy(n, slot, dst, dst, source).wait_recv()

    def add(self, item, stage):
        z, x, y, c = self.at
        kind = item[0]

        def plus(there, *where):
            there[...] = there[...] + self.land(item, stage, *where)[...]

        @pl.loop(0, 4)
        def _(n):
            if stage == 0:
                for i in range(2):
                    for j in range(2):
                        for h in range(2):
                            if kind == "gate":
                                plus(self.own(item, n, j, i, c, h), i, n, j, h)
                            elif kind == "up":
                                plus(self.own(item, n, i, j, c, h), h, n, i, j)
                            else:
                                plus(self.own(item, n, i, j, c, h), n, i, j, h)
            elif stage == 1:
                for i in range(2):
                    plus(self.own(item, n, i, y, c, 0), n, i)
            elif stage == 2:
                for i in range(2):
                    plus(self.own(item, n, x, i, c, 1), *((i, n) if kind == "gate" else (n, i)))
            else:
                for h in range(2):
                    plus(self.own(item, n, x, y, c, h), h, n)

    def total(self, item, h):
        z, x, y, c = self.at
        v = self.own(item, z, x, y, c, h)[...].astype(F32)
        for j in range(3):
            v = v + self.land(item, 4, j, h)[...].astype(F32)
        return v

    def stage(self, step, n, item):
        z, x, y, c = self.at
        v = lambda *where: self.own(item, *where)
        to_x = device(z, 1 - x, y, c)
        to_y = device(z, x, 1 - y, c)
        to_c = device(z, x, y, 1 - c)
        land = lambda *w: self.land(item, *w)
        if step == 0:
            self.go(n, 0, v(ALL, ALL, ALL, 1 - c, ALL), land(0), to_c)
        elif step == 1:
            self.landed(n, 0, land(0), to_c)
            self.add(item, 0)
            self.go(n, 1, v(ALL, ALL, 1 - y, c, 0), land(1), to_y)
            self.go(n, 2, v(ALL, 1 - x, ALL, c, 1), land(2), to_x)
        elif step == 2:
            self.landed(n, 1, land(1), to_y)
            self.add(item, 1)
            self.go(n, 3, v(ALL, 1 - x, y, c, 0), land(3, 0), to_x)
            self.landed(n, 2, land(2), to_x)
            self.add(item, 2)
            self.go(n, 4, v(ALL, x, 1 - y, c, 1), land(3, 1), to_y)
        elif step == 3:
            self.landed(n, 3, land(3, 0), to_x)
            self.landed(n, 4, land(3, 1), to_y)
            self.add(item, 3)
            for k in (1, 2, 3):
                there = lax.rem(z + k, 4)
                self.go(n, 4 + k, v(there, x, y, c, ALL), land(4, k - 1), device(there, x, y, c))
        else:
            for k in (1, 2, 3):
                source = lax.rem(z + 4 - k, 4)
                self.landed(n, 4 + k, land(4, k - 1), device(source, x, y, c))
            self.give(item, self)

    def tick(self, times=1):
        for _ in range(times):
            if self.queue:
                self.active.append([self.count, self.queue.pop(0), 0])
                self.sent[self.count] = []
                self.count += 1
            for entry in reversed(self.active):
                n, item, step = entry
                self.stage(step, n, item)
                entry[2] += 1
            self.active = [entry for entry in self.active if entry[2] < 5]

    def clear(self, kinds):
        while any(item[0] in kinds for item in self.queue + [entry[1] for entry in self.active]):
            self.tick()
        for n in list(self.sent):
            if all(entry[0] != n for entry in self.active):
                for cp in self.sent.pop(n):
                    cp.wait_send()


def spread_back(g, first, size, total, per_mp):
    r = lax.div(lax.broadcasted_iota(jnp.int32, (256, total), 0), 8)
    d = lax.broadcasted_iota(jnp.int32, (256, total), 1)
    if per_mp:
        owner = lax.div(lax.rem(d, total // 4), size) * 4 + lax.div(d, total // 4)
    else:
        owner = lax.div(d, size)
    rows = jnp.where(r == owner, g, 0.0)
    d = lax.broadcasted_iota(jnp.int32, (total, 128), 0)
    j = lax.broadcasted_iota(jnp.int32, (total, 128), 1)
    pick = jnp.where(j == first + lax.rem(d, size), 1.0, 0.0).astype(BF)
    high = rows.astype(BF)
    rest = rows - high.astype(F32)
    middle = rest.astype(BF)
    low = (rest - middle.astype(F32)).astype(BF)
    return dot(high, pick) + dot(middle, pick) + dot(low, pick)


def bwd_kernel(
    ct_in, w4_in, up_in, dn_in, gain_in, stream_in, mixed_in, keep_in, q_in, hid_in, ff_in,
    grad_hbm, gate_hbm, out_hbm, up_hbm, down_hbm, vec_hbm,
    w4, up, dn, gain, keep, pre, mixed, stream, ff, grad, acc, low, low_t, act_t, up_low, sg, c_out, c_in,
    ends, enter, gains, biases, g_w4, g_up, g_dn, g_vec,
    lw0, lw1, lw2, lw3, lw4, lu0, lu1, lu2, lu3, lu4, ld0, ld1, ld2, ld3, ld4, lv0, lv1, lv2, lv3, lv4,
    f_w4, f_up, f_dn, f_vec,
    rs_send, rs_recv, load_sem, save_sem, carry_send, carry_recv,
):
    z, x, y, c = place()
    mp = y * 2 + c
    rows_all = low.shape[0]
    chunks = rows_all // ROWS
    loads = {}
    n_load = 0
    saves = []

    def load(key, src, dst):
        nonlocal n_load
        cp = pltpu.make_async_copy(src, dst, load_sem.at[n_load])
        cp.start()
        loads[key] = cp
        n_load += 1

    def ready(key):
        loads.pop(key).wait()

    def save(src, dst):
        cp = pltpu.make_async_copy(src, dst, save_sem.at[len(saves)])
        cp.start()
        saves.append(cp)

    def load_feed(l):
        load("dn", dn_in.at[l], dn)
        load("up", up_in.at[l], up)

    def load_chunk(l, q):
        load(("ff", q), ff_in.at[l, q], ff.at[q % 2])

    def load_gates(l):
        load("w4", w4_in.at[l], w4)
        load("keep", keep_in.at[l], keep)
        load("q", q_in.at[l], pre.at[:, pl.ds(0, 2)])

    load("ct", ct_in, low)
    load("gain", gain_in, gain)
    load("mixed", mixed_in.at[1], mixed)
    load_feed(1)
    load_chunk(1, 0)
    load_chunk(1, 1)
    load_gates(1)
    load("stream", stream_in.at[1], stream)
    greet()

    def give(item, scatter):
        kind, l, part = item
        if kind == "gate":
            for h in range(2):
                f_w4[l, part, h] = scatter.total(item, h)
            save(f_w4.at[l, part], gate_hbm.at[l, part] if part < 3 else out_hbm.at[l])
        elif kind == "up":
            for h in range(2):
                f_up[l, part, h] = scatter.total(item, h)
                save(f_up.at[l, part, h], up_hbm.at[l, :, pl.ds((part * 2 + h) * 512, 512)])
        elif kind == "down":
            for h in range(2):
                f_dn[l, part, h] = scatter.total(item, h)
            save(f_dn.at[l, part], down_hbm.at[l, part])
        else:
            for h in range(2):
                f_vec[h] = scatter.total(item, h)
            save(f_vec, vec_hbm)

    landing = (
        (lw0, lw1, lw2, lw3, lw4), (lu0, lu1, lu2, lu3, lu4), (ld0, ld1, ld2, ld3, ld4), (lv0, lv1, lv2, lv3, lv4),
    )
    scatter = Scatter((g_w4, g_up, g_dn, g_vec), landing, rs_send, rs_recv, give)
    tick = scatter.tick

    def push(*item):
        scatter.queue.append(item)

    def each(fn):
        @pl.loop(0, chunks)
        def _(i):
            fn(i, pl.ds(pl.multiple_of(i * ROWS, ROWS), ROWS))

    def rms_t(src, dst_t, g):
        def part(i, r):
            v = src[r, :]
            scale = lax.rsqrt(jnp.mean(v * v, axis=-1, keepdims=True) + eps)
            dst_t[:, r] = (v * scale * g).astype(BF).T

        each(part)

    def feed(l, q):
        slot = q % 2
        w_down = dn[q].reshape(512, 512)
        w_up = up[q // 2, q % 2].reshape(512, 512)

        def part(i, r):
            act_grad = dot_nt(low[r, :], w_down)
            slope = jnp.concatenate([ff[slot, 0, r, :], ff[slot, 1, r, :]], axis=1).astype(F32)
            u = (act_grad * slope).astype(BF)
            up_low[r, :] = u
            back = dot_nt(u, w_up)
            acc[r, :] = back if q == 0 else acc[r, :] + back

        each(part)
        for half in range(2):
            g = dot(act_t[half * 256 : half * 256 + 256, :], up_low[...]).astype(BF)
            g_up[q // 2, q % 2, half * 2 : half * 2 + 2] = g.reshape(2, 2, 2, 2, 16, 512)
        for half in range(2):
            g = dot_tn(ff[slot, 2 + half], low[...]).astype(BF)
            g_dn[q, half] = g.reshape(2, 2, 2, 2, 16, 512)

    def rms_back(l, which, src, values_t):
        g = gain[l, which : which + 1, :]
        gains[l, which : which + 1, :] = jnp.zeros((1, 512), F32)

        def part(i, r):
            v = src[r, :]
            scale = lax.rsqrt(jnp.mean(v * v, axis=-1, keepdims=True) + eps)
            u = v * scale
            d = acc[r, :]
            gains[l, which : which + 1, :] += jnp.sum(d * u, axis=0, keepdims=True)
            dg = d * g
            new = grad[r, :] + scale * (dg - u * jnp.mean(dg * u, axis=-1, keepdims=True))
            grad[r, :] = new
            new = new.astype(BF)
            low[r, :] = new
            if values_t is not None:
                values_t[:, r] = new.T

        each(part)

    def out_back(p):
        g = dot(low_t[...], ff[0, p]).astype(BF)
        g_w4[p // 2, p % 2, 3] = g.reshape(4, 2, 2, 32, 256)

    def states_back(p):
        w = w4[p // 2, p % 2, 3].reshape(512, 256)

        def part(i, r):
            v = dot(low[r, :], w)
            share = keep[p, r, :]
            decay = 1.0 - share
            t = slice(ROWS - 8, ROWS)
            adjoint = v[t]
            parts = [adjoint]
            a = decay[t]
            passed = a * adjoint
            for j in range(STEPS - 2, -1, -1):
                t = slice(j * 8, j * 8 + 8)
                adjoint = v[t] + passed
                passed = decay[t] * adjoint
                a = a * decay[t]
                parts.append(adjoint)
            whole = jnp.concatenate(parts[::-1], axis=0)
            for n in range(2):
                sg[p * 2 + n, r, :] = whole[:, n * 128 : n * 128 + 128]
            columns = slice(p * 256, p * 256 + 256)
            ends[0, i, :, columns] = a
            ends[1, i, :, columns] = passed

        each(part)

    row = lax.broadcasted_iota(jnp.int32, (8, 1024), 0)
    first_chunk = first_of(mp, rows_all)

    def carries(entering):
        for i in range(chunks - 1, -1, -1):
            c0 = jnp.where(first_chunk == i + 1, 0.0, entering)
            a, v = combine(ends[0, i], ends[1, i], row, -1)
            enter[i] = jnp.where(row == 7, c0, pltpu.roll(a, 7, 0) * c0 + pltpu.roll(v, 7, 0))
            entering = jnp.broadcast_to(a[0:1] * c0[0:1] + v[0:1], (8, 1024))
        return entering

    def carry_copy(l, there):
        return pltpu.make_async_remote_copy(
            src_ref=c_out.at[l],
            dst_ref=c_in.at[l],
            send_sem=carry_send.at[l],
            recv_sem=carry_recv.at[l],
            device_id=device(z, x, lax.div(there, 2), lax.rem(there, 2)),
            device_id_type=MESH,
        )

    def carry_out(l):
        c_out[l] = carries(jnp.zeros((8, 1024), F32))

        @pl.when(mp > 0)
        def _():
            carry_copy(l, jnp.maximum(mp - 1, 0)).start()

    def carry_into(l):
        @pl.when(mp < 3)
        def _():
            carry_copy(l, jnp.minimum(mp + 1, 3)).wait_recv()
            carries(c_in[l])

        @pl.when(mp > 0)
        def _():
            carry_copy(l, jnp.maximum(mp - 1, 0)).wait_send()

    def gates_back(p):
        w = [w4[p // 2, p % 2, k].reshape(512, 256) for k in range(3)]

        def part(i, r):
            share = keep[p, r, :]
            local = jnp.concatenate([sg[p * 2, r, :], sg[p * 2 + 1, r, :]], axis=1)
            weight = enter[i, :, p * 256 : p * 256 + 256]
            parts = []
            for j in range(STEPS - 1, -1, -1):
                t = slice(j * 8, j * 8 + 8)
                parts.append(local[t] + weight)
                if j:
                    weight = weight - share[t] * weight
            adjoint = jnp.concatenate(parts[::-1], axis=0)
            back = None
            for k in range(3):
                v = share if k == 2 else pre[p, k, r, :].astype(F32)
                v = (adjoint * v).astype(BF)
                pre[p, k, r, :] = v
                d = dot_nt(v, w[k])
                back = d if back is None else back + d
            acc[r, :] = back if p == 0 else acc[r, :] + back

        each(part)

    def gate_grads(l, k):
        ones = jnp.ones((8, rows_all), BF)
        for p in range(4):
            values = pre[p, k]
            g_w4[p // 2, p % 2, k] = dot(act_t[...], values).astype(BF).reshape(4, 2, 2, 32, 256)
            biases[l, k : k + 1, p * 256 : p * 256 + 256] = dot(ones, values)[0:1, :]

    ready("ct")

    def widen(i, r):
        v = into_steps(low[r, :].astype(F32), sg, i)
        grad[r, :] = v
        low[r, :] = v.astype(BF)

    each(widen)
    ready("gain")
    for l in (1, 0):
        ready("mixed")
        rms_t(mixed, act_t, gain[l, 1:2, :])
        scatter.clear(("up", "down"))
        ready("dn")
        ready("up")
        for q in range(4):
            ready(("ff", q))
            feed(l, q)
            if q < 2:
                load_chunk(l, q + 2)
            elif q == 2:
                load("hid", hid_in.at[l], ff.at[0])
            if q % 2 == 1:
                push("up", l, q // 2)
            tick()
        push("down", l, 0)
        push("down", l, 1)
        rms_back(l, 1, mixed, low_t)
        tick()
        if l == 1:
            load_feed(0)
            load("mixed", mixed_in.at[0], mixed)
        scatter.clear(("gate",))
        ready("w4")
        ready("hid")
        for p in range(4):
            out_back(p)
        push("gate", l, 3)
        tick()
        if l == 1:
            load_chunk(0, 0)
        ready("keep")
        for p in range(4):
            states_back(p)
            if p == 1:
                tick()
        carry_out(l)
        ready("stream")
        rms_t(stream, act_t, gain[l, 0:1, :])
        tick()
        ready("q")
        carry_into(l)
        for p in range(4):
            gates_back(p)
            if p % 2 == 1:
                tick()
        for k in range(3):
            gate_grads(l, k)
            push("gate", l, k)
            tick()
        if l == 1:
            load_chunk(0, 1)
            load_gates(0)
        rms_back(l, 0, stream, None)
        if l == 1:
            load("stream", stream_in.at[0], stream)
            tick()
        rows = spread_back(gains[l, 0:1, :], 0, 16, 512, False) + spread_back(gains[l, 1:2, :], 16, 16, 512, False)
        for k in range(3):
            rows = rows + spread_back(biases[l, k : k + 1, :], 32 + 32 * k, 32, 1024, True)
        g_vec[:, :, :, :, l] = rows.reshape(4, 2, 2, 2, 8, 128)
    push("vec", 0, 0)
    tick()

    def finish(i, r):
        mixed[r, :] = unturn(grad[r, :], sg, i)

    each(finish)
    save(mixed, grad_hbm)
    scatter.clear(("vec", "gate", "up", "down"))
    for cp in saves:
        cp.wait()


def backward(cotangent, kept):
    w4_all, up_all, dn_all, gain, stream, mixed, keep, q, hid, ff = kept
    rows = cotangent.shape[0]
    any_space = pl.BlockSpec(memory_space=pl.ANY)
    s = jax.ShapeDtypeStruct
    dma = pltpu.SemaphoreType.DMA
    v = pltpu.VMEM
    args = (cotangent, w4_all, up_all, dn_all, gain, stream, mixed, keep, q, hid, ff)
    grad, gates, out, up, down, vec = pl.pallas_call(
        bwd_kernel,
        name="backward",
        out_shape=(
            s((rows, 512), F32), s((2, 3, 2, 32, 256), F32), s((2, 2, 32, 256), F32), s((2, 16, 2048), F32),
            s((2, 2, 2, 16, 512), F32), s((2, 8, 128), F32),
        ),
        in_specs=[any_space] * len(args),
        out_specs=(any_space,) * 6,
        scratch_shapes=[
            v((2, 2, 4, 4, 2, 2, 32, 256), BF), v((2, 2, 4, 2, 2, 2, 16, 512), BF), v((4, 2, 2, 2, 2, 2, 16, 512), BF),
            v((2, 8, 512), F32), v((4, rows, 256), F32), v((4, 3, rows, 256), BF), v((rows, 512), F32), v((rows, 512), F32),
            v((2, 4, rows, 256), BF), v((rows, 512), F32), v((rows, 512), F32), v((rows, 512), BF), v((512, rows), BF),
            v((512, rows), BF), v((rows, 512), BF), v((8, rows, 128), F32), v((2, 8, 1024), F32), v((2, 8, 1024), F32),
            v((2, 3, 8, 1024), F32), v((3, 8, 1024), F32), v((2, 8, 512), F32), v((2, 8, 1024), F32),
            v((2, 2, 4, 4, 2, 2, 32, 256), BF), v((2, 2, 4, 2, 2, 2, 16, 512), BF), v((4, 2, 2, 2, 2, 2, 16, 512), BF),
            v((4, 2, 2, 2, 2, 8, 128), F32),
            v((2, 4, 2, 4, 2, 2, 32, 256), BF), v((2, 4, 4, 2, 32, 256), BF), v((2, 4, 2, 4, 32, 256), BF),
            v((2, 4, 2, 4, 32, 256), BF), v((2, 4, 3, 2, 32, 256), BF),
            v((2, 2, 2, 4, 2, 2, 16, 512), BF), v((2, 2, 4, 2, 16, 512), BF), v((2, 2, 4, 2, 16, 512), BF),
            v((2, 2, 2, 4, 16, 512), BF), v((2, 2, 3, 2, 16, 512), BF),
            v((2, 2, 4, 2, 2, 2, 16, 512), BF), v((2, 2, 4, 2, 16, 512), BF), v((2, 2, 4, 2, 16, 512), BF),
            v((2, 2, 2, 4, 16, 512), BF), v((2, 2, 3, 2, 16, 512), BF),
            v((4, 2, 2, 2, 8, 128), F32), v((4, 2, 8, 128), F32), v((4, 2, 8, 128), F32), v((2, 4, 8, 128), F32),
            v((3, 2, 8, 128), F32),
            v((2, 4, 2, 32, 256), F32), v((2, 2, 2, 16, 512), F32), v((2, 2, 2, 16, 512), F32), v((2, 8, 128), F32),
            dma((17, 8)), dma((17, 8)), dma((32,)), dma((24,)), dma((2,)), dma((2,)),
        ],
        compiler_params=pltpu.CompilerParams(
            collective_id=1, has_side_effects=True, vmem_limit_bytes=63 * 2**20
        ),
    )(*args)
    vec = vec[:, 0, :]
    return (
        grad,
        gates.reshape(2, 3, 64, 256),
        vec[:, 32:].reshape(2, 3, 32),
        out.reshape(2, 64, 256).transpose(0, 2, 1),
        vec[:, :16],
        vec[:, 16:32],
        up,
        down.reshape(2, 64, 512),
    )


def fits(inputs, gate_weight, gate_bias, out_weight, gain_one, gain_two, up_weight, down_weight):
    rows = inputs.shape[0]
    shapes = (gate_weight.shape, gate_bias.shape, out_weight.shape, gain_one.shape, up_weight.shape, down_weight.shape)
    planned = ((2, 3, 64, 256), (2, 3, 32), (2, 256, 64), (2, 16), (2, 16, 2048), (2, 64, 512))
    axes = (lax.axis_size("dp"), lax.axis_size("mp"))
    return axes == (8, 4) and shapes == planned and rows == 768 and 4 * rows == 3 * LENGTH


def general_body(
    inputs,
    gate_weight,
    gate_bias,
    out_weight,
    norm_gain_one,
    norm_gain_two,
    up_weight,
    down_weight,
    cotangent,
):
    own_rows = inputs.shape[0]
    group = own_rows * lax.axis_size("mp")
    starts = (jnp.arange(group, dtype=jnp.int32) % LENGTH == 0)[:, None]
    layer_count = gate_weight.shape[0]
    width = gate_weight.shape[3]
    stream = inputs.astype(jnp.float32)
    saved = []
    held = []
    for layer_no in range(layer_count):
        gates_full, bias_full, out_full = (
            lax.all_gather(gate_weight[layer_no], "dp", axis=1, tiled=True),
            lax.all_gather(gate_bias[layer_no], "dp", axis=1, tiled=True),
            lax.all_gather(out_weight[layer_no], "dp", axis=1, tiled=True),
        )
        up_full, down_full, gain_first, gain_second = (
            lax.all_gather(up_weight[layer_no], ("dp", "mp"), axis=0, tiled=True),
            lax.all_gather(down_weight[layer_no], ("dp", "mp"), axis=0, tiled=True),
            lax.all_gather(norm_gain_one[layer_no], ("dp", "mp"), axis=0, tiled=True),
            lax.all_gather(norm_gain_two[layer_no], ("dp", "mp"), axis=0, tiled=True),
        )
        gain_first = gain_first.astype(jnp.float32)
        gain_second = gain_second.astype(jnp.float32)
        normed = rms_scale(stream, gain_first).astype(jnp.bfloat16)
        normed_all = lax.all_gather(normed, "mp", axis=0, tiled=True)
        pre_acts = (
            jnp.einsum("td,kdf->ktf", normed_all, gates_full, preferred_element_type=jnp.float32)
            + bias_full.astype(jnp.float32)[:, None, :]
        )
        decay, drive = gate_terms(pre_acts, starts)
        products, states = lax.associative_scan(link, (decay, drive), axis=0)
        hidden = states.astype(jnp.bfloat16)
        mixed = stream + lax.psum_scatter(
            dot_plain(hidden, out_full).astype(jnp.bfloat16), "mp", scatter_dimension=0, tiled=True
        ).astype(jnp.float32)
        second = rms_scale(mixed, gain_second).astype(jnp.bfloat16)
        up_acts = dot_plain(second, up_full)
        activated = jax.nn.gelu(up_acts).astype(jnp.bfloat16)
        saved.append(
            {
                "stream": stream,
                "gain_first": gain_first,
                "gain_second": gain_second,
                "normed": normed_all,
                "pre": pre_acts,
                "decay": decay,
                "states": states,
                "hidden": hidden,
                "mixed": mixed,
                "second": second,
                "up_acts": up_acts,
                "activated": activated,
            }
        )
        held.append((gates_full, out_full, up_full, down_full))
        stream = mixed + dot_plain(activated, down_full)
    grad = cotangent.astype(jnp.float32)
    gate_parts = []
    mlp_parts = []
    for layer_no in reversed(range(layer_count)):
        kept = saved[layer_no]
        gates_full, out_full, up_full, down_full = held[layer_no]
        grad_low = grad.astype(jnp.bfloat16)
        act_grad = dot_last(grad_low, down_full)
        down_grad = dot_first(kept["activated"], grad_low)
        unused_gelu, gelu_back = jax.vjp(jax.nn.gelu, kept["up_acts"])
        up_low = gelu_back(act_grad)[0].astype(jnp.bfloat16)
        up_grad = dot_first(kept["second"], up_low)
        second_grad = dot_last(up_low, up_full)
        unused_norm, norm_back = jax.vjp(rms_scale, kept["mixed"], kept["gain_second"])
        mixed_part, gain_two_grad = norm_back(second_grad)
        mixed_grad = grad + mixed_part
        mixed_low = mixed_grad.astype(jnp.bfloat16)
        mixed_all = lax.all_gather(mixed_low, "mp", axis=0, tiled=True)
        state_grad = dot_last(mixed_all, out_full)
        out_grad = dot_first(kept["hidden"], mixed_all)
        decay = kept["decay"]
        shifted = jnp.concatenate([decay[1:], jnp.ones((1, width), jnp.float32)], axis=0)
        back_products, back_partial = lax.associative_scan(
            link, (shifted[::-1], state_grad[::-1]), axis=0
        )
        adjoint = back_partial[::-1]
        previous = jnp.concatenate(
            [jnp.zeros((1, width), jnp.float32), kept["states"][:-1]], axis=0
        )
        unused_gate, gate_back = jax.vjp(partial(gate_terms, starts=starts), kept["pre"])
        pre_low = gate_back((adjoint * previous, adjoint))[0].astype(jnp.bfloat16)
        bias_grad = jnp.sum(pre_low.astype(jnp.float32), axis=1)
        gate_grad = jnp.einsum(
            "td,ktf->kdf", kept["normed"], pre_low, preferred_element_type=jnp.float32
        )
        normed_part = jnp.einsum(
            "ktf,kdf->td", pre_low, gates_full, preferred_element_type=jnp.float32
        )
        normed_grad = lax.psum_scatter(
            normed_part.astype(jnp.bfloat16), "mp", scatter_dimension=0, tiled=True
        ).astype(jnp.float32)
        unused_first, first_back = jax.vjp(rms_scale, kept["stream"], kept["gain_first"])
        stream_part, gain_one_grad = first_back(normed_grad)
        grad = mixed_grad + stream_part
        gate_parts.append(
            (
                sum_at_owner(gate_grad.astype(jnp.bfloat16), "dp", 1),
                sum_at_owner(bias_grad.astype(jnp.bfloat16), "dp", 1),
                sum_at_owner(out_grad.astype(jnp.bfloat16), "dp", 1),
            )
        )
        mlp_parts.append(
            (
                lax.psum_scatter(up_grad, ("dp", "mp"), scatter_dimension=0, tiled=True),
                lax.psum_scatter(down_grad, ("dp", "mp"), scatter_dimension=0, tiled=True),
                lax.psum_scatter(gain_one_grad, ("dp", "mp"), scatter_dimension=0, tiled=True),
                lax.psum_scatter(gain_two_grad, ("dp", "mp"), scatter_dimension=0, tiled=True),
            )
        )
    gate_parts = gate_parts[::-1]
    mlp_parts = mlp_parts[::-1]
    gate_stack = tuple((jnp.stack([entry[member] for entry in gate_parts]) for member in range(3)))
    mlp_stack = tuple((jnp.stack([entry[member] for entry in mlp_parts]) for member in range(4)))
    return (
        stream.astype(jnp.bfloat16),
        grad,
        gate_stack[0],
        gate_stack[1],
        gate_stack[2],
        mlp_stack[2],
        mlp_stack[3],
        mlp_stack[0],
        mlp_stack[1],
    )


def body(inputs, gate_weight, gate_bias, out_weight, gain_one, gain_two, up_weight, down_weight, cotangent):
    shards = (gate_weight, gate_bias, out_weight, gain_one, gain_two, up_weight, down_weight)
    if not fits(inputs, *shards):
        return general_body(inputs, *shards, cotangent)
    out, *kept = forward(inputs, *shards)
    grad, gates, biases, out_grad, gain_a, gain_b, up, down = backward(cotangent, kept)
    return (out, grad, gates, biases, out_grad, gain_a, gain_b, up, down)


def solution(mesh):
    placed = (
        P(("dp", "mp"), None),
        P(None, None, "dp", "mp"),
        P(None, None, ("mp", "dp")),
        P(None, "mp", "dp"),
        P(None, ("dp", "mp")),
        P(None, ("dp", "mp")),
        P(None, ("dp", "mp"), None),
        P(None, ("dp", "mp"), None),
        P(("dp", "mp"), None),
    )
    return jax.shard_map(
        body,
        mesh=mesh,
        in_specs=placed,
        out_specs=(
            P(("dp", "mp"), None),
            P(("dp", "mp"), None),
            P(None, None, "dp", "mp"),
            P(None, None, ("mp", "dp")),
            P(None, "mp", "dp"),
            P(None, ("dp", "mp")),
            P(None, ("dp", "mp")),
            P(None, ("dp", "mp"), None),
            P(None, ("dp", "mp"), None),
        ),
        check_vma=False,
    )
```

```python
from functools import partial

import jax
import jax.numpy as jnp
from jax import lax
from jax.experimental import pallas as pl
from jax.experimental.pallas import tpu as pltpu
from jax.sharding import PartitionSpec as P

LENGTH = 1024


eps = 1e-06


def cut_along(x, dim, size):
    shape = x.shape
    blocks = x.reshape(*shape[:dim], size, shape[dim] // size, *shape[dim + 1 :])
    return jnp.moveaxis(blocks, dim, 0)


def sum_at_owner(x, axis, dim):
    size = lax.axis_size(axis)
    blocks = lax.all_to_all(cut_along(x, dim, size), axis, 0, 0, tiled=True)
    return jnp.sum(blocks.astype(jnp.float32), axis=0)


def rms_scale(values, gain):
    return values * lax.rsqrt(jnp.mean(values * values, axis=-1, keepdims=True) + eps) * gain


def link(earlier, later):
    return (earlier[0] * later[0], later[0] * earlier[1] + later[1])


def gate_terms(pre_acts, starts):
    sig_forget = jax.nn.sigmoid(pre_acts[0])
    sig_input = jax.nn.sigmoid(pre_acts[1])
    total = sig_forget + sig_input
    decay = jnp.where(starts, 0.0, sig_forget / total)
    return (decay, sig_input / total * pre_acts[2])


def dot_plain(left, right):
    return jnp.dot(left, right, preferred_element_type=jnp.float32)


def dot_first(left, right):
    return lax.dot_general(
        left, right, (((0,), (0,)), ((), ())), preferred_element_type=jnp.float32
    )


def dot_last(left, right):
    return lax.dot_general(
        left, right, (((1,), (1,)), ((), ())), preferred_element_type=jnp.float32
    )


GATHER_PLAN = (
    (0, 5, 10, 15, 1, 20, 6, 25, 2, 11, 30, 7, 3, 16, 35, 12, 4),
    (),
    (),
    (),
    (21, 40, 8, 17, 26, 45, 9, 13, 31, 50, 22, 36, 55, 14, 18, 27, 41, 60, 32, 19),
    (),
    (46, 65, 23),
    (51, 70, 37),
    (56, 75, 28, 42, 24),
    (),
    (61, 80, 33),
    (66, 47, 29),
    (52,),
    (),
    (71, 34),
    (),
    (57, 76, 38),
    (),
    (),
    (81, 43, 62, 39, 67, 44),
    (),
    (48,),
    (53, 72, 49, 54, 58, 77, 82, 59),
    (),
    (),
    (63,),
    (68,),
    (73, 64),
    (),
    (69,),
    (78, 74),
    (),
    (),
    (),
    (83,),
    (),
    (79,),
    (84,),
    (),
)
SCATTER_PLAN = (
    (),
    (),
    (),
    (),
    (0,),
    (),
    (),
    (),
    (5,),
    (10, 15),
    (1,),
    (20,),
    (),
    (),
    (6,),
    (11,),
    (16, 21, 2),
    (),
    (7,),
    (),
    (12,),
    (25,),
    (30, 17),
    (35,),
    (22,),
    (26, 31, 3, 8, 36, 13),
    (18, 23, 27, 4, 32, 9, 37, 14, 28, 33, 19),
    (),
    (),
    (38,),
    (40, 24),
    (),
    (),
    (29,),
    (45,),
    (50, 55),
    (41, 34),
    (39,),
    (60,),
    (),
    (46,),
    (51,),
    (56,),
    (61, 42),
    (),
    (47,),
    (),
    (52,),
    (65,),
    (70, 57),
    (75,),
    (62,),
    (80, 66, 43, 48),
    (71, 76, 53, 81, 58, 63, 44, 67, 49, 72, 54, 77, 82, 68, 59, 73, 78, 83, 64, 69, 74, 79, 84),
)


ALL = slice(None)
MESH = pl.DeviceIdType.MESH
BF = jnp.bfloat16
F32 = jnp.float32
SHIFT = 0.25
LOG_SHIFT = -1.3862943611198906
TOP = 87.0
GELU_A = 0.7978845608028654
GELU_B = 0.044715
ROWS = 256
STEPS = ROWS // 8


def first_of(mp, rows):
    return lax.div(jnp.minimum(lax.rem(mp * (LENGTH - rows), LENGTH), rows), ROWS)


def place():
    dp = lax.axis_index("dp")
    mp = lax.axis_index("mp")
    return (lax.div(dp, 2), lax.rem(dp, 2), lax.div(mp, 2), lax.rem(mp, 2))


def device(z, x, y, c):
    return (z * 2 + x, y * 2 + c)


def greet():
    z, x, y, c = place()
    partners = [device(lax.rem(z + k, 4), x, y, c) for k in (1, 2, 3)]
    partners += [device(z, 1 - x, y, c), device(z, x, 1 - y, c)]
    partners += [device(z, x, y, 1 - c), device(z, x, 1 - y, 1 - c)]
    barrier = pltpu.get_barrier_semaphore()
    for partner in partners:
        pl.semaphore_signal(barrier, inc=1, device_id=partner, device_id_type=MESH)
    pl.semaphore_wait(barrier, len(partners))


class Gather:
    def __init__(self, bufs, own, items, plan, send, recv):
        self.bufs = bufs
        self.own = own
        self.items = items
        self.send = send
        self.recv = recv
        self.at = place()
        self.sent = []
        self.plan = [list(row) for row in plan]

    def view(self, item, z, x, y, c, h):
        kind, l, part = item
        w4, up, dn, vec = self.bufs
        if kind == "vec":
            return vec.at[z, x, y, c, h]
        if kind == "gate":
            return w4.at[l, y, c, part, z, x, h]
        if kind == "up":
            return up.at[l, part, h, z, x, y, c]
        return dn.at[l, z, x, y, c, part, h]

    def go(self, n, slot, ref, target):
        cp = pltpu.make_async_remote_copy(
            src_ref=ref,
            dst_ref=ref,
            send_sem=self.send.at[n, slot],
            recv_sem=self.recv.at[n, slot],
            device_id=target,
            device_id_type=MESH,
        )
        cp.start()
        self.sent.append(cp)

    def landed(self, n, slot, ref, source):
        pltpu.make_async_remote_copy(
            src_ref=ref,
            dst_ref=ref,
            send_sem=self.send.at[n, slot],
            recv_sem=self.recv.at[n, slot],
            device_id=source,
            device_id_type=MESH,
        ).wait_recv()

    def stage(self, step, n, item):
        z, x, y, c = self.at
        v = lambda *where: self.view(item, *where)
        to_x = device(z, 1 - x, y, c)
        to_y = device(z, x, 1 - y, c)
        to_c = device(z, x, y, 1 - c)
        if step == 0:
            for cp in self.own.pop(item):
                cp.wait()
            for k in (1, 2, 3):
                self.go(n, k - 1, v(z, x, y, c, ALL), device(lax.rem(z + k, 4), x, y, c))
        elif step == 1:
            for k in (1, 2, 3):
                source = lax.rem(z + 4 - k, 4)
                self.landed(n, k - 1, v(source, x, y, c, ALL), device(source, x, y, c))
            self.go(n, 3, v(ALL, x, y, c, 0), to_x)
            self.go(n, 4, v(ALL, x, y, c, 1), to_y)
            self.go(n, 7, v(ALL, x, y, c, ALL), to_c)
        elif step == 2:
            self.landed(n, 3, v(ALL, 1 - x, y, c, 0), to_x)
            self.go(n, 5, v(ALL, ALL, y, c, 0), to_y)
            self.landed(n, 4, v(ALL, x, 1 - y, c, 1), to_y)
            self.go(n, 6, v(ALL, x, ALL, c, 1), to_x)
            self.go(n, 8, v(ALL, 1 - x, y, c, 0), to_c)
            self.go(n, 9, v(ALL, x, 1 - y, c, 1), to_c)
        elif step == 3:
            self.landed(n, 5, v(ALL, ALL, 1 - y, c, 0), to_y)
            self.go(n, 10, v(ALL, ALL, 1 - y, c, 0), to_c)
            self.landed(n, 6, v(ALL, 1 - x, ALL, c, 1), to_x)
            self.go(n, 11, v(ALL, 1 - x, ALL, c, 1), to_c)
        else:
            self.landed(n, 7, v(ALL, x, y, 1 - c, ALL), to_c)
            self.landed(n, 8, v(ALL, 1 - x, y, 1 - c, 0), to_c)
            self.landed(n, 9, v(ALL, x, 1 - y, 1 - c, 1), to_c)
            self.landed(n, 10, v(ALL, ALL, 1 - y, 1 - c, 0), to_c)
            self.landed(n, 11, v(ALL, 1 - x, ALL, 1 - c, 1), to_c)

    def go_on(self):
        for code in self.plan.pop(0):
            n, step = divmod(code, 5)
            self.stage(step, n, self.items[n])

    def finish(self):
        for cp in self.sent:
            cp.wait_send()


def dot(a, b):
    return jnp.dot(a, b, preferred_element_type=F32)


def dot_nt(a, b):
    return lax.dot_general(a, b, (((1,), (1,)), ((), ())), preferred_element_type=F32)


def dot_tn(a, b):
    return lax.dot_general(a, b, (((0,), (0,)), ((), ())), preferred_element_type=F32)


def spread(vec, l, first, size, total, per_mp):
    rows = vec[:, :, :, :, l].reshape(256, 128).astype(BF)
    j = lax.broadcasted_iota(jnp.int32, (128, total), 0)
    d = lax.broadcasted_iota(jnp.int32, (128, total), 1)
    pick = jnp.where(j == first + lax.rem(d, size), 1.0, 0.0).astype(BF)
    wide = dot(rows, pick)
    r = lax.div(lax.broadcasted_iota(jnp.int32, (256, total), 0), 8)
    d = lax.broadcasted_iota(jnp.int32, (256, total), 1)
    if per_mp:
        owner = lax.div(lax.rem(d, total // 4), size) * 4 + lax.div(d, total // 4)
    else:
        owner = lax.div(d, size)
    return jnp.sum(jnp.where(r == owner, wide, 0.0), axis=0, keepdims=True)


def combine(a, b, row, sign):
    for s in (1, 2, 4):
        keep = (row >= s) if sign > 0 else (row < 8 - s)
        by = s if sign > 0 else 8 - s
        am = jnp.where(keep, a, 0.0)
        b = b + am * pltpu.roll(b, by, 0)
        if s < 4:
            a = jnp.where(keep, a * pltpu.roll(a, by, 0), a)
        else:
            a = jnp.where(keep, a * pltpu.roll(a, by, 0), a)
    return a, b


def into_steps(v, turn, i):
    for n in range(4):
        turn[n, pl.ds(i * ROWS, ROWS), :] = v[:, n * 128 : n * 128 + 128]
    parts = []
    for n in range(4):
        rows = [turn[n, pl.ds(i * ROWS + j, 8, stride=STEPS), :] for j in range(STEPS)]
        parts.append(jnp.concatenate(rows, axis=0))
    return jnp.concatenate(parts, axis=1)


def unturn(v, turn, i):
    for n in range(4):
        for j in range(STEPS):
            turn[n, pl.ds(i * ROWS + j, 8, stride=STEPS), :] = v[j * 8 : j * 8 + 8, n * 128 : n * 128 + 128]
    return jnp.concatenate([turn[n, pl.ds(i * ROWS, ROWS), :] for n in range(4)], axis=1)


def fwd_kernel(
    x_in, gate_in, out_in, up_in, down_in, gain_one_in, gain_two_in, bias_in,
    out_hbm, w4_hbm, up_hbm, dn_hbm, gain_hbm, stream_hbm, mixed_hbm, keep_hbm, q_hbm, hid_hbm, ff_hbm,
    w4, up, dn, vec, normed, stream, mixed, turn, ends, enter, keep, states, c3, hid, ff, bias, gain, c_out, c_in,
    ag_send, ag_recv, own_sem, spill_sem, carry_send, carry_recv,
):
    z, x, y, c = place()
    mp = y * 2 + c
    rows_all = normed.shape[0]
    chunks = rows_all // ROWS
    fill = []

    def local(src, dst, sem):
        cp = pltpu.make_async_copy(src, dst, sem)
        cp.start()
        return cp

    own = {}
    n_own = 0

    def add_own(key, src, dst):
        nonlocal n_own
        own.setdefault(key, []).append(local(src, dst, own_sem.at[n_own]))
        n_own += 1

    x_copy = local(x_in, normed, own_sem.at[48])
    own[("vec", 0, 0)] = []
    vec[z, x, y, c] = jnp.zeros((2, 8, 128), F32)
    for l in range(2):
        ours = [gain_one_in[l : l + 1, :], gain_two_in[l : l + 1, :]] + [bias_in[k, l : l + 1, :] for k in range(3)]
        vec[z, x, y, c, l, 0:1, :] = jnp.concatenate([v.astype(F32) for v in ours], axis=1)
    for l in range(2):
        for k in range(3):
            add_own(("gate", l, k), gate_in.at[l, k], w4.at[l, y, c, k, z, x])
        add_own(("gate", l, 3), out_in.at[l], w4.at[l, y, c, 3, z, x])
        for pair in range(2):
            for h in range(2):
                columns = pl.ds((pair * 2 + h) * 512, 512)
                add_own(("up", l, pair), up_in.at[l, :, columns], up.at[l, pair, h, z, x, y, c])
            add_own(("down", l, pair), down_in.at[l, pair], dn.at[l, z, x, y, c, pair])
    greet()
    items = [("vec", 0, 0)]
    for l in range(2):
        items += [("gate", l, k) for k in range(4)]
        items += [(kind, l, pair) for kind in ("up", "down") for pair in range(2)]
    gather = Gather((w4, up, dn, vec), own, items, GATHER_PLAN, ag_send, ag_recv)
    go_on = gather.go_on

    n_spill = 0
    spills = {}

    def spill(key, src, dst):
        nonlocal n_spill
        spills[key] = local(src, dst, spill_sem.at[n_spill])
        n_spill += 1

    def settle(key):
        if key in spills:
            spills.pop(key).wait()


    def rms(src, dst, g):
        @pl.loop(0, chunks)
        def _(i):
            r = pl.ds(pl.multiple_of(i * ROWS, ROWS), ROWS)
            v = src[r, :]
            scale = lax.rsqrt(jnp.mean(v * v, axis=-1, keepdims=True) + eps)
            dst[r, :] = (v * scale * g).astype(BF)

    def gate_panel(l, p):
        w = [w4[l, p // 2, p % 2, k].reshape(512, 256) for k in range(3)]
        bs = [bias[l, k : k + 1, p * 256 : (p + 1) * 256] for k in range(3)]

        @pl.loop(0, chunks)
        def _(i):
            r = pl.ds(pl.multiple_of(i * ROWS, ROWS), ROWS)
            n = normed[r, :]
            f, inp, cand = [dot(n, w[k]) + bs[k] for k in range(3)]
            e_f = jnp.exp(jnp.minimum(-f, TOP) + LOG_SHIFT)
            e_i = jnp.exp(jnp.minimum(-inp, TOP) + LOG_SHIFT)
            a_f = e_f + SHIFT
            a_i = e_i + SHIFT
            total = a_f + a_i
            inv = pl.reciprocal(total, approx=True)
            inv = inv * (2.0 - total * inv)
            share = a_f * inv
            decay = a_i * inv
            drive = share * cand
            keep[p, r, :] = share
            c3[p, 0, r, :] = (decay * (e_f * inv)).astype(BF)
            c3[p, 1, r, :] = (share * (e_i * inv)).astype(BF)
            c3[p, 2, r, :] = cand.astype(BF)
            s = drive[0:8]
            a = decay[0:8]
            local_states = [s]
            for j in range(1, STEPS):
                t = slice(j * 8, j * 8 + 8)
                s = decay[t] * s + drive[t]
                a = a * decay[t]
                local_states.append(s)
            states[p, r, :] = jnp.concatenate(local_states, axis=0)
            columns = slice(p * 256, p * 256 + 256)
            ends[0, i, :, columns] = a
            ends[1, i, :, columns] = s

    row = lax.broadcasted_iota(jnp.int32, (8, 1024), 0)
    first_chunk = first_of(mp, rows_all)

    def carries(entering):
        for i in range(chunks):
            c0 = jnp.where(first_chunk == i, 0.0, entering)
            a, s = combine(ends[0, i], ends[1, i], row, 1)
            enter[i] = jnp.where(row == 0, c0, pltpu.roll(a, 1, 0) * c0 + pltpu.roll(s, 1, 0))
            entering = jnp.broadcast_to(a[7:8] * c0[7:8] + s[7:8], (8, 1024))
        return entering

    def carry_copy(l, there):
        return pltpu.make_async_remote_copy(
            src_ref=c_out.at[l],
            dst_ref=c_in.at[l],
            send_sem=carry_send.at[l],
            recv_sem=carry_recv.at[l],
            device_id=device(z, x, lax.div(there, 2), lax.rem(there, 2)),
            device_id_type=MESH,
        )

    def carry_out(l):
        c_out[l] = carries(jnp.zeros((8, 1024), F32))

        @pl.when(mp < 3)
        def _():
            carry_copy(l, jnp.minimum(mp + 1, 3)).start()

    def carry_into(l):
        @pl.when(mp > 0)
        def _():
            carry_copy(l, jnp.maximum(mp - 1, 0)).wait_recv()
            carries(c_in[l])

        @pl.when(mp < 3)
        def _():
            carry_copy(l, jnp.minimum(mp + 1, 3)).wait_send()

    def project(l):
        g = gain[l, 1:2, :]
        w = [w4[l, p // 2, p % 2, 3].reshape(512, 256) for p in range(4)]

        @pl.loop(0, chunks)
        def _(i):
            r = pl.ds(pl.multiple_of(i * ROWS, ROWS), ROWS)
            v = stream[r, :]
            for p in range(4):
                share = keep[p, r, :]
                s_local = states[p, r, :]
                cand = c3[p, 2, r, :].astype(F32)
                enters = enter[i, :, p * 256 : p * 256 + 256]
                before = enters
                weight = enters
                now, gap = [], []
                for j in range(STEPS):
                    t = slice(j * 8, j * 8 + 8)
                    weight = weight - share[t] * weight
                    s = s_local[t] + weight
                    gap.append(before - cand[t])
                    now.append(s)
                    before = s
                gap = jnp.concatenate(gap, axis=0)
                h = jnp.concatenate(now, axis=0).astype(BF)
                hid[p, r, :] = h
                c3[p, 0, r, :] = (gap * c3[p, 0, r, :].astype(F32)).astype(BF)
                c3[p, 1, r, :] = (-gap * c3[p, 1, r, :].astype(F32)).astype(BF)
                v = v + dot_nt(h, w[p])
            mixed[r, :] = v
            scale = lax.rsqrt(jnp.mean(v * v, axis=-1, keepdims=True) + eps)
            normed[r, :] = (v * scale * g).astype(BF)

    def feed_up(l, q):
        w_up = up[l, q // 2, q % 2].reshape(512, 512)

        @pl.loop(0, chunks)
        def _(i):
            r = pl.ds(pl.multiple_of(i * ROWS, ROWS), ROWS)
            u = dot(normed[r, :], w_up)
            sq = u * u
            t = jnp.tanh(u * (GELU_A + (GELU_A * GELU_B) * sq))
            gate = 0.5 + 0.5 * t
            act = (u * gate).astype(BF)
            slope = gate + (0.5 * u) * (1.0 - t * t) * (GELU_A + (3.0 * GELU_A * GELU_B) * sq)
            for half in range(2):
                side = slice(half * 256, half * 256 + 256)
                ff[q, half, r, :] = slope[:, side].astype(BF)
                ff[q, 2 + half, r, :] = act[:, side]

    def feed_down(l):
        w_down = dn[l].reshape(2048, 512)

        @pl.loop(0, chunks)
        def _(i):
            r = pl.ds(pl.multiple_of(i * ROWS, ROWS), ROWS)
            acts = [ff[q, 2 + half, r, :] for q in range(4) for half in range(2)]
            v = mixed[r, :] + dot(jnp.concatenate(acts, axis=1), w_down)
            if l == 0:
                stream[r, :] = v
            else:
                normed[r, :] = unturn(v, turn, i).astype(BF)

    go_on()
    for l in range(2):
        gain[l, 0:1, :] = spread(vec, l, 0, 16, 512, False)
        gain[l, 1:2, :] = spread(vec, l, 16, 16, 512, False)
        for k in range(3):
            bias[l, k : k + 1, :] = spread(vec, l, 32 + 32 * k, 32, 1024, True)
        go_on()
    x_copy.wait()

    @pl.loop(0, chunks)
    def _(i):
        r = pl.ds(pl.multiple_of(i * ROWS, ROWS), ROWS)
        stream[r, :] = into_steps(normed[r, :].astype(F32), turn, i)

    spill("gain", gain, gain_hbm)
    for l in range(2):
        rms(stream, normed, gain[l, 0:1, :])
        settle(("keep", 0))
        settle(("q", 0))
        spill(("stream", l), stream, stream_hbm.at[l])
        go_on()
        go_on()
        for p in range(4):
            gate_panel(l, p)
            go_on()
        spill(("keep", l), keep, keep_hbm.at[l])
        carry_out(l)
        settle(("hid", 0))
        settle(("mixed", 0))
        go_on()
        carry_into(l)
        project(l)
        spill(("q", l), c3.at[:, pl.ds(0, 2)], q_hbm.at[l])
        spill(("hid", l), hid, hid_hbm.at[l])
        spill(("w4", l), w4.at[l], w4_hbm.at[l])
        spill(("mixed", l), mixed, mixed_hbm.at[l])
        go_on()
        for q in range(4):
            settle(("ff", 0, q))
            go_on()
            feed_up(l, q)
            spill(("ff", l, q), ff.at[q], ff_hbm.at[l, q])
            go_on()
        spill(("up", l), up.at[l], up_hbm.at[l])
        settle(("stream", l))
        go_on()
        feed_down(l)
        spill(("dn", l), dn.at[l], dn_hbm.at[l])
        go_on()
    spill("result", normed, out_hbm)
    for key in list(spills):
        settle(key)
    gather.finish()


def forward(x, gate_weight, gate_bias, out_weight, gain_one, gain_two, up_weight, down_weight):
    rows = x.shape[0]
    any_space = pl.BlockSpec(memory_space=pl.ANY)
    args = (
        x,
        gate_weight.reshape(2, 3, 2, 32, 256),
        out_weight.transpose(0, 2, 1).reshape(2, 2, 32, 256),
        up_weight,
        down_weight.reshape(2, 2, 2, 16, 512),
        gain_one,
        gain_two,
        gate_bias.transpose(1, 0, 2),
    )
    s = jax.ShapeDtypeStruct
    w4 = (2, 2, 2, 4, 4, 2, 2, 32, 256)
    up = (2, 2, 2, 4, 2, 2, 2, 16, 512)
    dn = (2, 4, 2, 2, 2, 2, 2, 16, 512)
    dma = pltpu.SemaphoreType.DMA
    return pl.pallas_call(
        fwd_kernel,
        name="forward",
        out_shape=(
            s((rows, 512), BF), s(w4, BF), s(up, BF), s(dn, BF), s((2, 8, 512), F32), s((2, rows, 512), F32),
            s((2, rows, 512), F32), s((2, 4, rows, 256), F32), s((2, 4, 2, rows, 256), BF),
            s((2, 4, rows, 256), BF), s((2, 4, 4, rows, 256), BF),
        ),
        in_specs=[any_space] * 5 + [pl.BlockSpec(memory_space=pltpu.VMEM)] * 3,
        out_specs=(any_space,) * 11,
        scratch_shapes=[
            pltpu.VMEM(w4, BF), pltpu.VMEM(up, BF), pltpu.VMEM(dn, BF), pltpu.VMEM((4, 2, 2, 2, 2, 8, 128), F32),
            pltpu.VMEM((rows, 512), BF), pltpu.VMEM((rows, 512), F32), pltpu.VMEM((rows, 512), F32), pltpu.VMEM((4, rows, 128), F32),
            pltpu.VMEM((2, 3, 8, 1024), F32), pltpu.VMEM((3, 8, 1024), F32),
            pltpu.VMEM((4, rows, 256), F32), pltpu.VMEM((4, rows, 256), F32), pltpu.VMEM((4, 3, rows, 256), BF),
            pltpu.VMEM((4, rows, 256), BF), pltpu.VMEM((4, 4, rows, 256), BF),
            pltpu.VMEM((2, 8, 1024), F32), pltpu.VMEM((2, 8, 512), F32),
            pltpu.VMEM((2, 8, 1024), F32), pltpu.VMEM((2, 8, 1024), F32),
            dma((17, 12)), dma((17, 12)), dma((49,)), dma((32,)), dma((2,)), dma((2,)),
        ],
        compiler_params=pltpu.CompilerParams(
            collective_id=0, has_side_effects=True, vmem_limit_bytes=62 * 2**20
        ),
    )(*args)


class Scatter:
    def __init__(self, grads, landing, plan, send, recv, give):
        self.grads = grads
        self.landing = landing
        self.send = send
        self.recv = recv
        self.give = give
        self.at = place()
        self.sent = {}
        self.items = []
        self.plan = [list(row) for row in plan]

    def own(self, item, z, x, y, c, h):
        kind, l, part = item
        w4, up, dn, vec = self.grads
        if kind == "vec":
            return vec.at[z, x, y, c, h]
        if kind == "gate":
            return w4.at[y, c, part, z, x, h]
        if kind == "up":
            return up.at[part, h, z, x, y, c]
        return dn.at[z, x, y, c, part, h]

    def land(self, item, stage, *where):
        kind, l, part = item
        ref = self.landing[("gate", "up", "down", "vec").index(kind)][stage]
        where = where if kind == "vec" else (l, part, *where)
        return ref.at[where] if where else ref

    def copy(self, n, slot, src, dst, target):
        return pltpu.make_async_remote_copy(
            src_ref=src,
            dst_ref=dst,
            send_sem=self.send.at[n, slot],
            recv_sem=self.recv.at[n, slot],
            device_id=target,
            device_id_type=MESH,
        )

    def go(self, n, slot, src, dst, target):
        cp = self.copy(n, slot, src, dst, target)
        cp.start()
        self.sent.setdefault(n, []).append(cp)

    def landed(self, n, slot, dst, source):
        self.copy(n, slot, dst, dst, source).wait_recv()

    def add(self, item, stage):
        z, x, y, c = self.at
        kind = item[0]

        def plus(there, *where):
            there[...] = there[...] + self.land(item, stage, *where)[...]

        @pl.loop(0, 4)
        def _(n):
            if stage == 0:
                for i in range(2):
                    for j in range(2):
                        for h in range(2):
                            if kind == "gate":
                                plus(self.own(item, n, j, i, c, h), i, n, j, h)
                            elif kind == "up":
                                plus(self.own(item, n, i, j, c, h), h, n, i, j)
                            else:
                                plus(self.own(item, n, i, j, c, h), n, i, j, h)
            elif stage == 1:
                for i in range(2):
                    plus(self.own(item, n, i, y, c, 0), n, i)
            elif stage == 2:
                for i in range(2):
                    plus(self.own(item, n, x, i, c, 1), *((i, n) if kind == "gate" else (n, i)))
            else:
                for h in range(2):
                    plus(self.own(item, n, x, y, c, h), h, n)

    def total(self, item, h):
        z, x, y, c = self.at
        v = self.own(item, z, x, y, c, h)[...].astype(F32)
        for j in range(3):
            v = v + self.land(item, 4, j, h)[...].astype(F32)
        return v

    def stage(self, step, n, item):
        z, x, y, c = self.at
        v = lambda *where: self.own(item, *where)
        to_x = device(z, 1 - x, y, c)
        to_y = device(z, x, 1 - y, c)
        to_c = device(z, x, y, 1 - c)
        land = lambda *w: self.land(item, *w)
        if step == 0:
            self.go(n, 0, v(ALL, ALL, ALL, 1 - c, ALL), land(0), to_c)
        elif step == 1:
            self.landed(n, 0, land(0), to_c)
            self.add(item, 0)
            self.go(n, 1, v(ALL, ALL, 1 - y, c, 0), land(1), to_y)
            self.go(n, 2, v(ALL, 1 - x, ALL, c, 1), land(2), to_x)
        elif step == 2:
            self.landed(n, 1, land(1), to_y)
            self.add(item, 1)
            self.go(n, 3, v(ALL, 1 - x, y, c, 0), land(3, 0), to_x)
            self.landed(n, 2, land(2), to_x)
            self.add(item, 2)
            self.go(n, 4, v(ALL, x, 1 - y, c, 1), land(3, 1), to_y)
        elif step == 3:
            self.landed(n, 3, land(3, 0), to_x)
            self.landed(n, 4, land(3, 1), to_y)
            self.add(item, 3)
            for k in (1, 2, 3):
                there = lax.rem(z + k, 4)
                self.go(n, 4 + k, v(there, x, y, c, ALL), land(4, k - 1), device(there, x, y, c))
        else:
            for k in (1, 2, 3):
                source = lax.rem(z + 4 - k, 4)
                self.landed(n, 4 + k, land(4, k - 1), device(source, x, y, c))
            self.give(item, self)

    def go_on(self):
        for code in self.plan.pop(0):
            n, step = divmod(code, 5)
            self.stage(step, n, self.items[n])

    def settle(self, numbers):
        for n in numbers:
            for cp in self.sent.pop(n):
                cp.wait_send()


def spread_back(g, first, size, total, per_mp):
    r = lax.div(lax.broadcasted_iota(jnp.int32, (256, total), 0), 8)
    d = lax.broadcasted_iota(jnp.int32, (256, total), 1)
    if per_mp:
        owner = lax.div(lax.rem(d, total // 4), size) * 4 + lax.div(d, total // 4)
    else:
        owner = lax.div(d, size)
    rows = jnp.where(r == owner, g, 0.0)
    d = lax.broadcasted_iota(jnp.int32, (total, 128), 0)
    j = lax.broadcasted_iota(jnp.int32, (total, 128), 1)
    pick = jnp.where(j == first + lax.rem(d, size), 1.0, 0.0).astype(BF)
    high = rows.astype(BF)
    rest = rows - high.astype(F32)
    middle = rest.astype(BF)
    low = (rest - middle.astype(F32)).astype(BF)
    return dot(high, pick) + dot(middle, pick) + dot(low, pick)


def bwd_kernel(
    ct_in, w4_in, up_in, dn_in, gain_in, stream_in, mixed_in, keep_in, q_in, hid_in, ff_in,
    grad_hbm, gate_hbm, out_hbm, up_hbm, down_hbm, vec_hbm,
    w4, up, dn, gain, keep, pre, mixed, stream, ff, grad, acc, low, low_t, act_t, up_low, sg, c_out, c_in,
    ends, enter, gains, biases, g_w4, g_up, g_dn, g_vec,
    lw0, lw1, lw2, lw3, lw4, lu0, lu1, lu2, lu3, lu4, ld0, ld1, ld2, ld3, ld4, lv0, lv1, lv2, lv3, lv4,
    f_w4, f_up, f_dn, f_vec,
    rs_send, rs_recv, load_sem, save_sem, carry_send, carry_recv,
):
    z, x, y, c = place()
    mp = y * 2 + c
    rows_all = low.shape[0]
    chunks = rows_all // ROWS
    loads = {}
    n_load = 0
    saves = []

    def load(key, src, dst):
        nonlocal n_load
        cp = pltpu.make_async_copy(src, dst, load_sem.at[n_load])
        cp.start()
        loads[key] = cp
        n_load += 1

    def ready(key):
        loads.pop(key).wait()

    def save(src, dst):
        cp = pltpu.make_async_copy(src, dst, save_sem.at[len(saves)])
        cp.start()
        saves.append(cp)

    def load_feed(l):
        load("dn", dn_in.at[l], dn)
        load("up", up_in.at[l], up)

    def load_chunk(l, q):
        load(("ff", q), ff_in.at[l, q], ff.at[q % 2])

    def load_gates(l):
        load("w4", w4_in.at[l], w4)
        load("keep", keep_in.at[l], keep)
        load("q", q_in.at[l], pre.at[:, pl.ds(0, 2)])

    load("ct", ct_in, low)
    load("gain", gain_in, gain)
    load("mixed", mixed_in.at[1], mixed)
    load_feed(1)
    load_chunk(1, 0)
    load_chunk(1, 1)
    load_gates(1)
    load("stream", stream_in.at[1], stream)
    greet()

    def give(item, scatter):
        kind, l, part = item
        if kind == "gate":
            for h in range(2):
                f_w4[l, part, h] = scatter.total(item, h)
            save(f_w4.at[l, part], gate_hbm.at[l, part] if part < 3 else out_hbm.at[l])
        elif kind == "up":
            for h in range(2):
                f_up[l, part, h] = scatter.total(item, h)
                save(f_up.at[l, part, h], up_hbm.at[l, :, pl.ds((part * 2 + h) * 512, 512)])
        elif kind == "down":
            for h in range(2):
                f_dn[l, part, h] = scatter.total(item, h)
            save(f_dn.at[l, part], down_hbm.at[l, part])
        else:
            for h in range(2):
                f_vec[h] = scatter.total(item, h)
            save(f_vec, vec_hbm)

    landing = (
        (lw0, lw1, lw2, lw3, lw4), (lu0, lu1, lu2, lu3, lu4), (ld0, ld1, ld2, ld3, ld4), (lv0, lv1, lv2, lv3, lv4),
    )
    scatter = Scatter((g_w4, g_up, g_dn, g_vec), landing, SCATTER_PLAN, rs_send, rs_recv, give)
    go_on = scatter.go_on

    def push(*item):
        scatter.items.append(item)

    def each(fn):
        @pl.loop(0, chunks)
        def _(i):
            fn(i, pl.ds(pl.multiple_of(i * ROWS, ROWS), ROWS))

    def rms_t(src, dst_t, g):
        def part(i, r):
            v = src[r, :]
            scale = lax.rsqrt(jnp.mean(v * v, axis=-1, keepdims=True) + eps)
            dst_t[:, r] = (v * scale * g).astype(BF).T

        each(part)

    def feed(l, q):
        slot = q % 2
        w_down = dn[q].reshape(512, 512)
        w_up = up[q // 2, q % 2].reshape(512, 512)

        def part(i, r):
            act_grad = dot_nt(low[r, :], w_down)
            slope = jnp.concatenate([ff[slot, 0, r, :], ff[slot, 1, r, :]], axis=1).astype(F32)
            u = (act_grad * slope).astype(BF)
            up_low[r, :] = u
            back = dot_nt(u, w_up)
            acc[r, :] = back if q == 0 else acc[r, :] + back

        each(part)
        go_on()
        for half in range(2):
            g = dot(act_t[half * 256 : half * 256 + 256, :], up_low[...]).astype(BF)
            g_up[q // 2, q % 2, half * 2 : half * 2 + 2] = g.reshape(2, 2, 2, 2, 16, 512)
        for half in range(2):
            g = dot_tn(ff[slot, 2 + half], low[...]).astype(BF)
            g_dn[q, half] = g.reshape(2, 2, 2, 2, 16, 512)

    def rms_back(l, which, src, values_t):
        g = gain[l, which : which + 1, :]
        gains[l, which : which + 1, :] = jnp.zeros((1, 512), F32)

        def part(i, r):
            v = src[r, :]
            scale = lax.rsqrt(jnp.mean(v * v, axis=-1, keepdims=True) + eps)
            u = v * scale
            d = acc[r, :]
            gains[l, which : which + 1, :] += jnp.sum(d * u, axis=0, keepdims=True)
            dg = d * g
            new = grad[r, :] + scale * (dg - u * jnp.mean(dg * u, axis=-1, keepdims=True))
            grad[r, :] = new
            new = new.astype(BF)
            low[r, :] = new
            if values_t is not None:
                values_t[:, r] = new.T

        each(part)

    def out_back(p):
        g = dot(low_t[...], ff[0, p]).astype(BF)
        g_w4[p // 2, p % 2, 3] = g.reshape(4, 2, 2, 32, 256)

    def states_back(p):
        w = w4[p // 2, p % 2, 3].reshape(512, 256)

        def part(i, r):
            v = dot(low[r, :], w)
            share = keep[p, r, :]
            decay = 1.0 - share
            t = slice(ROWS - 8, ROWS)
            adjoint = v[t]
            parts = [adjoint]
            a = decay[t]
            passed = a * adjoint
            for j in range(STEPS - 2, -1, -1):
                t = slice(j * 8, j * 8 + 8)
                adjoint = v[t] + passed
                passed = decay[t] * adjoint
                a = a * decay[t]
                parts.append(adjoint)
            whole = jnp.concatenate(parts[::-1], axis=0)
            for n in range(2):
                sg[p * 2 + n, r, :] = whole[:, n * 128 : n * 128 + 128]
            columns = slice(p * 256, p * 256 + 256)
            ends[0, i, :, columns] = a
            ends[1, i, :, columns] = passed

        each(part)

    row = lax.broadcasted_iota(jnp.int32, (8, 1024), 0)
    first_chunk = first_of(mp, rows_all)

    def carries(entering):
        for i in range(chunks - 1, -1, -1):
            c0 = jnp.where(first_chunk == i + 1, 0.0, entering)
            a, v = combine(ends[0, i], ends[1, i], row, -1)
            enter[i] = jnp.where(row == 7, c0, pltpu.roll(a, 7, 0) * c0 + pltpu.roll(v, 7, 0))
            entering = jnp.broadcast_to(a[0:1] * c0[0:1] + v[0:1], (8, 1024))
        return entering

    def carry_copy(l, there):
        return pltpu.make_async_remote_copy(
            src_ref=c_out.at[l],
            dst_ref=c_in.at[l],
            send_sem=carry_send.at[l],
            recv_sem=carry_recv.at[l],
            device_id=device(z, x, lax.div(there, 2), lax.rem(there, 2)),
            device_id_type=MESH,
        )

    def carry_out(l):
        c_out[l] = carries(jnp.zeros((8, 1024), F32))

        @pl.when(mp > 0)
        def _():
            carry_copy(l, jnp.maximum(mp - 1, 0)).start()

    def carry_into(l):
        @pl.when(mp < 3)
        def _():
            carry_copy(l, jnp.minimum(mp + 1, 3)).wait_recv()
            carries(c_in[l])

        @pl.when(mp > 0)
        def _():
            carry_copy(l, jnp.maximum(mp - 1, 0)).wait_send()

    def gates_back(p):
        w = [w4[p // 2, p % 2, k].reshape(512, 256) for k in range(3)]

        def part(i, r):
            share = keep[p, r, :]
            local = jnp.concatenate([sg[p * 2, r, :], sg[p * 2 + 1, r, :]], axis=1)
            weight = enter[i, :, p * 256 : p * 256 + 256]
            parts = []
            for j in range(STEPS - 1, -1, -1):
                t = slice(j * 8, j * 8 + 8)
                parts.append(local[t] + weight)
                if j:
                    weight = weight - share[t] * weight
            adjoint = jnp.concatenate(parts[::-1], axis=0)
            back = None
            for k in range(3):
                v = share if k == 2 else pre[p, k, r, :].astype(F32)
                v = (adjoint * v).astype(BF)
                pre[p, k, r, :] = v
                d = dot_nt(v, w[k])
                back = d if back is None else back + d
            acc[r, :] = back if p == 0 else acc[r, :] + back

        each(part)

    def gate_grads(l, k):
        ones = jnp.ones((8, rows_all), BF)
        for p in range(4):
            values = pre[p, k]
            g_w4[p // 2, p % 2, k] = dot(act_t[...], values).astype(BF).reshape(4, 2, 2, 32, 256)
            biases[l, k : k + 1, p * 256 : p * 256 + 256] = dot(ones, values)[0:1, :]

    ready("ct")

    def widen(i, r):
        v = into_steps(low[r, :].astype(F32), sg, i)
        grad[r, :] = v
        low[r, :] = v.astype(BF)

    each(widen)
    ready("gain")
    for l in (1, 0):
        ready("mixed")
        rms_t(mixed, act_t, gain[l, 1:2, :])
        go_on()
        if l == 0:
            go_on()
            scatter.settle(range(4))
        ready("dn")
        ready("up")
        for q in range(4):
            ready(("ff", q))
            feed(l, q)
            if q < 2:
                load_chunk(l, q + 2)
            elif q == 2:
                load("hid", hid_in.at[l], ff.at[0])
            if q % 2 == 1:
                push("up", l, q // 2)
            go_on()
        push("down", l, 0)
        push("down", l, 1)
        go_on()
        rms_back(l, 1, mixed, low_t)
        go_on()
        if l == 1:
            load_feed(0)
            load("mixed", mixed_in.at[0], mixed)
        else:
            go_on()
            scatter.settle(range(4, 8))
        ready("w4")
        ready("hid")
        for p in range(4):
            out_back(p)
        push("gate", l, 3)
        go_on()
        if l == 1:
            load_chunk(0, 0)
        ready("keep")
        for p in range(4):
            states_back(p)
            go_on()
        carry_out(l)
        ready("stream")
        rms_t(stream, act_t, gain[l, 0:1, :])
        go_on()
        ready("q")
        carry_into(l)
        for p in range(4):
            gates_back(p)
            go_on()
        for k in range(3):
            gate_grads(l, k)
            push("gate", l, k)
            go_on()
        if l == 1:
            load_chunk(0, 1)
            load_gates(0)
        rms_back(l, 0, stream, None)
        if l == 1:
            load("stream", stream_in.at[0], stream)
        go_on()
        rows = spread_back(gains[l, 0:1, :], 0, 16, 512, False) + spread_back(gains[l, 1:2, :], 16, 16, 512, False)
        for k in range(3):
            rows = rows + spread_back(biases[l, k : k + 1, :], 32 + 32 * k, 32, 1024, True)
        g_vec[:, :, :, :, l] = rows.reshape(4, 2, 2, 2, 8, 128)
    push("vec", 0, 0)
    go_on()

    def finish(i, r):
        mixed[r, :] = unturn(grad[r, :], sg, i)

    each(finish)
    save(mixed, grad_hbm)
    go_on()
    scatter.settle(range(8, 17))
    for cp in saves:
        cp.wait()


def backward(cotangent, kept):
    w4_all, up_all, dn_all, gain, stream, mixed, keep, q, hid, ff = kept
    rows = cotangent.shape[0]
    any_space = pl.BlockSpec(memory_space=pl.ANY)
    s = jax.ShapeDtypeStruct
    dma = pltpu.SemaphoreType.DMA
    v = pltpu.VMEM
    args = (cotangent, w4_all, up_all, dn_all, gain, stream, mixed, keep, q, hid, ff)
    grad, gates, out, up, down, vec = pl.pallas_call(
        bwd_kernel,
        name="backward",
        out_shape=(
            s((rows, 512), F32), s((2, 3, 2, 32, 256), F32), s((2, 2, 32, 256), F32), s((2, 16, 2048), F32),
            s((2, 2, 2, 16, 512), F32), s((2, 8, 128), F32),
        ),
        in_specs=[any_space] * len(args),
        out_specs=(any_space,) * 6,
        scratch_shapes=[
            v((2, 2, 4, 4, 2, 2, 32, 256), BF), v((2, 2, 4, 2, 2, 2, 16, 512), BF), v((4, 2, 2, 2, 2, 2, 16, 512), BF),
            v((2, 8, 512), F32), v((4, rows, 256), F32), v((4, 3, rows, 256), BF), v((rows, 512), F32), v((rows, 512), F32),
            v((2, 4, rows, 256), BF), v((rows, 512), F32), v((rows, 512), F32), v((rows, 512), BF), v((512, rows), BF),
            v((512, rows), BF), v((rows, 512), BF), v((8, rows, 128), F32), v((2, 8, 1024), F32), v((2, 8, 1024), F32),
            v((2, 3, 8, 1024), F32), v((3, 8, 1024), F32), v((2, 8, 512), F32), v((2, 8, 1024), F32),
            v((2, 2, 4, 4, 2, 2, 32, 256), BF), v((2, 2, 4, 2, 2, 2, 16, 512), BF), v((4, 2, 2, 2, 2, 2, 16, 512), BF),
            v((4, 2, 2, 2, 2, 8, 128), F32),
            v((2, 4, 2, 4, 2, 2, 32, 256), BF), v((2, 4, 4, 2, 32, 256), BF), v((2, 4, 2, 4, 32, 256), BF),
            v((2, 4, 2, 4, 32, 256), BF), v((2, 4, 3, 2, 32, 256), BF),
            v((2, 2, 2, 4, 2, 2, 16, 512), BF), v((2, 2, 4, 2, 16, 512), BF), v((2, 2, 4, 2, 16, 512), BF),
            v((2, 2, 2, 4, 16, 512), BF), v((2, 2, 3, 2, 16, 512), BF),
            v((2, 2, 4, 2, 2, 2, 16, 512), BF), v((2, 2, 4, 2, 16, 512), BF), v((2, 2, 4, 2, 16, 512), BF),
            v((2, 2, 2, 4, 16, 512), BF), v((2, 2, 3, 2, 16, 512), BF),
            v((4, 2, 2, 2, 8, 128), F32), v((4, 2, 8, 128), F32), v((4, 2, 8, 128), F32), v((2, 4, 8, 128), F32),
            v((3, 2, 8, 128), F32),
            v((2, 4, 2, 32, 256), F32), v((2, 2, 2, 16, 512), F32), v((2, 2, 2, 16, 512), F32), v((2, 8, 128), F32),
            dma((17, 8)), dma((17, 8)), dma((32,)), dma((24,)), dma((2,)), dma((2,)),
        ],
        compiler_params=pltpu.CompilerParams(
            collective_id=1, has_side_effects=True, vmem_limit_bytes=63 * 2**20
        ),
    )(*args)
    return grad, gates, out, up, down, vec


def settle_kernel(*refs):
    vec, biases, gain_one, gain_two = refs[6], *refs[13:]
    for src, dst in zip(refs[:6], refs[7:13]):
        dst[...] = src[...]
    for l in range(2):
        gain_one[l : l + 1, :] = vec[l, 0:1, 0:16]
        gain_two[l : l + 1, :] = vec[l, 0:1, 16:32]
        for k in range(3):
            biases[k, l : l + 1, :] = vec[l, 0:1, 32 + 32 * k : 64 + 32 * k]


def settle(result, grad, gates, out, up, down, vec):
    rows = result.shape[0]
    s = jax.ShapeDtypeStruct
    args = (
        result, grad, gates.reshape(12, 32, 256), out.reshape(4, 32, 256), up, down.reshape(8, 16, 512),
    )
    whole = lambda *shape: pl.BlockSpec(shape, lambda i: (0,) * len(shape))
    blocks = [
        pl.BlockSpec((rows // 4, 512), lambda i: (i, 0)),
        pl.BlockSpec((rows // 4, 512), lambda i: (i, 0)),
        pl.BlockSpec((3, 32, 256), lambda i: (i, 0, 0)),
        pl.BlockSpec((1, 32, 256), lambda i: (i, 0, 0)),
        pl.BlockSpec((2, 16, 512), lambda i: (0, 0, i)),
        pl.BlockSpec((2, 16, 512), lambda i: (i, 0, 0)),
    ]
    result, grad, gates, out, up, down, biases, gain_one, gain_two = pl.pallas_call(
        settle_kernel,
        name="settle",
        grid=(4,),
        out_shape=tuple(s(v.shape, v.dtype) for v in args) + (s((3, 2, 32), F32), s((2, 16), F32), s((2, 16), F32)),
        in_specs=blocks + [whole(2, 8, 128)],
        out_specs=tuple(blocks) + (whole(3, 2, 32), whole(2, 16), whole(2, 16)),
    )(*args, vec)
    return (
        result,
        grad,
        gates.reshape(2, 3, 64, 256),
        biases.transpose(1, 0, 2),
        out.reshape(2, 64, 256).transpose(0, 2, 1),
        gain_one,
        gain_two,
        up,
        down.reshape(2, 64, 512),
    )


def fits(inputs, gate_weight, gate_bias, out_weight, gain_one, gain_two, up_weight, down_weight):
    rows = inputs.shape[0]
    shapes = (gate_weight.shape, gate_bias.shape, out_weight.shape, gain_one.shape, up_weight.shape, down_weight.shape)
    planned = ((2, 3, 64, 256), (2, 3, 32), (2, 256, 64), (2, 16), (2, 16, 2048), (2, 64, 512))
    axes = (lax.axis_size("dp"), lax.axis_size("mp"))
    return axes == (8, 4) and shapes == planned and rows == 768 and 4 * rows == 3 * LENGTH


def general_body(
    inputs,
    gate_weight,
    gate_bias,
    out_weight,
    norm_gain_one,
    norm_gain_two,
    up_weight,
    down_weight,
    cotangent,
):
    own_rows = inputs.shape[0]
    group = own_rows * lax.axis_size("mp")
    starts = (jnp.arange(group, dtype=jnp.int32) % LENGTH == 0)[:, None]
    layer_count = gate_weight.shape[0]
    width = gate_weight.shape[3]
    stream = inputs.astype(jnp.float32)
    saved = []
    held = []
    for layer_no in range(layer_count):
        gates_full, bias_full, out_full = (
            lax.all_gather(gate_weight[layer_no], "dp", axis=1, tiled=True),
            lax.all_gather(gate_bias[layer_no], "dp", axis=1, tiled=True),
            lax.all_gather(out_weight[layer_no], "dp", axis=1, tiled=True),
        )
        up_full, down_full, gain_first, gain_second = (
            lax.all_gather(up_weight[layer_no], ("dp", "mp"), axis=0, tiled=True),
            lax.all_gather(down_weight[layer_no], ("dp", "mp"), axis=0, tiled=True),
            lax.all_gather(norm_gain_one[layer_no], ("dp", "mp"), axis=0, tiled=True),
            lax.all_gather(norm_gain_two[layer_no], ("dp", "mp"), axis=0, tiled=True),
        )
        gain_first = gain_first.astype(jnp.float32)
        gain_second = gain_second.astype(jnp.float32)
        normed = rms_scale(stream, gain_first).astype(jnp.bfloat16)
        normed_all = lax.all_gather(normed, "mp", axis=0, tiled=True)
        pre_acts = (
            jnp.einsum("td,kdf->ktf", normed_all, gates_full, preferred_element_type=jnp.float32)
            + bias_full.astype(jnp.float32)[:, None, :]
        )
        decay, drive = gate_terms(pre_acts, starts)
        products, states = lax.associative_scan(link, (decay, drive), axis=0)
        hidden = states.astype(jnp.bfloat16)
        mixed = stream + lax.psum_scatter(
            dot_plain(hidden, out_full).astype(jnp.bfloat16), "mp", scatter_dimension=0, tiled=True
        ).astype(jnp.float32)
        second = rms_scale(mixed, gain_second).astype(jnp.bfloat16)
        up_acts = dot_plain(second, up_full)
        activated = jax.nn.gelu(up_acts).astype(jnp.bfloat16)
        saved.append(
            {
                "stream": stream,
                "gain_first": gain_first,
                "gain_second": gain_second,
                "normed": normed_all,
                "pre": pre_acts,
                "decay": decay,
                "states": states,
                "hidden": hidden,
                "mixed": mixed,
                "second": second,
                "up_acts": up_acts,
                "activated": activated,
            }
        )
        held.append((gates_full, out_full, up_full, down_full))
        stream = mixed + dot_plain(activated, down_full)
    grad = cotangent.astype(jnp.float32)
    gate_parts = []
    mlp_parts = []
    for layer_no in reversed(range(layer_count)):
        kept = saved[layer_no]
        gates_full, out_full, up_full, down_full = held[layer_no]
        grad_low = grad.astype(jnp.bfloat16)
        act_grad = dot_last(grad_low, down_full)
        down_grad = dot_first(kept["activated"], grad_low)
        unused_gelu, gelu_back = jax.vjp(jax.nn.gelu, kept["up_acts"])
        up_low = gelu_back(act_grad)[0].astype(jnp.bfloat16)
        up_grad = dot_first(kept["second"], up_low)
        second_grad = dot_last(up_low, up_full)
        unused_norm, norm_back = jax.vjp(rms_scale, kept["mixed"], kept["gain_second"])
        mixed_part, gain_two_grad = norm_back(second_grad)
        mixed_grad = grad + mixed_part
        mixed_low = mixed_grad.astype(jnp.bfloat16)
        mixed_all = lax.all_gather(mixed_low, "mp", axis=0, tiled=True)
        state_grad = dot_last(mixed_all, out_full)
        out_grad = dot_first(kept["hidden"], mixed_all)
        decay = kept["decay"]
        shifted = jnp.concatenate([decay[1:], jnp.ones((1, width), jnp.float32)], axis=0)
        back_products, back_partial = lax.associative_scan(
            link, (shifted[::-1], state_grad[::-1]), axis=0
        )
        adjoint = back_partial[::-1]
        previous = jnp.concatenate(
            [jnp.zeros((1, width), jnp.float32), kept["states"][:-1]], axis=0
        )
        unused_gate, gate_back = jax.vjp(partial(gate_terms, starts=starts), kept["pre"])
        pre_low = gate_back((adjoint * previous, adjoint))[0].astype(jnp.bfloat16)
        bias_grad = jnp.sum(pre_low.astype(jnp.float32), axis=1)
        gate_grad = jnp.einsum(
            "td,ktf->kdf", kept["normed"], pre_low, preferred_element_type=jnp.float32
        )
        normed_part = jnp.einsum(
            "ktf,kdf->td", pre_low, gates_full, preferred_element_type=jnp.float32
        )
        normed_grad = lax.psum_scatter(
            normed_part.astype(jnp.bfloat16), "mp", scatter_dimension=0, tiled=True
        ).astype(jnp.float32)
        unused_first, first_back = jax.vjp(rms_scale, kept["stream"], kept["gain_first"])
        stream_part, gain_one_grad = first_back(normed_grad)
        grad = mixed_grad + stream_part
        gate_parts.append(
            (
                sum_at_owner(gate_grad.astype(jnp.bfloat16), "dp", 1),
                sum_at_owner(bias_grad.astype(jnp.bfloat16), "dp", 1),
                sum_at_owner(out_grad.astype(jnp.bfloat16), "dp", 1),
            )
        )
        mlp_parts.append(
            (
                lax.psum_scatter(up_grad, ("dp", "mp"), scatter_dimension=0, tiled=True),
                lax.psum_scatter(down_grad, ("dp", "mp"), scatter_dimension=0, tiled=True),
                lax.psum_scatter(gain_one_grad, ("dp", "mp"), scatter_dimension=0, tiled=True),
                lax.psum_scatter(gain_two_grad, ("dp", "mp"), scatter_dimension=0, tiled=True),
            )
        )
    gate_parts = gate_parts[::-1]
    mlp_parts = mlp_parts[::-1]
    gate_stack = tuple((jnp.stack([entry[member] for entry in gate_parts]) for member in range(3)))
    mlp_stack = tuple((jnp.stack([entry[member] for entry in mlp_parts]) for member in range(4)))
    return (
        stream.astype(jnp.bfloat16),
        grad,
        gate_stack[0],
        gate_stack[1],
        gate_stack[2],
        mlp_stack[2],
        mlp_stack[3],
        mlp_stack[0],
        mlp_stack[1],
    )


def body(inputs, gate_weight, gate_bias, out_weight, gain_one, gain_two, up_weight, down_weight, cotangent):
    shards = (gate_weight, gate_bias, out_weight, gain_one, gain_two, up_weight, down_weight)
    if not fits(inputs, *shards):
        return general_body(inputs, *shards, cotangent)
    out, *kept = forward(inputs, *shards)
    return settle(out, *backward(cotangent, kept))


def solution(mesh):
    placed = (
        P(("dp", "mp"), None),
        P(None, None, "dp", "mp"),
        P(None, None, ("mp", "dp")),
        P(None, "mp", "dp"),
        P(None, ("dp", "mp")),
        P(None, ("dp", "mp")),
        P(None, ("dp", "mp"), None),
        P(None, ("dp", "mp"), None),
        P(("dp", "mp"), None),
    )
    return jax.shard_map(
        body,
        mesh=mesh,
        in_specs=placed,
        out_specs=(
            P(("dp", "mp"), None),
            P(("dp", "mp"), None),
            P(None, None, "dp", "mp"),
            P(None, None, ("mp", "dp")),
            P(None, "mp", "dp"),
            P(None, ("dp", "mp")),
            P(None, ("dp", "mp")),
            P(None, ("dp", "mp"), None),
            P(None, ("dp", "mp"), None),
        ),
        check_vma=False,
    )
```

```python
from functools import partial

import jax
import jax.numpy as jnp
from jax import lax
from jax.experimental import pallas as pl
from jax.experimental.pallas import tpu as pltpu
from jax.sharding import PartitionSpec as P

LENGTH = 1024


eps = 1e-06


def cut_along(x, dim, size):
    shape = x.shape
    blocks = x.reshape(*shape[:dim], size, shape[dim] // size, *shape[dim + 1 :])
    return jnp.moveaxis(blocks, dim, 0)


def sum_at_owner(x, axis, dim):
    size = lax.axis_size(axis)
    blocks = lax.all_to_all(cut_along(x, dim, size), axis, 0, 0, tiled=True)
    return jnp.sum(blocks.astype(jnp.float32), axis=0)


def rms_scale(values, gain):
    return values * lax.rsqrt(jnp.mean(values * values, axis=-1, keepdims=True) + eps) * gain


def link(earlier, later):
    return (earlier[0] * later[0], later[0] * earlier[1] + later[1])


def gate_terms(pre_acts, starts):
    sig_forget = jax.nn.sigmoid(pre_acts[0])
    sig_input = jax.nn.sigmoid(pre_acts[1])
    total = sig_forget + sig_input
    decay = jnp.where(starts, 0.0, sig_forget / total)
    return (decay, sig_input / total * pre_acts[2])


def dot_plain(left, right):
    return jnp.dot(left, right, preferred_element_type=jnp.float32)


def dot_first(left, right):
    return lax.dot_general(
        left, right, (((0,), (0,)), ((), ())), preferred_element_type=jnp.float32
    )


def dot_last(left, right):
    return lax.dot_general(
        left, right, (((1,), (1,)), ((), ())), preferred_element_type=jnp.float32
    )


GATHER_PLAN = (
    (0, 5, 10, 15, 1, 20, 6, 25, 2, 11, 30, 7, 3, 16, 35, 12, 4),
    (),
    (),
    (),
    (21, 40, 8, 17, 26, 45, 9, 13, 31, 50, 22, 36, 55, 14, 18, 27, 41, 60, 32, 19),
    (),
    (46, 65, 23),
    (51, 70, 37),
    (56, 75, 28, 42, 24),
    (),
    (61, 80, 33),
    (66, 47, 29),
    (52,),
    (),
    (71, 34),
    (),
    (57, 76, 38),
    (),
    (),
    (81, 43, 62, 39, 67, 44),
    (),
    (48,),
    (53, 72, 49, 54, 58, 77, 82, 59),
    (),
    (),
    (63,),
    (68,),
    (73, 64),
    (),
    (69,),
    (78, 74),
    (),
    (),
    (),
    (83,),
    (),
    (79,),
    (84,),
    (),
)
SCATTER_PLAN = (
    (),
    (),
    (),
    (),
    (0,),
    (),
    (),
    (),
    (5,),
    (10, 15),
    (1,),
    (20,),
    (),
    (),
    (6,),
    (11,),
    (16,),
    (21, 2),
    (),
    (25, 7),
    (30,),
    (35,),
    (12,),
    (26, 17, 31),
    (36, 22),
    (3,),
    (8, 13, 27, 18, 4, 32, 9, 37, 14, 23, 28, 19),
    (),
    (),
    (33, 38),
    (40,),
    (24,),
    (),
    (),
    (45, 29),
    (50, 55),
    (41, 34),
    (39,),
    (60,),
    (46,),
    (51,),
    (56,),
    (42,),
    (61,),
    (),
    (47,),
    (65,),
    (70, 52),
    (75,),
    (57,),
    (66, 43, 71),
    (76, 62, 48),
    (80,),
    (53, 58, 44, 81, 67, 49, 72, 54, 77, 63, 82, 59, 68, 73, 78, 83, 64, 69, 74, 79, 84),
)


ALL = slice(None)
MESH = pl.DeviceIdType.MESH
BF = jnp.bfloat16
F32 = jnp.float32
SHIFT = 0.25
LOG_SHIFT = -1.3862943611198906
TOP = 87.0
GELU_A = 0.7978845608028654
GELU_B = 0.044715
ROWS = 256
STEPS = ROWS // 8


def first_of(mp, rows):
    return lax.div(jnp.minimum(lax.rem(mp * (LENGTH - rows), LENGTH), rows), ROWS)


def place():
    dp = lax.axis_index("dp")
    mp = lax.axis_index("mp")
    return (lax.div(dp, 2), lax.rem(dp, 2), lax.div(mp, 2), lax.rem(mp, 2))


def device(z, x, y, c):
    return (z * 2 + x, y * 2 + c)


def greet():
    z, x, y, c = place()
    partners = [device(lax.rem(z + k, 4), x, y, c) for k in (1, 2, 3)]
    partners += [device(z, 1 - x, y, c), device(z, x, 1 - y, c)]
    partners += [device(z, x, y, 1 - c), device(z, x, 1 - y, 1 - c)]
    barrier = pltpu.get_barrier_semaphore()
    for partner in partners:
        pl.semaphore_signal(barrier, inc=1, device_id=partner, device_id_type=MESH)
    pl.semaphore_wait(barrier, len(partners))


class Gather:
    def __init__(self, bufs, own, items, plan, send, recv):
        self.bufs = bufs
        self.own = own
        self.items = items
        self.send = send
        self.recv = recv
        self.at = place()
        self.sent = []
        self.plan = [list(row) for row in plan]

    def view(self, item, z, x, y, c, h):
        kind, l, part = item
        w4, up, dn, vec = self.bufs
        if kind == "vec":
            return vec.at[z, x, y, c, h]
        if kind == "gate":
            return w4.at[l, y, c, part, z, x, h]
        if kind == "up":
            return up.at[l, part, h, z, x, y, c]
        return dn.at[l, z, x, y, c, part, h]

    def go(self, n, slot, ref, target):
        cp = pltpu.make_async_remote_copy(
            src_ref=ref,
            dst_ref=ref,
            send_sem=self.send.at[n, slot],
            recv_sem=self.recv.at[n, slot],
            device_id=target,
            device_id_type=MESH,
        )
        cp.start()
        self.sent.append(cp)

    def landed(self, n, slot, ref, source):
        pltpu.make_async_remote_copy(
            src_ref=ref,
            dst_ref=ref,
            send_sem=self.send.at[n, slot],
            recv_sem=self.recv.at[n, slot],
            device_id=source,
            device_id_type=MESH,
        ).wait_recv()

    def stage(self, step, n, item):
        z, x, y, c = self.at
        v = lambda *where: self.view(item, *where)
        to_x = device(z, 1 - x, y, c)
        to_y = device(z, x, 1 - y, c)
        to_c = device(z, x, y, 1 - c)
        if step == 0:
            for cp in self.own.pop(item):
                cp.wait()
            for k in (1, 2, 3):
                self.go(n, k - 1, v(z, x, y, c, ALL), device(lax.rem(z + k, 4), x, y, c))
        elif step == 1:
            for k in (1, 2, 3):
                source = lax.rem(z + 4 - k, 4)
                self.landed(n, k - 1, v(source, x, y, c, ALL), device(source, x, y, c))
            self.go(n, 3, v(ALL, x, y, c, 0), to_x)
            self.go(n, 4, v(ALL, x, y, c, 1), to_y)
            self.go(n, 7, v(ALL, x, y, c, ALL), to_c)
        elif step == 2:
            self.landed(n, 3, v(ALL, 1 - x, y, c, 0), to_x)
            self.go(n, 5, v(ALL, ALL, y, c, 0), to_y)
            self.landed(n, 4, v(ALL, x, 1 - y, c, 1), to_y)
            self.go(n, 6, v(ALL, x, ALL, c, 1), to_x)
            self.go(n, 8, v(ALL, 1 - x, y, c, 0), to_c)
            self.go(n, 9, v(ALL, x, 1 - y, c, 1), to_c)
        elif step == 3:
            self.landed(n, 5, v(ALL, ALL, 1 - y, c, 0), to_y)
            self.go(n, 10, v(ALL, ALL, 1 - y, c, 0), to_c)
            self.landed(n, 6, v(ALL, 1 - x, ALL, c, 1), to_x)
            self.go(n, 11, v(ALL, 1 - x, ALL, c, 1), to_c)
        else:
            self.landed(n, 7, v(ALL, x, y, 1 - c, ALL), to_c)
            self.landed(n, 8, v(ALL, 1 - x, y, 1 - c, 0), to_c)
            self.landed(n, 9, v(ALL, x, 1 - y, 1 - c, 1), to_c)
            self.landed(n, 10, v(ALL, ALL, 1 - y, 1 - c, 0), to_c)
            self.landed(n, 11, v(ALL, 1 - x, ALL, 1 - c, 1), to_c)

    def go_on(self):
        for code in self.plan.pop(0):
            n, step = divmod(code, 5)
            self.stage(step, n, self.items[n])

    def finish(self):
        for cp in self.sent:
            cp.wait_send()


def dot(a, b):
    return jnp.dot(a, b, preferred_element_type=F32)


def dot_nt(a, b):
    return lax.dot_general(a, b, (((1,), (1,)), ((), ())), preferred_element_type=F32)


def dot_tn(a, b):
    return lax.dot_general(a, b, (((0,), (0,)), ((), ())), preferred_element_type=F32)


def spread(vec, l, first, size, total, per_mp):
    rows = vec[:, :, :, :, l].reshape(256, 128).astype(BF)
    j = lax.broadcasted_iota(jnp.int32, (128, total), 0)
    d = lax.broadcasted_iota(jnp.int32, (128, total), 1)
    pick = jnp.where(j == first + lax.rem(d, size), 1.0, 0.0).astype(BF)
    wide = dot(rows, pick)
    r = lax.div(lax.broadcasted_iota(jnp.int32, (256, total), 0), 8)
    d = lax.broadcasted_iota(jnp.int32, (256, total), 1)
    if per_mp:
        owner = lax.div(lax.rem(d, total // 4), size) * 4 + lax.div(d, total // 4)
    else:
        owner = lax.div(d, size)
    return jnp.sum(jnp.where(r == owner, wide, 0.0), axis=0, keepdims=True)


def combine(a, b, row, sign):
    for s in (1, 2, 4):
        keep = (row >= s) if sign > 0 else (row < 8 - s)
        by = s if sign > 0 else 8 - s
        am = jnp.where(keep, a, 0.0)
        b = b + am * pltpu.roll(b, by, 0)
        if s < 4:
            a = jnp.where(keep, a * pltpu.roll(a, by, 0), a)
        else:
            a = jnp.where(keep, a * pltpu.roll(a, by, 0), a)
    return a, b


def into_steps(v, turn, i):
    for n in range(4):
        turn[n, pl.ds(i * ROWS, ROWS), :] = v[:, n * 128 : n * 128 + 128]
    parts = []
    for n in range(4):
        rows = [turn[n, pl.ds(i * ROWS + j, 8, stride=STEPS), :] for j in range(STEPS)]
        parts.append(jnp.concatenate(rows, axis=0))
    return jnp.concatenate(parts, axis=1)


def unturn(v, turn, i):
    for n in range(4):
        for j in range(STEPS):
            turn[n, pl.ds(i * ROWS + j, 8, stride=STEPS), :] = v[j * 8 : j * 8 + 8, n * 128 : n * 128 + 128]
    return jnp.concatenate([turn[n, pl.ds(i * ROWS, ROWS), :] for n in range(4)], axis=1)


def fwd_kernel(
    x_in, gate_in, out_in, up_in, down_in, gain_one_in, gain_two_in, bias_in,
    out_hbm, w4_hbm, up_hbm, dn_hbm, gain_hbm, stream_hbm, mixed_hbm, keep_hbm, q_hbm, hid_hbm, ff_hbm, turned_hbm,
    w4, up, dn, vec, normed, stream, mixed, turned, turn, ends, enter, keep, states, c3, hid, ff, bias, gain, c_out, c_in,
    ag_send, ag_recv, own_sem, spill_sem, carry_send, carry_recv,
):
    z, x, y, c = place()
    mp = y * 2 + c
    rows_all = normed.shape[0]
    chunks = rows_all // ROWS
    fill = []

    def local(src, dst, sem):
        cp = pltpu.make_async_copy(src, dst, sem)
        cp.start()
        return cp

    own = {}
    n_own = 0

    def add_own(key, src, dst):
        nonlocal n_own
        own.setdefault(key, []).append(local(src, dst, own_sem.at[n_own]))
        n_own += 1

    x_copy = local(x_in, normed, own_sem.at[48])
    own[("vec", 0, 0)] = []
    vec[z, x, y, c] = jnp.zeros((2, 8, 128), F32)
    for l in range(2):
        ours = [gain_one_in[l : l + 1, :], gain_two_in[l : l + 1, :]] + [bias_in[k, l : l + 1, :] for k in range(3)]
        vec[z, x, y, c, l, 0:1, :] = jnp.concatenate([v.astype(F32) for v in ours], axis=1)
    for l in range(2):
        for k in range(3):
            add_own(("gate", l, k), gate_in.at[l, k], w4.at[l, y, c, k, z, x])
        add_own(("gate", l, 3), out_in.at[l], w4.at[l, y, c, 3, z, x])
        for pair in range(2):
            for h in range(2):
                columns = pl.ds((pair * 2 + h) * 512, 512)
                add_own(("up", l, pair), up_in.at[l, :, columns], up.at[l, pair, h, z, x, y, c])
            add_own(("down", l, pair), down_in.at[l, pair], dn.at[l, z, x, y, c, pair])
    greet()
    items = [("vec", 0, 0)]
    for l in range(2):
        items += [("gate", l, k) for k in range(4)]
        items += [(kind, l, pair) for kind in ("up", "down") for pair in range(2)]
    gather = Gather((w4, up, dn, vec), own, items, GATHER_PLAN, ag_send, ag_recv)
    go_on = gather.go_on

    n_spill = 0
    spills = {}

    def spill(key, src, dst):
        nonlocal n_spill
        spills[key] = local(src, dst, spill_sem.at[n_spill])
        n_spill += 1

    def settle(key):
        if key in spills:
            spills.pop(key).wait()


    def rms(src, dst, g):
        @pl.loop(0, chunks)
        def _(i):
            r = pl.ds(pl.multiple_of(i * ROWS, ROWS), ROWS)
            v = src[r, :]
            scale = lax.rsqrt(jnp.mean(v * v, axis=-1, keepdims=True) + eps)
            n = (v * scale * g).astype(BF)
            dst[r, :] = n
            turned[0, :, r] = n.T

    def gate_panel(l, p):
        w = [w4[l, p // 2, p % 2, k].reshape(512, 256) for k in range(3)]
        bs = [bias[l, k : k + 1, p * 256 : (p + 1) * 256] for k in range(3)]

        @pl.loop(0, chunks)
        def _(i):
            r = pl.ds(pl.multiple_of(i * ROWS, ROWS), ROWS)
            n = normed[r, :]
            f, inp, cand = [dot(n, w[k]) + bs[k] for k in range(3)]
            e_f = jnp.exp(jnp.minimum(-f, TOP) + LOG_SHIFT)
            e_i = jnp.exp(jnp.minimum(-inp, TOP) + LOG_SHIFT)
            a_f = e_f + SHIFT
            a_i = e_i + SHIFT
            total = a_f + a_i
            inv = pl.reciprocal(total, approx=True)
            inv = inv * (2.0 - total * inv)
            share = a_f * inv
            decay = a_i * inv
            drive = share * cand
            keep[p, r, :] = share
            c3[p, 0, r, :] = (decay * (e_f * inv)).astype(BF)
            c3[p, 1, r, :] = (share * (e_i * inv)).astype(BF)
            c3[p, 2, r, :] = cand.astype(BF)
            s = drive[0:8]
            a = decay[0:8]
            local_states = [s]
            for j in range(1, STEPS):
                t = slice(j * 8, j * 8 + 8)
                s = decay[t] * s + drive[t]
                a = a * decay[t]
                local_states.append(s)
            states[p, r, :] = jnp.concatenate(local_states, axis=0)
            columns = slice(p * 256, p * 256 + 256)
            ends[0, i, :, columns] = a
            ends[1, i, :, columns] = s

    row = lax.broadcasted_iota(jnp.int32, (8, 1024), 0)
    first_chunk = first_of(mp, rows_all)

    def carries(entering):
        for i in range(chunks):
            c0 = jnp.where(first_chunk == i, 0.0, entering)
            a, s = combine(ends[0, i], ends[1, i], row, 1)
            enter[i] = jnp.where(row == 0, c0, pltpu.roll(a, 1, 0) * c0 + pltpu.roll(s, 1, 0))
            entering = jnp.broadcast_to(a[7:8] * c0[7:8] + s[7:8], (8, 1024))
        return entering

    def carry_copy(l, there):
        return pltpu.make_async_remote_copy(
            src_ref=c_out.at[l],
            dst_ref=c_in.at[l],
            send_sem=carry_send.at[l],
            recv_sem=carry_recv.at[l],
            device_id=device(z, x, lax.div(there, 2), lax.rem(there, 2)),
            device_id_type=MESH,
        )

    def carry_out(l):
        c_out[l] = carries(jnp.zeros((8, 1024), F32))

        @pl.when(mp < 3)
        def _():
            carry_copy(l, jnp.minimum(mp + 1, 3)).start()

    def carry_into(l):
        @pl.when(mp > 0)
        def _():
            carry_copy(l, jnp.maximum(mp - 1, 0)).wait_recv()
            carries(c_in[l])

        @pl.when(mp < 3)
        def _():
            carry_copy(l, jnp.minimum(mp + 1, 3)).wait_send()

    def project(l):
        g = gain[l, 1:2, :]
        w = [w4[l, p // 2, p % 2, 3].reshape(512, 256) for p in range(4)]

        @pl.loop(0, chunks)
        def _(i):
            r = pl.ds(pl.multiple_of(i * ROWS, ROWS), ROWS)
            v = stream[r, :]
            for p in range(4):
                share = keep[p, r, :]
                s_local = states[p, r, :]
                cand = c3[p, 2, r, :].astype(F32)
                enters = enter[i, :, p * 256 : p * 256 + 256]
                before = enters
                weight = enters
                now, gap = [], []
                for j in range(STEPS):
                    t = slice(j * 8, j * 8 + 8)
                    weight = weight - share[t] * weight
                    s = s_local[t] + weight
                    gap.append(before - cand[t])
                    now.append(s)
                    before = s
                gap = jnp.concatenate(gap, axis=0)
                h = jnp.concatenate(now, axis=0).astype(BF)
                hid[p, r, :] = h
                c3[p, 0, r, :] = (gap * c3[p, 0, r, :].astype(F32)).astype(BF)
                c3[p, 1, r, :] = (-gap * c3[p, 1, r, :].astype(F32)).astype(BF)
                v = v + dot_nt(h, w[p])
            mixed[r, :] = v
            scale = lax.rsqrt(jnp.mean(v * v, axis=-1, keepdims=True) + eps)
            n = (v * scale * g).astype(BF)
            normed[r, :] = n
            turned[1, :, r] = n.T

    def feed_up(l, q):
        w_up = up[l, q // 2, q % 2].reshape(512, 512)

        @pl.loop(0, chunks)
        def _(i):
            r = pl.ds(pl.multiple_of(i * ROWS, ROWS), ROWS)
            u = dot(normed[r, :], w_up)
            sq = u * u
            t = jnp.tanh(u * (GELU_A + (GELU_A * GELU_B) * sq))
            gate = 0.5 + 0.5 * t
            act = (u * gate).astype(BF)
            slope = gate + (0.5 * u) * (1.0 - t * t) * (GELU_A + (3.0 * GELU_A * GELU_B) * sq)
            for half in range(2):
                side = slice(half * 256, half * 256 + 256)
                ff[q, half, r, :] = slope[:, side].astype(BF)
                ff[q, 2 + half, r, :] = act[:, side]

    def feed_down(l):
        w_down = dn[l].reshape(2048, 512)

        @pl.loop(0, chunks)
        def _(i):
            r = pl.ds(pl.multiple_of(i * ROWS, ROWS), ROWS)
            acts = [ff[q, 2 + half, r, :] for q in range(4) for half in range(2)]
            v = mixed[r, :] + dot(jnp.concatenate(acts, axis=1), w_down)
            if l == 0:
                stream[r, :] = v
            else:
                normed[r, :] = unturn(v, turn, i).astype(BF)

    go_on()
    for l in range(2):
        gain[l, 0:1, :] = spread(vec, l, 0, 16, 512, False)
        gain[l, 1:2, :] = spread(vec, l, 16, 16, 512, False)
        for k in range(3):
            bias[l, k : k + 1, :] = spread(vec, l, 32 + 32 * k, 32, 1024, True)
        go_on()
    x_copy.wait()

    @pl.loop(0, chunks)
    def _(i):
        r = pl.ds(pl.multiple_of(i * ROWS, ROWS), ROWS)
        stream[r, :] = into_steps(normed[r, :].astype(F32), turn, i)

    spill("gain", gain, gain_hbm)
    for l in range(2):
        settle(("first", 0))
        rms(stream, normed, gain[l, 0:1, :])
        spill(("first", l), turned.at[0], turned_hbm.at[l, 0])
        settle(("keep", 0))
        settle(("q", 0))
        spill(("stream", l), stream, stream_hbm.at[l])
        go_on()
        go_on()
        for p in range(4):
            gate_panel(l, p)
            go_on()
        spill(("keep", l), keep, keep_hbm.at[l])
        carry_out(l)
        settle(("hid", 0))
        settle(("mixed", 0))
        go_on()
        carry_into(l)
        settle(("second", 0))
        project(l)
        spill(("second", l), turned.at[1], turned_hbm.at[l, 1])
        spill(("q", l), c3.at[:, pl.ds(0, 2)], q_hbm.at[l])
        spill(("hid", l), hid, hid_hbm.at[l])
        spill(("w4", l), w4.at[l], w4_hbm.at[l])
        spill(("mixed", l), mixed, mixed_hbm.at[l])
        go_on()
        for q in range(4):
            settle(("ff", 0, q))
            go_on()
            feed_up(l, q)
            spill(("ff", l, q), ff.at[q], ff_hbm.at[l, q])
            go_on()
        spill(("up", l), up.at[l], up_hbm.at[l])
        settle(("stream", l))
        go_on()
        feed_down(l)
        spill(("dn", l), dn.at[l], dn_hbm.at[l])
        go_on()
    spill("result", normed, out_hbm)
    for key in list(spills):
        settle(key)
    gather.finish()


def forward(x, gate_weight, gate_bias, out_weight, gain_one, gain_two, up_weight, down_weight):
    rows = x.shape[0]
    any_space = pl.BlockSpec(memory_space=pl.ANY)
    args = (
        x,
        gate_weight.reshape(2, 3, 2, 32, 256),
        out_weight.transpose(0, 2, 1).reshape(2, 2, 32, 256),
        up_weight,
        down_weight.reshape(2, 2, 2, 16, 512),
        gain_one,
        gain_two,
        gate_bias.transpose(1, 0, 2),
    )
    s = jax.ShapeDtypeStruct
    w4 = (2, 2, 2, 4, 4, 2, 2, 32, 256)
    up = (2, 2, 2, 4, 2, 2, 2, 16, 512)
    dn = (2, 4, 2, 2, 2, 2, 2, 16, 512)
    dma = pltpu.SemaphoreType.DMA
    return pl.pallas_call(
        fwd_kernel,
        name="forward",
        out_shape=(
            s((rows, 512), BF), s(w4, BF), s(up, BF), s(dn, BF), s((2, 8, 512), F32), s((2, rows, 512), F32),
            s((2, rows, 512), F32), s((2, 4, rows, 256), F32), s((2, 4, 2, rows, 256), BF),
            s((2, 4, rows, 256), BF), s((2, 4, 4, rows, 256), BF), s((2, 2, 512, rows), BF),
        ),
        in_specs=[any_space] * 5 + [pl.BlockSpec(memory_space=pltpu.VMEM)] * 3,
        out_specs=(any_space,) * 12,
        scratch_shapes=[
            pltpu.VMEM(w4, BF), pltpu.VMEM(up, BF), pltpu.VMEM(dn, BF), pltpu.VMEM((4, 2, 2, 2, 2, 8, 128), F32),
            pltpu.VMEM((rows, 512), BF), pltpu.VMEM((rows, 512), F32), pltpu.VMEM((rows, 512), F32), pltpu.VMEM((2, 512, rows), BF), pltpu.VMEM((4, rows, 128), F32),
            pltpu.VMEM((2, 3, 8, 1024), F32), pltpu.VMEM((3, 8, 1024), F32),
            pltpu.VMEM((4, rows, 256), F32), pltpu.VMEM((4, rows, 256), F32), pltpu.VMEM((4, 3, rows, 256), BF),
            pltpu.VMEM((4, rows, 256), BF), pltpu.VMEM((4, 4, rows, 256), BF),
            pltpu.VMEM((2, 8, 1024), F32), pltpu.VMEM((2, 8, 512), F32),
            pltpu.VMEM((2, 8, 1024), F32), pltpu.VMEM((2, 8, 1024), F32),
            dma((17, 12)), dma((17, 12)), dma((49,)), dma((32,)), dma((2,)), dma((2,)),
        ],
        compiler_params=pltpu.CompilerParams(
            collective_id=0, has_side_effects=True, vmem_limit_bytes=62 * 2**20
        ),
    )(*args)


class Scatter:
    def __init__(self, grads, landing, plan, send, recv, give):
        self.grads = grads
        self.landing = landing
        self.send = send
        self.recv = recv
        self.give = give
        self.at = place()
        self.sent = {}
        self.items = []
        self.plan = [list(row) for row in plan]

    def own(self, item, z, x, y, c, h):
        kind, l, part = item
        w4, up, dn, vec = self.grads
        if kind == "vec":
            return vec.at[z, x, y, c, h]
        if kind == "gate":
            return w4.at[y, c, part, z, x, h]
        if kind == "up":
            return up.at[part, h, z, x, y, c]
        return dn.at[z, x, y, c, part, h]

    def land(self, item, stage, *where):
        kind, l, part = item
        ref = self.landing[("gate", "up", "down", "vec").index(kind)][stage]
        where = where if kind == "vec" else (l, part, *where)
        return ref.at[where] if where else ref

    def copy(self, n, slot, src, dst, target):
        return pltpu.make_async_remote_copy(
            src_ref=src,
            dst_ref=dst,
            send_sem=self.send.at[n, slot],
            recv_sem=self.recv.at[n, slot],
            device_id=target,
            device_id_type=MESH,
        )

    def go(self, n, slot, src, dst, target):
        cp = self.copy(n, slot, src, dst, target)
        cp.start()
        self.sent.setdefault(n, []).append(cp)

    def landed(self, n, slot, dst, source):
        self.copy(n, slot, dst, dst, source).wait_recv()

    def add(self, item, stage):
        z, x, y, c = self.at
        kind = item[0]

        def plus(there, *where):
            there[...] = there[...] + self.land(item, stage, *where)[...]

        @pl.loop(0, 4)
        def _(n):
            if stage == 0:
                for i in range(2):
                    for j in range(2):
                        for h in range(2):
                            if kind == "gate":
                                plus(self.own(item, n, j, i, c, h), i, n, j, h)
                            elif kind == "up":
                                plus(self.own(item, n, i, j, c, h), h, n, i, j)
                            else:
                                plus(self.own(item, n, i, j, c, h), n, i, j, h)
            elif stage == 1:
                for i in range(2):
                    plus(self.own(item, n, i, y, c, 0), n, i)
            elif stage == 2:
                for i in range(2):
                    plus(self.own(item, n, x, i, c, 1), *((i, n) if kind == "gate" else (n, i)))
            else:
                for h in range(2):
                    plus(self.own(item, n, x, y, c, h), h, n)

    def total(self, item, h):
        z, x, y, c = self.at
        v = self.own(item, z, x, y, c, h)[...].astype(F32)
        for j in range(3):
            v = v + self.land(item, 4, j, h)[...].astype(F32)
        return v

    def stage(self, step, n, item):
        z, x, y, c = self.at
        v = lambda *where: self.own(item, *where)
        to_x = device(z, 1 - x, y, c)
        to_y = device(z, x, 1 - y, c)
        to_c = device(z, x, y, 1 - c)
        land = lambda *w: self.land(item, *w)
        if step == 0:
            self.go(n, 0, v(ALL, ALL, ALL, 1 - c, ALL), land(0), to_c)
        elif step == 1:
            self.landed(n, 0, land(0), to_c)
            self.add(item, 0)
            self.go(n, 1, v(ALL, ALL, 1 - y, c, 0), land(1), to_y)
            self.go(n, 2, v(ALL, 1 - x, ALL, c, 1), land(2), to_x)
        elif step == 2:
            self.landed(n, 1, land(1), to_y)
            self.add(item, 1)
            self.go(n, 3, v(ALL, 1 - x, y, c, 0), land(3, 0), to_x)
            self.landed(n, 2, land(2), to_x)
            self.add(item, 2)
            self.go(n, 4, v(ALL, x, 1 - y, c, 1), land(3, 1), to_y)
        elif step == 3:
            self.landed(n, 3, land(3, 0), to_x)
            self.landed(n, 4, land(3, 1), to_y)
            self.add(item, 3)
            for k in (1, 2, 3):
                there = lax.rem(z + k, 4)
                self.go(n, 4 + k, v(there, x, y, c, ALL), land(4, k - 1), device(there, x, y, c))
        else:
            for k in (1, 2, 3):
                source = lax.rem(z + 4 - k, 4)
                self.landed(n, 4 + k, land(4, k - 1), device(source, x, y, c))
            self.give(item, self)

    def go_on(self):
        for code in self.plan.pop(0):
            n, step = divmod(code, 5)
            self.stage(step, n, self.items[n])

    def settle(self, numbers):
        for n in numbers:
            for cp in self.sent.pop(n):
                cp.wait_send()


def spread_back(g, first, size, total, per_mp):
    r = lax.broadcasted_iota(jnp.int32, (32, total), 0)
    d = lax.broadcasted_iota(jnp.int32, (32, total), 1)
    if per_mp:
        owner = lax.div(lax.rem(d, total // 4), size) * 4 + lax.div(d, total // 4)
    else:
        owner = lax.div(d, size)
    rows = jnp.where(r == owner, g, 0.0)
    d = lax.broadcasted_iota(jnp.int32, (total, 128), 0)
    j = lax.broadcasted_iota(jnp.int32, (total, 128), 1)
    pick = jnp.where(j == first + lax.rem(d, size), 1.0, 0.0).astype(BF)
    high = rows.astype(BF)
    rest = rows - high.astype(F32)
    middle = rest.astype(BF)
    low = (rest - middle.astype(F32)).astype(BF)
    return dot(high, pick) + dot(middle, pick) + dot(low, pick)


def bwd_kernel(
    ct_in, w4_in, up_in, dn_in, gain_in, stream_in, mixed_in, keep_in, q_in, hid_in, ff_in, turned_in,
    grad_hbm, gate_hbm, out_hbm, up_hbm, down_hbm, vec_hbm,
    w4, up, dn, gain, keep, pre, mixed, stream, ff, grad, acc, low, low_t, act_t, up_low, sg, c_out, c_in,
    ends, enter, gains, biases, g_w4, g_up, g_dn, g_vec,
    lw0, lw1, lw2, lw3, lw4, lu0, lu1, lu2, lu3, lu4, ld0, ld1, ld2, ld3, ld4, lv0, lv1, lv2, lv3, lv4,
    f_w4, f_up, f_dn, f_vec,
    rs_send, rs_recv, load_sem, save_sem, carry_send, carry_recv,
):
    z, x, y, c = place()
    mp = y * 2 + c
    rows_all = low.shape[0]
    chunks = rows_all // ROWS
    loads = {}
    n_load = 0
    saves = []

    def load(key, src, dst):
        nonlocal n_load
        cp = pltpu.make_async_copy(src, dst, load_sem.at[n_load])
        cp.start()
        loads[key] = cp
        n_load += 1

    def ready(key):
        loads.pop(key).wait()

    def save(src, dst):
        cp = pltpu.make_async_copy(src, dst, save_sem.at[len(saves)])
        cp.start()
        saves.append(cp)

    def load_feed(l):
        load("dn", dn_in.at[l], dn)
        load("up", up_in.at[l], up)

    def load_chunk(l, q):
        load(("ff", q), ff_in.at[l, q], ff.at[q % 2])

    def load_gates(l):
        load("w4", w4_in.at[l], w4)
        load("keep", keep_in.at[l], keep)
        load("q", q_in.at[l], pre.at[:, pl.ds(0, 2)])

    load("ct", ct_in, low)
    load("gain", gain_in, gain)
    load_feed(1)
    load_chunk(1, 0)
    load("act_t", turned_in.at[1, 1], act_t)
    load("mixed", mixed_in.at[1], mixed)
    load_chunk(1, 1)
    load_gates(1)
    load("stream", stream_in.at[1], stream)
    greet()

    def give(item, scatter):
        kind, l, part = item
        if kind == "gate":
            for h in range(2):
                f_w4[l, part, h] = scatter.total(item, h)
            save(f_w4.at[l, part], gate_hbm.at[l, part] if part < 3 else out_hbm.at[l])
        elif kind == "up":
            for h in range(2):
                f_up[l, part, h] = scatter.total(item, h)
                save(f_up.at[l, part, h], up_hbm.at[l, :, pl.ds((part * 2 + h) * 512, 512)])
        elif kind == "down":
            for h in range(2):
                f_dn[l, part, h] = scatter.total(item, h)
            save(f_dn.at[l, part], down_hbm.at[l, part])
        else:
            for h in range(2):
                f_vec[h] = scatter.total(item, h)
            save(f_vec, vec_hbm)

    landing = (
        (lw0, lw1, lw2, lw3, lw4), (lu0, lu1, lu2, lu3, lu4), (ld0, ld1, ld2, ld3, ld4), (lv0, lv1, lv2, lv3, lv4),
    )
    scatter = Scatter((g_w4, g_up, g_dn, g_vec), landing, SCATTER_PLAN, rs_send, rs_recv, give)
    go_on = scatter.go_on

    def push(*item):
        scatter.items.append(item)

    def each(fn):
        @pl.loop(0, chunks)
        def _(i):
            fn(i, pl.ds(pl.multiple_of(i * ROWS, ROWS), ROWS))

    def feed(l, q):
        slot = q % 2
        w_down = dn[q].reshape(512, 512)
        w_up = up[q // 2, q % 2].reshape(512, 512)

        def part(i, r):
            act_grad = dot_nt(low[r, :], w_down)
            slope = jnp.concatenate([ff[slot, 0, r, :], ff[slot, 1, r, :]], axis=1).astype(F32)
            u = (act_grad * slope).astype(BF)
            up_low[r, :] = u
            back = dot_nt(u, w_up)
            acc[r, :] = back if q == 0 else acc[r, :] + back

        each(part)
        go_on()
        for half in range(2):
            g = dot(act_t[half * 256 : half * 256 + 256, :], up_low[...]).astype(BF)
            g_up[q // 2, q % 2, half * 2 : half * 2 + 2] = g.reshape(2, 2, 2, 2, 16, 512)
        for half in range(2):
            g = dot_tn(ff[slot, 2 + half], low[...]).astype(BF)
            g_dn[q, half] = g.reshape(2, 2, 2, 2, 16, 512)

    def rms_back(l, which, src, values_t):
        g = gain[l, which : which + 1, :]
        gains[l, which : which + 1, :] = jnp.zeros((1, 512), F32)

        def part(i, r):
            v = src[r, :]
            scale = lax.rsqrt(jnp.mean(v * v, axis=-1, keepdims=True) + eps)
            u = v * scale
            d = acc[r, :]
            gains[l, which : which + 1, :] += jnp.sum(d * u, axis=0, keepdims=True)
            dg = d * g
            new = grad[r, :] + scale * (dg - u * jnp.mean(dg * u, axis=-1, keepdims=True))
            grad[r, :] = new
            new = new.astype(BF)
            low[r, :] = new
            if values_t is not None:
                values_t[:, r] = new.T

        each(part)

    def out_back(p):
        g = dot(low_t[...], ff[0, p]).astype(BF)
        g_w4[p // 2, p % 2, 3] = g.reshape(4, 2, 2, 32, 256)

    def states_back(p):
        w = w4[p // 2, p % 2, 3].reshape(512, 256)

        def part(i, r):
            v = dot(low[r, :], w)
            share = keep[p, r, :]
            decay = 1.0 - share
            t = slice(ROWS - 8, ROWS)
            adjoint = v[t]
            parts = [adjoint]
            a = decay[t]
            passed = a * adjoint
            for j in range(STEPS - 2, -1, -1):
                t = slice(j * 8, j * 8 + 8)
                adjoint = v[t] + passed
                passed = decay[t] * adjoint
                a = a * decay[t]
                parts.append(adjoint)
            whole = jnp.concatenate(parts[::-1], axis=0)
            for n in range(2):
                sg[p * 2 + n, r, :] = whole[:, n * 128 : n * 128 + 128]
            columns = slice(p * 256, p * 256 + 256)
            ends[0, i, :, columns] = a
            ends[1, i, :, columns] = passed

        each(part)

    row = lax.broadcasted_iota(jnp.int32, (8, 1024), 0)
    first_chunk = first_of(mp, rows_all)

    def carries(entering):
        for i in range(chunks - 1, -1, -1):
            c0 = jnp.where(first_chunk == i + 1, 0.0, entering)
            a, v = combine(ends[0, i], ends[1, i], row, -1)
            enter[i] = jnp.where(row == 7, c0, pltpu.roll(a, 7, 0) * c0 + pltpu.roll(v, 7, 0))
            entering = jnp.broadcast_to(a[0:1] * c0[0:1] + v[0:1], (8, 1024))
        return entering

    def carry_copy(l, there):
        return pltpu.make_async_remote_copy(
            src_ref=c_out.at[l],
            dst_ref=c_in.at[l],
            send_sem=carry_send.at[l],
            recv_sem=carry_recv.at[l],
            device_id=device(z, x, lax.div(there, 2), lax.rem(there, 2)),
            device_id_type=MESH,
        )

    def carry_out(l):
        c_out[l] = carries(jnp.zeros((8, 1024), F32))

        @pl.when(mp > 0)
        def _():
            carry_copy(l, jnp.maximum(mp - 1, 0)).start()

    def carry_into(l):
        @pl.when(mp < 3)
        def _():
            carry_copy(l, jnp.minimum(mp + 1, 3)).wait_recv()
            carries(c_in[l])

        @pl.when(mp > 0)
        def _():
            carry_copy(l, jnp.maximum(mp - 1, 0)).wait_send()

    def pre_back(p):
        def part(i, r):
            share = keep[p, r, :]
            local = jnp.concatenate([sg[p * 2, r, :], sg[p * 2 + 1, r, :]], axis=1)
            weight = enter[i, :, p * 256 : p * 256 + 256]
            parts = []
            for j in range(STEPS - 1, -1, -1):
                t = slice(j * 8, j * 8 + 8)
                parts.append(local[t] + weight)
                if j:
                    weight = weight - share[t] * weight
            adjoint = jnp.concatenate(parts[::-1], axis=0)
            for k in range(3):
                v = share if k == 2 else pre[p, k, r, :].astype(F32)
                pre[p, k, r, :] = (adjoint * v).astype(BF)

        each(part)

    def normed_back(first):
        w = {(p, k): w4[p // 2, p % 2, k].reshape(512, 256) for p in (first, first + 1) for k in range(3)}

        def part(i, r):
            back = 0.0 if first == 0 else acc[r, :]
            for p, k in w:
                back = back + dot_nt(pre[p, k, r, :], w[p, k])
            acc[r, :] = back

        each(part)

    def gate_grads(l, k):
        ones = jnp.ones((8, rows_all), BF)
        for p in range(4):
            values = pre[p, k]
            g_w4[p // 2, p % 2, k] = dot(act_t[...], values).astype(BF).reshape(4, 2, 2, 32, 256)
            biases[l, k : k + 1, p * 256 : p * 256 + 256] = dot(ones, values)[0:1, :]

    ready("ct")

    def widen(i, r):
        v = into_steps(low[r, :].astype(F32), sg, i)
        grad[r, :] = v
        low[r, :] = v.astype(BF)

    each(widen)
    ready("gain")
    for l in (1, 0):
        ready("act_t")
        go_on()
        if l == 0:
            go_on()
            scatter.settle(range(4))
        ready("dn")
        ready("up")
        for q in range(4):
            ready(("ff", q))
            feed(l, q)
            if q < 2:
                load_chunk(l, q + 2)
            elif q == 2:
                load("hid", hid_in.at[l], ff.at[0])
            if q % 2 == 1:
                push("up", l, q // 2)
            go_on()
        push("down", l, 0)
        push("down", l, 1)
        go_on()
        load("act_t", turned_in.at[l, 0], act_t)
        ready("mixed")
        rms_back(l, 1, mixed, low_t)
        go_on()
        if l == 1:
            load_feed(0)
            load("mixed", mixed_in.at[0], mixed)
        else:
            go_on()
            scatter.settle(range(4, 8))
        ready("w4")
        ready("hid")
        for p in range(4):
            out_back(p)
        push("gate", l, 3)
        go_on()
        if l == 1:
            load_chunk(0, 0)
        ready("keep")
        for p in range(4):
            states_back(p)
            go_on()
        carry_out(l)
        go_on()
        ready("q")
        carry_into(l)
        for p in range(4):
            pre_back(p)
            if p % 2 == 1:
                go_on()
        ready("act_t")
        for k in range(3):
            gate_grads(l, k)
            push("gate", l, k)
            go_on()
        if l == 1:
            load("act_t", turned_in.at[0, 1], act_t)
        for first in (0, 2):
            normed_back(first)
            go_on()
        ready("stream")
        if l == 1:
            load_chunk(0, 1)
            load_gates(0)
        rms_back(l, 0, stream, None)
        if l == 1:
            load("stream", stream_in.at[0], stream)
        go_on()
        rows = spread_back(gains[l, 0:1, :], 0, 16, 512, False) + spread_back(gains[l, 1:2, :], 16, 16, 512, False)
        for k in range(3):
            rows = rows + spread_back(biases[l, k : k + 1, :], 32 + 32 * k, 32, 1024, True)
        for n in range(32):
            g_vec[n // 8, n // 4 % 2, n // 2 % 2, n % 2, l] = jnp.broadcast_to(rows[n : n + 1, :], (8, 128))
    push("vec", 0, 0)
    go_on()

    def finish(i, r):
        mixed[r, :] = unturn(grad[r, :], sg, i)

    each(finish)
    save(mixed, grad_hbm)
    go_on()
    scatter.settle(range(8, 17))
    for cp in saves:
        cp.wait()


def backward(cotangent, kept):
    w4_all, up_all, dn_all, gain, stream, mixed, keep, q, hid, ff, turned = kept
    rows = cotangent.shape[0]
    any_space = pl.BlockSpec(memory_space=pl.ANY)
    s = jax.ShapeDtypeStruct
    dma = pltpu.SemaphoreType.DMA
    v = pltpu.VMEM
    args = (cotangent, w4_all, up_all, dn_all, gain, stream, mixed, keep, q, hid, ff, turned)
    grad, gates, out, up, down, vec = pl.pallas_call(
        bwd_kernel,
        name="backward",
        out_shape=(
            s((rows, 512), F32), s((2, 3, 2, 32, 256), F32), s((2, 2, 32, 256), F32), s((2, 16, 2048), F32),
            s((2, 2, 2, 16, 512), F32), s((2, 8, 128), F32),
        ),
        in_specs=[any_space] * len(args),
        out_specs=(any_space,) * 6,
        scratch_shapes=[
            v((2, 2, 4, 4, 2, 2, 32, 256), BF), v((2, 2, 4, 2, 2, 2, 16, 512), BF), v((4, 2, 2, 2, 2, 2, 16, 512), BF),
            v((2, 8, 512), F32), v((4, rows, 256), F32), v((4, 3, rows, 256), BF), v((rows, 512), F32), v((rows, 512), F32),
            v((2, 4, rows, 256), BF), v((rows, 512), F32), v((rows, 512), F32), v((rows, 512), BF), v((512, rows), BF),
            v((512, rows), BF), v((rows, 512), BF), v((8, rows, 128), F32), v((2, 8, 1024), F32), v((2, 8, 1024), F32),
            v((2, 3, 8, 1024), F32), v((3, 8, 1024), F32), v((2, 8, 512), F32), v((2, 8, 1024), F32),
            v((2, 2, 4, 4, 2, 2, 32, 256), BF), v((2, 2, 4, 2, 2, 2, 16, 512), BF), v((4, 2, 2, 2, 2, 2, 16, 512), BF),
            v((4, 2, 2, 2, 2, 8, 128), F32),
            v((2, 4, 2, 4, 2, 2, 32, 256), BF), v((2, 4, 4, 2, 32, 256), BF), v((2, 4, 2, 4, 32, 256), BF),
            v((2, 4, 2, 4, 32, 256), BF), v((2, 4, 3, 2, 32, 256), BF),
            v((2, 2, 2, 4, 2, 2, 16, 512), BF), v((2, 2, 4, 2, 16, 512), BF), v((2, 2, 4, 2, 16, 512), BF),
            v((2, 2, 2, 4, 16, 512), BF), v((2, 2, 3, 2, 16, 512), BF),
            v((2, 2, 4, 2, 2, 2, 16, 512), BF), v((2, 2, 4, 2, 16, 512), BF), v((2, 2, 4, 2, 16, 512), BF),
            v((2, 2, 2, 4, 16, 512), BF), v((2, 2, 3, 2, 16, 512), BF),
            v((4, 2, 2, 2, 8, 128), F32), v((4, 2, 8, 128), F32), v((4, 2, 8, 128), F32), v((2, 4, 8, 128), F32),
            v((3, 2, 8, 128), F32),
            v((2, 4, 2, 32, 256), F32), v((2, 2, 2, 16, 512), F32), v((2, 2, 2, 16, 512), F32), v((2, 8, 128), F32),
            dma((17, 8)), dma((17, 8)), dma((32,)), dma((24,)), dma((2,)), dma((2,)),
        ],
        compiler_params=pltpu.CompilerParams(
            collective_id=1, has_side_effects=True, vmem_limit_bytes=63 * 2**20
        ),
    )(*args)
    return grad, gates, out, up, down, vec


def settle_kernel(*refs):
    vec, biases, gain_one, gain_two = refs[6], *refs[13:]
    for src, dst in zip(refs[:6], refs[7:13]):
        dst[...] = src[...]
    for l in range(2):
        gain_one[l : l + 1, :] = vec[l, 0:1, 0:16]
        gain_two[l : l + 1, :] = vec[l, 0:1, 16:32]
        for k in range(3):
            biases[k, l : l + 1, :] = vec[l, 0:1, 32 + 32 * k : 64 + 32 * k]


def settle(result, grad, gates, out, up, down, vec):
    rows = result.shape[0]
    s = jax.ShapeDtypeStruct
    args = (
        result, grad, gates.reshape(12, 32, 256), out.reshape(4, 32, 256), up, down.reshape(8, 16, 512),
    )
    whole = lambda *shape: pl.BlockSpec(shape, lambda i: (0,) * len(shape))
    blocks = [
        pl.BlockSpec((rows // 4, 512), lambda i: (i, 0)),
        pl.BlockSpec((rows // 4, 512), lambda i: (i, 0)),
        pl.BlockSpec((3, 32, 256), lambda i: (i, 0, 0)),
        pl.BlockSpec((1, 32, 256), lambda i: (i, 0, 0)),
        pl.BlockSpec((2, 16, 512), lambda i: (0, 0, i)),
        pl.BlockSpec((2, 16, 512), lambda i: (i, 0, 0)),
    ]
    result, grad, gates, out, up, down, biases, gain_one, gain_two = pl.pallas_call(
        settle_kernel,
        name="settle",
        grid=(4,),
        out_shape=tuple(s(v.shape, v.dtype) for v in args) + (s((3, 2, 32), F32), s((2, 16), F32), s((2, 16), F32)),
        in_specs=blocks + [whole(2, 8, 128)],
        out_specs=tuple(blocks) + (whole(3, 2, 32), whole(2, 16), whole(2, 16)),
    )(*args, vec)
    return (
        result,
        grad,
        gates.reshape(2, 3, 64, 256),
        biases.transpose(1, 0, 2),
        out.reshape(2, 64, 256).transpose(0, 2, 1),
        gain_one,
        gain_two,
        up,
        down.reshape(2, 64, 512),
    )


def fits(inputs, gate_weight, gate_bias, out_weight, gain_one, gain_two, up_weight, down_weight):
    rows = inputs.shape[0]
    shapes = (gate_weight.shape, gate_bias.shape, out_weight.shape, gain_one.shape, up_weight.shape, down_weight.shape)
    planned = ((2, 3, 64, 256), (2, 3, 32), (2, 256, 64), (2, 16), (2, 16, 2048), (2, 64, 512))
    axes = (lax.axis_size("dp"), lax.axis_size("mp"))
    return axes == (8, 4) and shapes == planned and rows == 768 and 4 * rows == 3 * LENGTH


def general_body(
    inputs,
    gate_weight,
    gate_bias,
    out_weight,
    norm_gain_one,
    norm_gain_two,
    up_weight,
    down_weight,
    cotangent,
):
    own_rows = inputs.shape[0]
    group = own_rows * lax.axis_size("mp")
    starts = (jnp.arange(group, dtype=jnp.int32) % LENGTH == 0)[:, None]
    layer_count = gate_weight.shape[0]
    width = gate_weight.shape[3]
    stream = inputs.astype(jnp.float32)
    saved = []
    held = []
    for layer_no in range(layer_count):
        gates_full, bias_full, out_full = (
            lax.all_gather(gate_weight[layer_no], "dp", axis=1, tiled=True),
            lax.all_gather(gate_bias[layer_no], "dp", axis=1, tiled=True),
            lax.all_gather(out_weight[layer_no], "dp", axis=1, tiled=True),
        )
        up_full, down_full, gain_first, gain_second = (
            lax.all_gather(up_weight[layer_no], ("dp", "mp"), axis=0, tiled=True),
            lax.all_gather(down_weight[layer_no], ("dp", "mp"), axis=0, tiled=True),
            lax.all_gather(norm_gain_one[layer_no], ("dp", "mp"), axis=0, tiled=True),
            lax.all_gather(norm_gain_two[layer_no], ("dp", "mp"), axis=0, tiled=True),
        )
        gain_first = gain_first.astype(jnp.float32)
        gain_second = gain_second.astype(jnp.float32)
        normed = rms_scale(stream, gain_first).astype(jnp.bfloat16)
        normed_all = lax.all_gather(normed, "mp", axis=0, tiled=True)
        pre_acts = (
            jnp.einsum("td,kdf->ktf", normed_all, gates_full, preferred_element_type=jnp.float32)
            + bias_full.astype(jnp.float32)[:, None, :]
        )
        decay, drive = gate_terms(pre_acts, starts)
        products, states = lax.associative_scan(link, (decay, drive), axis=0)
        hidden = states.astype(jnp.bfloat16)
        mixed = stream + lax.psum_scatter(
            dot_plain(hidden, out_full).astype(jnp.bfloat16), "mp", scatter_dimension=0, tiled=True
        ).astype(jnp.float32)
        second = rms_scale(mixed, gain_second).astype(jnp.bfloat16)
        up_acts = dot_plain(second, up_full)
        activated = jax.nn.gelu(up_acts).astype(jnp.bfloat16)
        saved.append(
            {
                "stream": stream,
                "gain_first": gain_first,
                "gain_second": gain_second,
                "normed": normed_all,
                "pre": pre_acts,
                "decay": decay,
                "states": states,
                "hidden": hidden,
                "mixed": mixed,
                "second": second,
                "up_acts": up_acts,
                "activated": activated,
            }
        )
        held.append((gates_full, out_full, up_full, down_full))
        stream = mixed + dot_plain(activated, down_full)
    grad = cotangent.astype(jnp.float32)
    gate_parts = []
    mlp_parts = []
    for layer_no in reversed(range(layer_count)):
        kept = saved[layer_no]
        gates_full, out_full, up_full, down_full = held[layer_no]
        grad_low = grad.astype(jnp.bfloat16)
        act_grad = dot_last(grad_low, down_full)
        down_grad = dot_first(kept["activated"], grad_low)
        unused_gelu, gelu_back = jax.vjp(jax.nn.gelu, kept["up_acts"])
        up_low = gelu_back(act_grad)[0].astype(jnp.bfloat16)
        up_grad = dot_first(kept["second"], up_low)
        second_grad = dot_last(up_low, up_full)
        unused_norm, norm_back = jax.vjp(rms_scale, kept["mixed"], kept["gain_second"])
        mixed_part, gain_two_grad = norm_back(second_grad)
        mixed_grad = grad + mixed_part
        mixed_low = mixed_grad.astype(jnp.bfloat16)
        mixed_all = lax.all_gather(mixed_low, "mp", axis=0, tiled=True)
        state_grad = dot_last(mixed_all, out_full)
        out_grad = dot_first(kept["hidden"], mixed_all)
        decay = kept["decay"]
        shifted = jnp.concatenate([decay[1:], jnp.ones((1, width), jnp.float32)], axis=0)
        back_products, back_partial = lax.associative_scan(
            link, (shifted[::-1], state_grad[::-1]), axis=0
        )
        adjoint = back_partial[::-1]
        previous = jnp.concatenate(
            [jnp.zeros((1, width), jnp.float32), kept["states"][:-1]], axis=0
        )
        unused_gate, gate_back = jax.vjp(partial(gate_terms, starts=starts), kept["pre"])
        pre_low = gate_back((adjoint * previous, adjoint))[0].astype(jnp.bfloat16)
        bias_grad = jnp.sum(pre_low.astype(jnp.float32), axis=1)
        gate_grad = jnp.einsum(
            "td,ktf->kdf", kept["normed"], pre_low, preferred_element_type=jnp.float32
        )
        normed_part = jnp.einsum(
            "ktf,kdf->td", pre_low, gates_full, preferred_element_type=jnp.float32
        )
        normed_grad = lax.psum_scatter(
            normed_part.astype(jnp.bfloat16), "mp", scatter_dimension=0, tiled=True
        ).astype(jnp.float32)
        unused_first, first_back = jax.vjp(rms_scale, kept["stream"], kept["gain_first"])
        stream_part, gain_one_grad = first_back(normed_grad)
        grad = mixed_grad + stream_part
        gate_parts.append(
            (
                sum_at_owner(gate_grad.astype(jnp.bfloat16), "dp", 1),
                sum_at_owner(bias_grad.astype(jnp.bfloat16), "dp", 1),
                sum_at_owner(out_grad.astype(jnp.bfloat16), "dp", 1),
            )
        )
        mlp_parts.append(
            (
                lax.psum_scatter(up_grad, ("dp", "mp"), scatter_dimension=0, tiled=True),
                lax.psum_scatter(down_grad, ("dp", "mp"), scatter_dimension=0, tiled=True),
                lax.psum_scatter(gain_one_grad, ("dp", "mp"), scatter_dimension=0, tiled=True),
                lax.psum_scatter(gain_two_grad, ("dp", "mp"), scatter_dimension=0, tiled=True),
            )
        )
    gate_parts = gate_parts[::-1]
    mlp_parts = mlp_parts[::-1]
    gate_stack = tuple((jnp.stack([entry[member] for entry in gate_parts]) for member in range(3)))
    mlp_stack = tuple((jnp.stack([entry[member] for entry in mlp_parts]) for member in range(4)))
    return (
        stream.astype(jnp.bfloat16),
        grad,
        gate_stack[0],
        gate_stack[1],
        gate_stack[2],
        mlp_stack[2],
        mlp_stack[3],
        mlp_stack[0],
        mlp_stack[1],
    )


def body(inputs, gate_weight, gate_bias, out_weight, gain_one, gain_two, up_weight, down_weight, cotangent):
    shards = (gate_weight, gate_bias, out_weight, gain_one, gain_two, up_weight, down_weight)
    if not fits(inputs, *shards):
        return general_body(inputs, *shards, cotangent)
    out, *kept = forward(inputs, *shards)
    return settle(out, *backward(cotangent, kept))


def solution(mesh):
    placed = (
        P(("dp", "mp"), None),
        P(None, None, "dp", "mp"),
        P(None, None, ("mp", "dp")),
        P(None, "mp", "dp"),
        P(None, ("dp", "mp")),
        P(None, ("dp", "mp")),
        P(None, ("dp", "mp"), None),
        P(None, ("dp", "mp"), None),
        P(("dp", "mp"), None),
    )
    return jax.shard_map(
        body,
        mesh=mesh,
        in_specs=placed,
        out_specs=(
            P(("dp", "mp"), None),
            P(("dp", "mp"), None),
            P(None, None, "dp", "mp"),
            P(None, None, ("mp", "dp")),
            P(None, "mp", "dp"),
            P(None, ("dp", "mp")),
            P(None, ("dp", "mp")),
            P(None, ("dp", "mp"), None),
            P(None, ("dp", "mp"), None),
        ),
        check_vma=False,
    )
```

```python
from functools import partial

import jax
import jax.numpy as jnp
from jax import lax
from jax.experimental import pallas as pl
from jax.experimental.pallas import tpu as pltpu
from jax.sharding import PartitionSpec as P

LENGTH = 1024


eps = 1e-06


def cut_along(x, dim, size):
    shape = x.shape
    blocks = x.reshape(*shape[:dim], size, shape[dim] // size, *shape[dim + 1 :])
    return jnp.moveaxis(blocks, dim, 0)


def sum_at_owner(x, axis, dim):
    size = lax.axis_size(axis)
    blocks = lax.all_to_all(cut_along(x, dim, size), axis, 0, 0, tiled=True)
    return jnp.sum(blocks.astype(jnp.float32), axis=0)


def rms_scale(values, gain):
    return values * lax.rsqrt(jnp.mean(values * values, axis=-1, keepdims=True) + eps) * gain


def link(earlier, later):
    return (earlier[0] * later[0], later[0] * earlier[1] + later[1])


def gate_terms(pre_acts, starts):
    sig_forget = jax.nn.sigmoid(pre_acts[0])
    sig_input = jax.nn.sigmoid(pre_acts[1])
    total = sig_forget + sig_input
    decay = jnp.where(starts, 0.0, sig_forget / total)
    return (decay, sig_input / total * pre_acts[2])


def dot_plain(left, right):
    return jnp.dot(left, right, preferred_element_type=jnp.float32)


def dot_first(left, right):
    return lax.dot_general(
        left, right, (((0,), (0,)), ((), ())), preferred_element_type=jnp.float32
    )


def dot_last(left, right):
    return lax.dot_general(
        left, right, (((1,), (1,)), ((), ())), preferred_element_type=jnp.float32
    )


GATHER_PLAN = (
    (0, 5, 10, 15, 1, 20, 6, 25, 2, 11, 30, 7, 3, 16, 35, 12, 4),
    (),
    (),
    (),
    (21, 40, 8, 17, 26, 45, 9, 13, 31, 50, 22, 36, 55, 14, 18, 27, 41, 60, 32, 19),
    (),
    (46, 65, 23),
    (51, 70, 37),
    (56, 75, 28, 42, 24),
    (),
    (61, 80, 33),
    (66, 47, 29),
    (52,),
    (),
    (71, 34),
    (),
    (57, 76, 38),
    (),
    (),
    (81, 43, 62, 39, 67, 44),
    (),
    (48,),
    (53, 72, 49, 54, 58, 77, 82, 59),
    (),
    (),
    (63,),
    (68,),
    (73, 64),
    (),
    (69,),
    (78, 74),
    (),
    (),
    (),
    (83,),
    (),
    (79,),
    (84,),
    (),
)
SCATTER_PLAN = (
    (),
    (),
    (),
    (),
    (0,),
    (),
    (),
    (),
    (5,),
    (10, 15),
    (1,),
    (20,),
    (),
    (),
    (6,),
    (11,),
    (16,),
    (21, 2),
    (),
    (25, 7),
    (30,),
    (35,),
    (12,),
    (26, 17, 31),
    (36, 22),
    (3,),
    (8,),
    (13,),
    (),
    (40,),
    (27,),
    (18, 4),
    (),
    (45, 32, 9),
    (50, 55, 41),
    (),
    (37, 14, 23, 46, 28, 19, 51, 33, 56, 42, 24, 38, 29, 47, 34, 52, 39),
    (60,),
    (),
    (57,),
    (43,),
    (48,),
    (),
    (61, 53),
    (58,),
    (65, 44),
    (70,),
    (75,),
    (62, 49),
    (66, 54),
    (71, 76, 59),
    (80,),
    (63, 67, 81, 72, 64, 77, 68, 82, 73, 78, 83, 69, 74, 79, 84),
)


ALL = slice(None)
MESH = pl.DeviceIdType.MESH
BF = jnp.bfloat16
F32 = jnp.float32
SHIFT = 0.25
LOG_SHIFT = -1.3862943611198906
TOP = 87.0
GELU_A = 0.7978845608028654
GELU_B = 0.044715
ROWS = 256
STEPS = ROWS // 8


def first_of(mp, rows):
    return lax.div(jnp.minimum(lax.rem(mp * (LENGTH - rows), LENGTH), rows), ROWS)


def place():
    dp = lax.axis_index("dp")
    mp = lax.axis_index("mp")
    return (lax.div(dp, 2), lax.rem(dp, 2), lax.div(mp, 2), lax.rem(mp, 2))


def device(z, x, y, c):
    return (z * 2 + x, y * 2 + c)


def greet(wait=True):
    z, x, y, c = place()
    partners = [device(lax.rem(z + k, 4), x, y, c) for k in (1, 2, 3)]
    partners += [device(z, 1 - x, y, c), device(z, x, 1 - y, c)]
    partners += [device(z, x, y, 1 - c), device(z, x, 1 - y, 1 - c)]
    barrier = pltpu.get_barrier_semaphore()
    for partner in partners:
        pl.semaphore_signal(barrier, inc=1, device_id=partner, device_id_type=MESH)
    if wait:
        greeted()


def greeted():
    pl.semaphore_wait(pltpu.get_barrier_semaphore(), 7)


class Gather:
    def __init__(self, bufs, own, items, plan, send, recv):
        self.bufs = bufs
        self.own = own
        self.items = items
        self.send = send
        self.recv = recv
        self.at = place()
        self.sent = []
        self.plan = [list(row) for row in plan]

    def view(self, item, z, x, y, c, h):
        kind, l, part = item
        w4, up, dn, vec = self.bufs
        if kind == "vec":
            return vec.at[z, x, y, c, h]
        if kind == "gate":
            return w4.at[l, y, c, part, z, x, h]
        if kind == "up":
            return up.at[l, part, h, z, x, y, c]
        return dn.at[l, z, x, y, c, part, h]

    def go(self, n, slot, ref, target):
        cp = pltpu.make_async_remote_copy(
            src_ref=ref,
            dst_ref=ref,
            send_sem=self.send.at[n, slot],
            recv_sem=self.recv.at[n, slot],
            device_id=target,
            device_id_type=MESH,
        )
        cp.start()
        self.sent.append(cp)

    def landed(self, n, slot, ref, source):
        pltpu.make_async_remote_copy(
            src_ref=ref,
            dst_ref=ref,
            send_sem=self.send.at[n, slot],
            recv_sem=self.recv.at[n, slot],
            device_id=source,
            device_id_type=MESH,
        ).wait_recv()

    def stage(self, step, n, item):
        z, x, y, c = self.at
        v = lambda *where: self.view(item, *where)
        to_x = device(z, 1 - x, y, c)
        to_y = device(z, x, 1 - y, c)
        to_c = device(z, x, y, 1 - c)
        if step == 0:
            for cp in self.own.pop(item):
                cp.wait()
            for k in (1, 2, 3):
                self.go(n, k - 1, v(z, x, y, c, ALL), device(lax.rem(z + k, 4), x, y, c))
        elif step == 1:
            for k in (1, 2, 3):
                source = lax.rem(z + 4 - k, 4)
                self.landed(n, k - 1, v(source, x, y, c, ALL), device(source, x, y, c))
            self.go(n, 3, v(ALL, x, y, c, 0), to_x)
            self.go(n, 4, v(ALL, x, y, c, 1), to_y)
            self.go(n, 7, v(ALL, x, y, c, ALL), to_c)
        elif step == 2:
            self.landed(n, 3, v(ALL, 1 - x, y, c, 0), to_x)
            self.go(n, 5, v(ALL, ALL, y, c, 0), to_y)
            self.landed(n, 4, v(ALL, x, 1 - y, c, 1), to_y)
            self.go(n, 6, v(ALL, x, ALL, c, 1), to_x)
            self.go(n, 8, v(ALL, 1 - x, y, c, 0), to_c)
            self.go(n, 9, v(ALL, x, 1 - y, c, 1), to_c)
        elif step == 3:
            self.landed(n, 5, v(ALL, ALL, 1 - y, c, 0), to_y)
            self.go(n, 10, v(ALL, ALL, 1 - y, c, 0), to_c)
            self.landed(n, 6, v(ALL, 1 - x, ALL, c, 1), to_x)
            self.go(n, 11, v(ALL, 1 - x, ALL, c, 1), to_c)
        else:
            self.landed(n, 7, v(ALL, x, y, 1 - c, ALL), to_c)
            self.landed(n, 8, v(ALL, 1 - x, y, 1 - c, 0), to_c)
            self.landed(n, 9, v(ALL, x, 1 - y, 1 - c, 1), to_c)
            self.landed(n, 10, v(ALL, ALL, 1 - y, 1 - c, 0), to_c)
            self.landed(n, 11, v(ALL, 1 - x, ALL, 1 - c, 1), to_c)

    def go_on(self):
        for code in self.plan.pop(0):
            n, step = divmod(code, 5)
            self.stage(step, n, self.items[n])

    def finish(self):
        for cp in self.sent:
            cp.wait_send()


def dot(a, b):
    return jnp.dot(a, b, preferred_element_type=F32)


def dot_nt(a, b):
    return lax.dot_general(a, b, (((1,), (1,)), ((), ())), preferred_element_type=F32)


def dot_tn(a, b):
    return lax.dot_general(a, b, (((0,), (0,)), ((), ())), preferred_element_type=F32)


def spread(vec, l, first, size, total, per_mp):
    rows = vec[:, :, :, :, l].reshape(256, 128).astype(BF)
    j = lax.broadcasted_iota(jnp.int32, (128, total), 0)
    d = lax.broadcasted_iota(jnp.int32, (128, total), 1)
    pick = jnp.where(j == first + lax.rem(d, size), 1.0, 0.0).astype(BF)
    wide = dot(rows, pick)
    r = lax.div(lax.broadcasted_iota(jnp.int32, (256, total), 0), 8)
    d = lax.broadcasted_iota(jnp.int32, (256, total), 1)
    if per_mp:
        owner = lax.div(lax.rem(d, total // 4), size) * 4 + lax.div(d, total // 4)
    else:
        owner = lax.div(d, size)
    return jnp.sum(jnp.where(r == owner, wide, 0.0), axis=0, keepdims=True)


def combine(a, b, row, sign):
    for s in (1, 2, 4):
        keep = (row >= s) if sign > 0 else (row < 8 - s)
        by = s if sign > 0 else 8 - s
        am = jnp.where(keep, a, 0.0)
        b = b + am * pltpu.roll(b, by, 0)
        if s < 4:
            a = jnp.where(keep, a * pltpu.roll(a, by, 0), a)
        else:
            a = jnp.where(keep, a * pltpu.roll(a, by, 0), a)
    return a, b


def into_steps(v, turn, i):
    for n in range(4):
        turn[n, pl.ds(i * ROWS, ROWS), :] = v[:, n * 128 : n * 128 + 128]
    parts = []
    for n in range(4):
        rows = [turn[n, pl.ds(i * ROWS + j, 8, stride=STEPS), :] for j in range(STEPS)]
        parts.append(jnp.concatenate(rows, axis=0))
    return jnp.concatenate(parts, axis=1)


def unturn(v, turn, i):
    for n in range(4):
        for j in range(STEPS):
            turn[n, pl.ds(i * ROWS + j, 8, stride=STEPS), :] = v[j * 8 : j * 8 + 8, n * 128 : n * 128 + 128]
    return jnp.concatenate([turn[n, pl.ds(i * ROWS, ROWS), :] for n in range(4)], axis=1)


def fwd_kernel(
    x_in, gate_in, out_in, up_in, down_in, gain_one_in, gain_two_in, bias_in,
    out_hbm, w4_hbm, up_hbm, dn_hbm, gain_hbm, stream_hbm, mixed_hbm, keep_hbm, q_hbm, hid_hbm, ff_hbm, turned_hbm,
    w4, up, dn, vec, normed, stream, mixed, turned, turn, ends, enter, keep, states, c3, hid, ff, bias, gain, c_out, c_in,
    ag_send, ag_recv, own_sem, spill_sem, carry_send, carry_recv,
):
    z, x, y, c = place()
    mp = y * 2 + c
    rows_all = normed.shape[0]
    chunks = rows_all // ROWS
    fill = []

    def local(src, dst, sem):
        cp = pltpu.make_async_copy(src, dst, sem)
        cp.start()
        return cp

    own = {}
    n_own = 0

    def add_own(key, src, dst):
        nonlocal n_own
        own.setdefault(key, []).append(local(src, dst, own_sem.at[n_own]))
        n_own += 1

    x_copy = local(x_in, normed, own_sem.at[48])
    own[("vec", 0, 0)] = []
    vec[z, x, y, c] = jnp.zeros((2, 8, 128), F32)
    for l in range(2):
        ours = [gain_one_in[l : l + 1, :], gain_two_in[l : l + 1, :]] + [bias_in[k, l : l + 1, :] for k in range(3)]
        vec[z, x, y, c, l, 0:1, :] = jnp.concatenate([v.astype(F32) for v in ours], axis=1)
    for l in range(2):
        for k in range(3):
            add_own(("gate", l, k), gate_in.at[l, k], w4.at[l, y, c, k, z, x])
        add_own(("gate", l, 3), out_in.at[l], w4.at[l, y, c, 3, z, x])
        for pair in range(2):
            for h in range(2):
                columns = pl.ds((pair * 2 + h) * 512, 512)
                add_own(("up", l, pair), up_in.at[l, :, columns], up.at[l, pair, h, z, x, y, c])
            add_own(("down", l, pair), down_in.at[l, pair], dn.at[l, z, x, y, c, pair])
    greet()
    items = [("vec", 0, 0)]
    for l in range(2):
        items += [("gate", l, k) for k in range(4)]
        items += [(kind, l, pair) for kind in ("up", "down") for pair in range(2)]
    gather = Gather((w4, up, dn, vec), own, items, GATHER_PLAN, ag_send, ag_recv)
    go_on = gather.go_on

    n_spill = 0
    spills = {}

    def spill(key, src, dst):
        nonlocal n_spill
        spills[key] = local(src, dst, spill_sem.at[n_spill])
        n_spill += 1

    def settle(key):
        if key in spills:
            spills.pop(key).wait()


    def rms(src, dst, g):
        @pl.loop(0, chunks)
        def _(i):
            r = pl.ds(pl.multiple_of(i * ROWS, ROWS), ROWS)
            v = src[r, :]
            scale = lax.rsqrt(jnp.mean(v * v, axis=-1, keepdims=True) + eps)
            n = (v * scale * g).astype(BF)
            dst[r, :] = n
            turned[0, :, r] = n.T

    def gate_panel(l, p):
        w = [w4[l, p // 2, p % 2, k].reshape(512, 256) for k in range(3)]
        bs = [bias[l, k : k + 1, p * 256 : (p + 1) * 256] for k in range(3)]

        @pl.loop(0, chunks)
        def _(i):
            r = pl.ds(pl.multiple_of(i * ROWS, ROWS), ROWS)
            n = normed[r, :]
            f, inp, cand = [dot(n, w[k]) + bs[k] for k in range(3)]
            e_f = jnp.exp(jnp.minimum(-f, TOP) + LOG_SHIFT)
            e_i = jnp.exp(jnp.minimum(-inp, TOP) + LOG_SHIFT)
            a_f = e_f + SHIFT
            a_i = e_i + SHIFT
            total = a_f + a_i
            inv = pl.reciprocal(total, approx=True)
            inv = inv * (2.0 - total * inv)
            share = a_f * inv
            decay = a_i * inv
            drive = share * cand
            keep[p, r, :] = share
            c3[p, 0, r, :] = (decay * (e_f * inv)).astype(BF)
            c3[p, 1, r, :] = (share * (e_i * inv)).astype(BF)
            c3[p, 2, r, :] = cand.astype(BF)
            s = drive[0:8]
            a = decay[0:8]
            local_states = [s]
            for j in range(1, STEPS):
                t = slice(j * 8, j * 8 + 8)
                s = decay[t] * s + drive[t]
                a = a * decay[t]
                local_states.append(s)
            states[p, r, :] = jnp.concatenate(local_states, axis=0)
            columns = slice(p * 256, p * 256 + 256)
            ends[0, i, :, columns] = a
            ends[1, i, :, columns] = s

    row = lax.broadcasted_iota(jnp.int32, (8, 1024), 0)
    first_chunk = first_of(mp, rows_all)

    def carries(entering):
        for i in range(chunks):
            c0 = jnp.where(first_chunk == i, 0.0, entering)
            a, s = combine(ends[0, i], ends[1, i], row, 1)
            enter[i] = jnp.where(row == 0, c0, pltpu.roll(a, 1, 0) * c0 + pltpu.roll(s, 1, 0))
            entering = jnp.broadcast_to(a[7:8] * c0[7:8] + s[7:8], (8, 1024))
        return entering

    def carry_copy(l, there):
        return pltpu.make_async_remote_copy(
            src_ref=c_out.at[l],
            dst_ref=c_in.at[l],
            send_sem=carry_send.at[l],
            recv_sem=carry_recv.at[l],
            device_id=device(z, x, lax.div(there, 2), lax.rem(there, 2)),
            device_id_type=MESH,
        )

    def carry_out(l):
        c_out[l] = carries(jnp.zeros((8, 1024), F32))

        @pl.when(mp < 3)
        def _():
            carry_copy(l, jnp.minimum(mp + 1, 3)).start()

    def carry_into(l):
        @pl.when(mp > 0)
        def _():
            carry_copy(l, jnp.maximum(mp - 1, 0)).wait_recv()
            carries(c_in[l])

        @pl.when(mp < 3)
        def _():
            carry_copy(l, jnp.minimum(mp + 1, 3)).wait_send()

    def project(l):
        g = gain[l, 1:2, :]
        w = [w4[l, p // 2, p % 2, 3].reshape(512, 256) for p in range(4)]

        @pl.loop(0, chunks)
        def _(i):
            r = pl.ds(pl.multiple_of(i * ROWS, ROWS), ROWS)
            v = stream[r, :]
            for p in range(4):
                share = keep[p, r, :]
                s_local = states[p, r, :]
                cand = c3[p, 2, r, :].astype(F32)
                enters = enter[i, :, p * 256 : p * 256 + 256]
                before = enters
                weight = enters
                now, gap = [], []
                for j in range(STEPS):
                    t = slice(j * 8, j * 8 + 8)
                    weight = weight - share[t] * weight
                    s = s_local[t] + weight
                    gap.append(before - cand[t])
                    now.append(s)
                    before = s
                gap = jnp.concatenate(gap, axis=0)
                h = jnp.concatenate(now, axis=0).astype(BF)
                hid[p, r, :] = h
                c3[p, 0, r, :] = (gap * c3[p, 0, r, :].astype(F32)).astype(BF)
                c3[p, 1, r, :] = (-gap * c3[p, 1, r, :].astype(F32)).astype(BF)
                v = v + dot_nt(h, w[p])
            mixed[r, :] = v
            scale = lax.rsqrt(jnp.mean(v * v, axis=-1, keepdims=True) + eps)
            n = (v * scale * g).astype(BF)
            normed[r, :] = n
            turned[1, :, r] = n.T

    def feed_up(l, q):
        w_up = up[l, q // 2, q % 2].reshape(512, 512)

        @pl.loop(0, chunks)
        def _(i):
            r = pl.ds(pl.multiple_of(i * ROWS, ROWS), ROWS)
            u = dot(normed[r, :], w_up)
            sq = u * u
            t = jnp.tanh(u * (GELU_A + (GELU_A * GELU_B) * sq))
            gate = 0.5 + 0.5 * t
            act = (u * gate).astype(BF)
            slope = gate + (0.5 * u) * (1.0 - t * t) * (GELU_A + (3.0 * GELU_A * GELU_B) * sq)
            for half in range(2):
                side = slice(half * 256, half * 256 + 256)
                ff[q, half, r, :] = slope[:, side].astype(BF)
                ff[q, 2 + half, r, :] = act[:, side]

    def feed_down(l):
        w_down = dn[l].reshape(2048, 512)

        @pl.loop(0, chunks)
        def _(i):
            r = pl.ds(pl.multiple_of(i * ROWS, ROWS), ROWS)
            acts = [ff[q, 2 + half, r, :] for q in range(4) for half in range(2)]
            v = mixed[r, :] + dot(jnp.concatenate(acts, axis=1), w_down)
            if l == 0:
                stream[r, :] = v
            else:
                normed[r, :] = unturn(v, turn, i).astype(BF)

    go_on()
    for l in range(2):
        gain[l, 0:1, :] = spread(vec, l, 0, 16, 512, False)
        gain[l, 1:2, :] = spread(vec, l, 16, 16, 512, False)
        for k in range(3):
            bias[l, k : k + 1, :] = spread(vec, l, 32 + 32 * k, 32, 1024, True)
        go_on()
    x_copy.wait()

    @pl.loop(0, chunks)
    def _(i):
        r = pl.ds(pl.multiple_of(i * ROWS, ROWS), ROWS)
        stream[r, :] = into_steps(normed[r, :].astype(F32), turn, i)

    spill("gain", gain, gain_hbm)
    for l in range(2):
        settle(("first", 0))
        rms(stream, normed, gain[l, 0:1, :])
        spill(("first", l), turned.at[0], turned_hbm.at[l, 0])
        settle(("keep", 0))
        settle(("q", 0))
        spill(("stream", l), stream, stream_hbm.at[l])
        go_on()
        go_on()
        for p in range(4):
            gate_panel(l, p)
            go_on()
        spill(("keep", l), keep, keep_hbm.at[l])
        carry_out(l)
        settle(("hid", 0))
        settle(("mixed", 0))
        go_on()
        carry_into(l)
        settle(("second", 0))
        project(l)
        spill(("second", l), turned.at[1], turned_hbm.at[l, 1])
        spill(("q", l), c3.at[:, pl.ds(0, 2)], q_hbm.at[l])
        spill(("hid", l), hid, hid_hbm.at[l])
        spill(("w4", l), w4.at[l], w4_hbm.at[l])
        spill(("mixed", l), mixed, mixed_hbm.at[l])
        go_on()
        for q in range(4):
            settle(("ff", 0, q))
            go_on()
            feed_up(l, q)
            spill(("ff", l, q), ff.at[q], ff_hbm.at[l, q])
            go_on()
        spill(("up", l), up.at[l], up_hbm.at[l])
        settle(("stream", l))
        go_on()
        feed_down(l)
        spill(("dn", l), dn.at[l], dn_hbm.at[l])
        go_on()
    spill("result", normed, out_hbm)
    for key in list(spills):
        settle(key)
    gather.finish()


def forward(x, gate_weight, gate_bias, out_weight, gain_one, gain_two, up_weight, down_weight):
    rows = x.shape[0]
    any_space = pl.BlockSpec(memory_space=pl.ANY)
    args = (
        x,
        gate_weight.reshape(2, 3, 2, 32, 256),
        out_weight.transpose(0, 2, 1).reshape(2, 2, 32, 256),
        up_weight,
        down_weight.reshape(2, 2, 2, 16, 512),
        gain_one,
        gain_two,
        gate_bias.transpose(1, 0, 2),
    )
    s = jax.ShapeDtypeStruct
    w4 = (2, 2, 2, 4, 4, 2, 2, 32, 256)
    up = (2, 2, 2, 4, 2, 2, 2, 16, 512)
    dn = (2, 4, 2, 2, 2, 2, 2, 16, 512)
    dma = pltpu.SemaphoreType.DMA
    return pl.pallas_call(
        fwd_kernel,
        name="forward",
        out_shape=(
            s((rows, 512), BF), s(w4, BF), s(up, BF), s(dn, BF), s((2, 8, 512), F32), s((2, rows, 512), F32),
            s((2, rows, 512), F32), s((2, 4, rows, 256), F32), s((2, 4, 2, rows, 256), BF),
            s((2, 4, rows, 256), BF), s((2, 4, 4, rows, 256), BF), s((2, 2, 512, rows), BF),
        ),
        in_specs=[any_space] * 5 + [pl.BlockSpec(memory_space=pltpu.VMEM)] * 3,
        out_specs=(any_space,) * 12,
        scratch_shapes=[
            pltpu.VMEM(w4, BF), pltpu.VMEM(up, BF), pltpu.VMEM(dn, BF), pltpu.VMEM((4, 2, 2, 2, 2, 8, 128), F32),
            pltpu.VMEM((rows, 512), BF), pltpu.VMEM((rows, 512), F32), pltpu.VMEM((rows, 512), F32), pltpu.VMEM((2, 512, rows), BF), pltpu.VMEM((4, rows, 128), F32),
            pltpu.VMEM((2, 3, 8, 1024), F32), pltpu.VMEM((3, 8, 1024), F32),
            pltpu.VMEM((4, rows, 256), F32), pltpu.VMEM((4, rows, 256), F32), pltpu.VMEM((4, 3, rows, 256), BF),
            pltpu.VMEM((4, rows, 256), BF), pltpu.VMEM((4, 4, rows, 256), BF),
            pltpu.VMEM((2, 8, 1024), F32), pltpu.VMEM((2, 8, 512), F32),
            pltpu.VMEM((2, 8, 1024), F32), pltpu.VMEM((2, 8, 1024), F32),
            dma((17, 12)), dma((17, 12)), dma((49,)), dma((32,)), dma((2,)), dma((2,)),
        ],
        compiler_params=pltpu.CompilerParams(
            collective_id=0, has_side_effects=True, vmem_limit_bytes=62 * 2**20
        ),
    )(*args)


class Scatter:
    def __init__(self, grads, landing, plan, send, recv, give):
        self.grads = grads
        self.landing = landing
        self.send = send
        self.recv = recv
        self.give = give
        self.at = place()
        self.sent = {}
        self.items = []
        self.plan = [list(row) for row in plan]

    def own(self, item, z, x, y, c, h):
        kind, l, part = item
        w4, up, dn, vec = self.grads
        if kind == "vec":
            return vec.at[z, x, y, c, h]
        if kind == "gate":
            return w4.at[y, c, part, z, x, h]
        if kind == "up":
            return up.at[l, part, h, z, x, y, c]
        return dn.at[l, z, x, y, c, part, h]

    def land(self, item, stage, *where):
        kind, l, part = item
        ref = self.landing[("gate", "up", "down", "vec").index(kind)][stage]
        where = where if kind == "vec" else (l, part, *where)
        return ref.at[where] if where else ref

    def copy(self, n, slot, src, dst, target):
        return pltpu.make_async_remote_copy(
            src_ref=src,
            dst_ref=dst,
            send_sem=self.send.at[n, slot],
            recv_sem=self.recv.at[n, slot],
            device_id=target,
            device_id_type=MESH,
        )

    def go(self, n, slot, src, dst, target):
        cp = self.copy(n, slot, src, dst, target)
        cp.start()
        self.sent.setdefault(n, []).append(cp)

    def landed(self, n, slot, dst, source):
        self.copy(n, slot, dst, dst, source).wait_recv()

    def add(self, item, stage):
        z, x, y, c = self.at
        kind = item[0]

        def plus(there, *where):
            there[...] = there[...] + self.land(item, stage, *where)[...]

        @pl.loop(0, 4)
        def _(n):
            if stage == 0:
                for i in range(2):
                    for j in range(2):
                        for h in range(2):
                            if kind == "gate":
                                plus(self.own(item, n, j, i, c, h), i, n, j, h)
                            elif kind == "up":
                                plus(self.own(item, n, i, j, c, h), h, n, i, j)
                            else:
                                plus(self.own(item, n, i, j, c, h), n, i, j, h)
            elif stage == 1:
                for i in range(2):
                    plus(self.own(item, n, i, y, c, 0), n, i)
            elif stage == 2:
                for i in range(2):
                    plus(self.own(item, n, x, i, c, 1), *((i, n) if kind == "gate" else (n, i)))
            else:
                for h in range(2):
                    plus(self.own(item, n, x, y, c, h), h, n)

    def total(self, item, h):
        z, x, y, c = self.at
        v = self.own(item, z, x, y, c, h)[...].astype(F32)
        for j in range(3):
            v = v + self.land(item, 4, j, h)[...].astype(F32)
        return v

    def stage(self, step, n, item):
        z, x, y, c = self.at
        v = lambda *where: self.own(item, *where)
        to_x = device(z, 1 - x, y, c)
        to_y = device(z, x, 1 - y, c)
        to_c = device(z, x, y, 1 - c)
        land = lambda *w: self.land(item, *w)
        if step == 0:
            self.go(n, 0, v(ALL, ALL, ALL, 1 - c, ALL), land(0), to_c)
        elif step == 1:
            self.landed(n, 0, land(0), to_c)
            self.add(item, 0)
            self.go(n, 1, v(ALL, ALL, 1 - y, c, 0), land(1), to_y)
            self.go(n, 2, v(ALL, 1 - x, ALL, c, 1), land(2), to_x)
        elif step == 2:
            self.landed(n, 1, land(1), to_y)
            self.add(item, 1)
            self.go(n, 3, v(ALL, 1 - x, y, c, 0), land(3, 0), to_x)
            self.landed(n, 2, land(2), to_x)
            self.add(item, 2)
            self.go(n, 4, v(ALL, x, 1 - y, c, 1), land(3, 1), to_y)
        elif step == 3:
            self.landed(n, 3, land(3, 0), to_x)
            self.landed(n, 4, land(3, 1), to_y)
            self.add(item, 3)
            for k in (1, 2, 3):
                there = lax.rem(z + k, 4)
                self.go(n, 4 + k, v(there, x, y, c, ALL), land(4, k - 1), device(there, x, y, c))
        else:
            for k in (1, 2, 3):
                source = lax.rem(z + 4 - k, 4)
                self.landed(n, 4 + k, land(4, k - 1), device(source, x, y, c))
            self.give(item, self)

    def go_on(self):
        for code in self.plan.pop(0):
            n, step = divmod(code, 5)
            self.stage(step, n, self.items[n])

    def settle(self, numbers):
        for n in numbers:
            for cp in self.sent.pop(n):
                cp.wait_send()


def spread_back(g, first, size, total, per_mp):
    r = lax.broadcasted_iota(jnp.int32, (32, total), 0)
    d = lax.broadcasted_iota(jnp.int32, (32, total), 1)
    if per_mp:
        owner = lax.div(lax.rem(d, total // 4), size) * 4 + lax.div(d, total // 4)
    else:
        owner = lax.div(d, size)
    rows = jnp.where(r == owner, g, 0.0)
    d = lax.broadcasted_iota(jnp.int32, (total, 128), 0)
    j = lax.broadcasted_iota(jnp.int32, (total, 128), 1)
    pick = jnp.where(j == first + lax.rem(d, size), 1.0, 0.0).astype(BF)
    high = rows.astype(BF)
    rest = rows - high.astype(F32)
    middle = rest.astype(BF)
    low = (rest - middle.astype(F32)).astype(BF)
    return dot(high, pick) + dot(middle, pick) + dot(low, pick)


def bwd_kernel(
    ct_in, w4_in, up_in, dn_in, gain_in, stream_in, mixed_in, keep_in, q_in, hid_in, ff_in, turned_in,
    grad_hbm, gate_hbm, out_hbm, up_hbm, down_hbm, vec_hbm,
    w4, up, dn, gain, keep, pre, mixed, ff, grad, acc, low, low_t, act_t, up_low, sg, c_out, c_in,
    ends, enter, gains, biases, g_w4, g_up, g_dn, g_vec,
    lw0, lw1, lw2, lw3, lw4, lu0, lu1, lu2, lu3, lu4, ld0, ld1, ld2, ld3, ld4, lv0, lv1, lv2, lv3, lv4,
    f_w4, f_up, f_dn, f_vec,
    rs_send, rs_recv, load_sem, save_sem, carry_send, carry_recv,
):
    z, x, y, c = place()
    mp = y * 2 + c
    rows_all = low.shape[0]
    chunks = rows_all // ROWS
    loads = {}
    n_load = 0
    saves = []

    def load(key, src, dst):
        nonlocal n_load
        cp = pltpu.make_async_copy(src, dst, load_sem.at[n_load])
        cp.start()
        loads[key] = cp
        n_load += 1

    def ready(key):
        loads.pop(key).wait()

    def save(src, dst):
        cp = pltpu.make_async_copy(src, dst, save_sem.at[len(saves)])
        cp.start()
        saves.append(cp)

    def load_feed(l):
        load("dn", dn_in.at[l], dn)
        load("up", up_in.at[l], up)

    def load_chunk(l, q):
        load(("ff", q), ff_in.at[l, q], ff.at[q % 2])

    def load_gates(l):
        load("w4", w4_in.at[l], w4)
        load("keep", keep_in.at[l], keep)
        load("q", q_in.at[l], pre.at[:, pl.ds(0, 2)])

    load("ct", ct_in, low)
    load("gain", gain_in, gain)
    load_feed(1)
    load_chunk(1, 0)
    load("act_t", turned_in.at[1, 1], act_t)
    load("mixed", mixed_in.at[1], mixed)
    load_chunk(1, 1)
    load_gates(1)
    greet(wait=False)

    def give(item, scatter):
        kind, l, part = item
        if kind == "gate":
            for h in range(2):
                f_w4[l, part, h] = scatter.total(item, h)
            save(f_w4.at[l, part], gate_hbm.at[l, part] if part < 3 else out_hbm.at[l])
        elif kind == "up":
            for h in range(2):
                f_up[l, part, h] = scatter.total(item, h)
                save(f_up.at[l, part, h], up_hbm.at[l, :, pl.ds((part * 2 + h) * 512, 512)])
        elif kind == "down":
            for h in range(2):
                f_dn[l, part, h] = scatter.total(item, h)
            save(f_dn.at[l, part], down_hbm.at[l, part])
        else:
            for h in range(2):
                f_vec[h] = scatter.total(item, h)
            save(f_vec, vec_hbm)

    landing = (
        (lw0, lw1, lw2, lw3, lw4), (lu0, lu1, lu2, lu3, lu4), (ld0, ld1, ld2, ld3, ld4), (lv0, lv1, lv2, lv3, lv4),
    )
    scatter = Scatter((g_w4, g_up, g_dn, g_vec), landing, SCATTER_PLAN, rs_send, rs_recv, give)
    go_on = scatter.go_on

    def push(*item):
        scatter.items.append(item)

    def each(fn):
        @pl.loop(0, chunks)
        def _(i):
            fn(i, pl.ds(pl.multiple_of(i * ROWS, ROWS), ROWS))

    def feed(l, q):
        slot = q % 2
        w_down = dn[q].reshape(512, 512)
        w_up = up[q // 2, q % 2].reshape(512, 512)

        def part(i, r):
            act_grad = dot_nt(low[r, :], w_down)
            slope = jnp.concatenate([ff[slot, 0, r, :], ff[slot, 1, r, :]], axis=1).astype(F32)
            u = (act_grad * slope).astype(BF)
            up_low[r, :] = u
            back = dot_nt(u, w_up)
            acc[r, :] = back if q == 0 else acc[r, :] + back

        each(part)
        go_on()
        for half in range(2):
            g = dot(act_t[half * 256 : half * 256 + 256, :], up_low[...]).astype(BF)
            g_up[l, q // 2, q % 2, half * 2 : half * 2 + 2] = g.reshape(2, 2, 2, 2, 16, 512)
        for half in range(2):
            g = dot_tn(ff[slot, 2 + half], low[...]).astype(BF)
            g_dn[l, q, half] = g.reshape(2, 2, 2, 2, 16, 512)

    def rms_back(l, which, src, values_t):
        g = gain[l, which : which + 1, :]
        gains[l, which : which + 1, :] = jnp.zeros((1, 512), F32)

        def part(i, r):
            v = src[r, :]
            scale = lax.rsqrt(jnp.mean(v * v, axis=-1, keepdims=True) + eps)
            u = v * scale
            d = acc[r, :]
            gains[l, which : which + 1, :] += jnp.sum(d * u, axis=0, keepdims=True)
            dg = d * g
            new = grad[r, :] + scale * (dg - u * jnp.mean(dg * u, axis=-1, keepdims=True))
            grad[r, :] = new
            new = new.astype(BF)
            low[r, :] = new
            if values_t is not None:
                values_t[:, r] = new.T

        each(part)

    def out_back(p):
        g = dot(low_t[...], ff[0, p]).astype(BF)
        g_w4[p // 2, p % 2, 3] = g.reshape(4, 2, 2, 32, 256)

    def states_back(p):
        w = w4[p // 2, p % 2, 3].reshape(512, 256)

        def part(i, r):
            v = dot(low[r, :], w)
            share = keep[p, r, :]
            decay = 1.0 - share
            t = slice(ROWS - 8, ROWS)
            adjoint = v[t]
            parts = [adjoint]
            a = decay[t]
            passed = a * adjoint
            for j in range(STEPS - 2, -1, -1):
                t = slice(j * 8, j * 8 + 8)
                adjoint = v[t] + passed
                passed = decay[t] * adjoint
                a = a * decay[t]
                parts.append(adjoint)
            whole = jnp.concatenate(parts[::-1], axis=0)
            for n in range(2):
                sg[p * 2 + n, r, :] = whole[:, n * 128 : n * 128 + 128]
            columns = slice(p * 256, p * 256 + 256)
            ends[0, i, :, columns] = a
            ends[1, i, :, columns] = passed

        each(part)

    row = lax.broadcasted_iota(jnp.int32, (8, 1024), 0)
    first_chunk = first_of(mp, rows_all)

    def carries(entering):
        for i in range(chunks - 1, -1, -1):
            c0 = jnp.where(first_chunk == i + 1, 0.0, entering)
            a, v = combine(ends[0, i], ends[1, i], row, -1)
            enter[i] = jnp.where(row == 7, c0, pltpu.roll(a, 7, 0) * c0 + pltpu.roll(v, 7, 0))
            entering = jnp.broadcast_to(a[0:1] * c0[0:1] + v[0:1], (8, 1024))
        return entering

    def carry_copy(l, there):
        return pltpu.make_async_remote_copy(
            src_ref=c_out.at[l],
            dst_ref=c_in.at[l],
            send_sem=carry_send.at[l],
            recv_sem=carry_recv.at[l],
            device_id=device(z, x, lax.div(there, 2), lax.rem(there, 2)),
            device_id_type=MESH,
        )

    def carry_out(l):
        c_out[l] = carries(jnp.zeros((8, 1024), F32))

        @pl.when(mp > 0)
        def _():
            carry_copy(l, jnp.maximum(mp - 1, 0)).start()

    def carry_into(l):
        @pl.when(mp < 3)
        def _():
            carry_copy(l, jnp.minimum(mp + 1, 3)).wait_recv()
            carries(c_in[l])

        @pl.when(mp > 0)
        def _():
            carry_copy(l, jnp.maximum(mp - 1, 0)).wait_send()

    def pre_back(p):
        def part(i, r):
            share = keep[p, r, :]
            local = jnp.concatenate([sg[p * 2, r, :], sg[p * 2 + 1, r, :]], axis=1)
            weight = enter[i, :, p * 256 : p * 256 + 256]
            parts = []
            for j in range(STEPS - 1, -1, -1):
                t = slice(j * 8, j * 8 + 8)
                parts.append(local[t] + weight)
                if j:
                    weight = weight - share[t] * weight
            adjoint = jnp.concatenate(parts[::-1], axis=0)
            for k in range(3):
                v = share if k == 2 else pre[p, k, r, :].astype(F32)
                pre[p, k, r, :] = (adjoint * v).astype(BF)

        each(part)

    def normed_back(first):
        w = {(p, k): w4[p // 2, p % 2, k].reshape(512, 256) for p in (first, first + 1) for k in range(3)}

        def part(i, r):
            back = 0.0 if first == 0 else acc[r, :]
            for p, k in w:
                back = back + dot_nt(pre[p, k, r, :], w[p, k])
            acc[r, :] = back

        each(part)

    def gate_grads(l, k):
        ones = jnp.ones((8, rows_all), BF)
        for p in range(4):
            values = pre[p, k]
            g_w4[p // 2, p % 2, k] = dot(act_t[...], values).astype(BF).reshape(4, 2, 2, 32, 256)
            biases[l, k : k + 1, p * 256 : p * 256 + 256] = dot(ones, values)[0:1, :]

    ready("ct")

    def widen(i, r):
        v = into_steps(low[r, :].astype(F32), sg, i)
        grad[r, :] = v
        low[r, :] = v.astype(BF)

    each(widen)
    ready("gain")
    for l in (1, 0):
        ready("act_t")
        go_on()
        ready("dn")
        ready("up")
        for q in range(4):
            ready(("ff", q))
            feed(l, q)
            if l == 1 and q == 0:
                greeted()
            if q < 2:
                load_chunk(l, q + 2)
            elif q == 2:
                load("hid", hid_in.at[l], ff.at[0])
            if q % 2 == 1:
                push("up", l, q // 2)
            go_on()
        push("down", l, 0)
        push("down", l, 1)
        go_on()
        load("act_t", turned_in.at[l, 0], act_t)
        ready("mixed")
        rms_back(l, 1, mixed, low_t)
        load("stream", stream_in.at[l], mixed)
        go_on()
        if l == 1:
            load_feed(0)
        else:
            go_on()
            scatter.settle(range(4, 8))
        ready("w4")
        ready("hid")
        for p in range(4):
            out_back(p)
        push("gate", l, 3)
        go_on()
        if l == 1:
            load_chunk(0, 0)
        ready("keep")
        for p in range(4):
            states_back(p)
            go_on()
        carry_out(l)
        go_on()
        ready("q")
        carry_into(l)
        for p in range(4):
            pre_back(p)
            if p % 2 == 1:
                go_on()
        ready("act_t")
        for k in range(3):
            gate_grads(l, k)
            push("gate", l, k)
            go_on()
        if l == 1:
            load("act_t", turned_in.at[0, 1], act_t)
        for first in (0, 2):
            normed_back(first)
            go_on()
        ready("stream")
        if l == 1:
            load_chunk(0, 1)
            load_gates(0)
        rms_back(l, 0, mixed, None)
        if l == 1:
            load("mixed", mixed_in.at[0], mixed)
        go_on()
        rows = spread_back(gains[l, 0:1, :], 0, 16, 512, False) + spread_back(gains[l, 1:2, :], 16, 16, 512, False)
        for k in range(3):
            rows = rows + spread_back(biases[l, k : k + 1, :], 32 + 32 * k, 32, 1024, True)
        for n in range(32):
            g_vec[n // 8, n // 4 % 2, n // 2 % 2, n % 2, l] = jnp.broadcast_to(rows[n : n + 1, :], (8, 128))
    push("vec", 0, 0)
    go_on()

    def finish(i, r):
        mixed[r, :] = unturn(grad[r, :], sg, i)

    each(finish)
    save(mixed, grad_hbm)
    go_on()
    scatter.settle([*range(4), *range(8, 17)])
    for cp in saves:
        cp.wait()


def backward(cotangent, kept):
    w4_all, up_all, dn_all, gain, stream, mixed, keep, q, hid, ff, turned = kept
    rows = cotangent.shape[0]
    any_space = pl.BlockSpec(memory_space=pl.ANY)
    s = jax.ShapeDtypeStruct
    dma = pltpu.SemaphoreType.DMA
    v = pltpu.VMEM
    args = (cotangent, w4_all, up_all, dn_all, gain, stream, mixed, keep, q, hid, ff, turned)
    grad, gates, out, up, down, vec = pl.pallas_call(
        bwd_kernel,
        name="backward",
        out_shape=(
            s((rows, 512), F32), s((2, 3, 2, 32, 256), F32), s((2, 2, 32, 256), F32), s((2, 16, 2048), F32),
            s((2, 2, 2, 16, 512), F32), s((2, 8, 128), F32),
        ),
        in_specs=[any_space] * len(args),
        out_specs=(any_space,) * 6,
        scratch_shapes=[
            v((2, 2, 4, 4, 2, 2, 32, 256), BF), v((2, 2, 4, 2, 2, 2, 16, 512), BF), v((4, 2, 2, 2, 2, 2, 16, 512), BF),
            v((2, 8, 512), F32), v((4, rows, 256), F32), v((4, 3, rows, 256), BF), v((rows, 512), F32),
            v((2, 4, rows, 256), BF), v((rows, 512), F32), v((rows, 512), F32), v((rows, 512), BF), v((512, rows), BF),
            v((512, rows), BF), v((rows, 512), BF), v((8, rows, 128), F32), v((2, 8, 1024), F32), v((2, 8, 1024), F32),
            v((2, 3, 8, 1024), F32), v((3, 8, 1024), F32), v((2, 8, 512), F32), v((2, 8, 1024), F32),
            v((2, 2, 4, 4, 2, 2, 32, 256), BF), v((2, 2, 2, 4, 2, 2, 2, 16, 512), BF), v((2, 4, 2, 2, 2, 2, 2, 16, 512), BF),
            v((4, 2, 2, 2, 2, 8, 128), F32),
            v((2, 4, 2, 4, 2, 2, 32, 256), BF), v((2, 4, 4, 2, 32, 256), BF), v((2, 4, 2, 4, 32, 256), BF),
            v((2, 4, 2, 4, 32, 256), BF), v((2, 4, 3, 2, 32, 256), BF),
            v((2, 2, 2, 4, 2, 2, 16, 512), BF), v((2, 2, 4, 2, 16, 512), BF), v((2, 2, 4, 2, 16, 512), BF),
            v((2, 2, 2, 4, 16, 512), BF), v((2, 2, 3, 2, 16, 512), BF),
            v((2, 2, 4, 2, 2, 2, 16, 512), BF), v((2, 2, 4, 2, 16, 512), BF), v((2, 2, 4, 2, 16, 512), BF),
            v((2, 2, 2, 4, 16, 512), BF), v((2, 2, 3, 2, 16, 512), BF),
            v((4, 2, 2, 2, 8, 128), F32), v((4, 2, 8, 128), F32), v((4, 2, 8, 128), F32), v((2, 4, 8, 128), F32),
            v((3, 2, 8, 128), F32),
            v((2, 4, 2, 32, 256), F32), v((2, 2, 2, 16, 512), F32), v((2, 2, 2, 16, 512), F32), v((2, 8, 128), F32),
            dma((17, 8)), dma((17, 8)), dma((32,)), dma((24,)), dma((2,)), dma((2,)),
        ],
        compiler_params=pltpu.CompilerParams(
            collective_id=1, has_side_effects=True, vmem_limit_bytes=63 * 2**20
        ),
    )(*args)
    return grad, gates, out, up, down, vec


def settle_kernel(*refs):
    vec, biases, gain_one, gain_two = refs[6], *refs[13:]
    for src, dst in zip(refs[:6], refs[7:13]):
        dst[...] = src[...]
    for l in range(2):
        gain_one[l : l + 1, :] = vec[l, 0:1, 0:16]
        gain_two[l : l + 1, :] = vec[l, 0:1, 16:32]
        for k in range(3):
            biases[k, l : l + 1, :] = vec[l, 0:1, 32 + 32 * k : 64 + 32 * k]


def settle(result, grad, gates, out, up, down, vec):
    rows = result.shape[0]
    s = jax.ShapeDtypeStruct
    args = (
        result, grad, gates.reshape(12, 32, 256), out.reshape(4, 32, 256), up, down.reshape(8, 16, 512),
    )
    whole = lambda *shape: pl.BlockSpec(shape, lambda i: (0,) * len(shape))
    blocks = [
        pl.BlockSpec((rows // 4, 512), lambda i: (i, 0)),
        pl.BlockSpec((rows // 4, 512), lambda i: (i, 0)),
        pl.BlockSpec((3, 32, 256), lambda i: (i, 0, 0)),
        pl.BlockSpec((1, 32, 256), lambda i: (i, 0, 0)),
        pl.BlockSpec((2, 16, 512), lambda i: (0, 0, i)),
        pl.BlockSpec((2, 16, 512), lambda i: (i, 0, 0)),
    ]
    result, grad, gates, out, up, down, biases, gain_one, gain_two = pl.pallas_call(
        settle_kernel,
        name="settle",
        grid=(4,),
        out_shape=tuple(s(v.shape, v.dtype) for v in args) + (s((3, 2, 32), F32), s((2, 16), F32), s((2, 16), F32)),
        in_specs=blocks + [whole(2, 8, 128)],
        out_specs=tuple(blocks) + (whole(3, 2, 32), whole(2, 16), whole(2, 16)),
    )(*args, vec)
    return (
        result,
        grad,
        gates.reshape(2, 3, 64, 256),
        biases.transpose(1, 0, 2),
        out.reshape(2, 64, 256).transpose(0, 2, 1),
        gain_one,
        gain_two,
        up,
        down.reshape(2, 64, 512),
    )


def fits(inputs, gate_weight, gate_bias, out_weight, gain_one, gain_two, up_weight, down_weight):
    rows = inputs.shape[0]
    shapes = (gate_weight.shape, gate_bias.shape, out_weight.shape, gain_one.shape, up_weight.shape, down_weight.shape)
    planned = ((2, 3, 64, 256), (2, 3, 32), (2, 256, 64), (2, 16), (2, 16, 2048), (2, 64, 512))
    axes = (lax.axis_size("dp"), lax.axis_size("mp"))
    return axes == (8, 4) and shapes == planned and rows == 768 and 4 * rows == 3 * LENGTH


def general_body(
    inputs,
    gate_weight,
    gate_bias,
    out_weight,
    norm_gain_one,
    norm_gain_two,
    up_weight,
    down_weight,
    cotangent,
):
    own_rows = inputs.shape[0]
    group = own_rows * lax.axis_size("mp")
    starts = (jnp.arange(group, dtype=jnp.int32) % LENGTH == 0)[:, None]
    layer_count = gate_weight.shape[0]
    width = gate_weight.shape[3]
    stream = inputs.astype(jnp.float32)
    saved = []
    held = []
    for layer_no in range(layer_count):
        gates_full, bias_full, out_full = (
            lax.all_gather(gate_weight[layer_no], "dp", axis=1, tiled=True),
            lax.all_gather(gate_bias[layer_no], "dp", axis=1, tiled=True),
            lax.all_gather(out_weight[layer_no], "dp", axis=1, tiled=True),
        )
        up_full, down_full, gain_first, gain_second = (
            lax.all_gather(up_weight[layer_no], ("dp", "mp"), axis=0, tiled=True),
            lax.all_gather(down_weight[layer_no], ("dp", "mp"), axis=0, tiled=True),
            lax.all_gather(norm_gain_one[layer_no], ("dp", "mp"), axis=0, tiled=True),
            lax.all_gather(norm_gain_two[layer_no], ("dp", "mp"), axis=0, tiled=True),
        )
        gain_first = gain_first.astype(jnp.float32)
        gain_second = gain_second.astype(jnp.float32)
        normed = rms_scale(stream, gain_first).astype(jnp.bfloat16)
        normed_all = lax.all_gather(normed, "mp", axis=0, tiled=True)
        pre_acts = (
            jnp.einsum("td,kdf->ktf", normed_all, gates_full, preferred_element_type=jnp.float32)
            + bias_full.astype(jnp.float32)[:, None, :]
        )
        decay, drive = gate_terms(pre_acts, starts)
        products, states = lax.associative_scan(link, (decay, drive), axis=0)
        hidden = states.astype(jnp.bfloat16)
        mixed = stream + lax.psum_scatter(
            dot_plain(hidden, out_full).astype(jnp.bfloat16), "mp", scatter_dimension=0, tiled=True
        ).astype(jnp.float32)
        second = rms_scale(mixed, gain_second).astype(jnp.bfloat16)
        up_acts = dot_plain(second, up_full)
        activated = jax.nn.gelu(up_acts).astype(jnp.bfloat16)
        saved.append(
            {
                "stream": stream,
                "gain_first": gain_first,
                "gain_second": gain_second,
                "normed": normed_all,
                "pre": pre_acts,
                "decay": decay,
                "states": states,
                "hidden": hidden,
                "mixed": mixed,
                "second": second,
                "up_acts": up_acts,
                "activated": activated,
            }
        )
        held.append((gates_full, out_full, up_full, down_full))
        stream = mixed + dot_plain(activated, down_full)
    grad = cotangent.astype(jnp.float32)
    gate_parts = []
    mlp_parts = []
    for layer_no in reversed(range(layer_count)):
        kept = saved[layer_no]
        gates_full, out_full, up_full, down_full = held[layer_no]
        grad_low = grad.astype(jnp.bfloat16)
        act_grad = dot_last(grad_low, down_full)
        down_grad = dot_first(kept["activated"], grad_low)
        unused_gelu, gelu_back = jax.vjp(jax.nn.gelu, kept["up_acts"])
        up_low = gelu_back(act_grad)[0].astype(jnp.bfloat16)
        up_grad = dot_first(kept["second"], up_low)
        second_grad = dot_last(up_low, up_full)
        unused_norm, norm_back = jax.vjp(rms_scale, kept["mixed"], kept["gain_second"])
        mixed_part, gain_two_grad = norm_back(second_grad)
        mixed_grad = grad + mixed_part
        mixed_low = mixed_grad.astype(jnp.bfloat16)
        mixed_all = lax.all_gather(mixed_low, "mp", axis=0, tiled=True)
        state_grad = dot_last(mixed_all, out_full)
        out_grad = dot_first(kept["hidden"], mixed_all)
        decay = kept["decay"]
        shifted = jnp.concatenate([decay[1:], jnp.ones((1, width), jnp.float32)], axis=0)
        back_products, back_partial = lax.associative_scan(
            link, (shifted[::-1], state_grad[::-1]), axis=0
        )
        adjoint = back_partial[::-1]
        previous = jnp.concatenate(
            [jnp.zeros((1, width), jnp.float32), kept["states"][:-1]], axis=0
        )
        unused_gate, gate_back = jax.vjp(partial(gate_terms, starts=starts), kept["pre"])
        pre_low = gate_back((adjoint * previous, adjoint))[0].astype(jnp.bfloat16)
        bias_grad = jnp.sum(pre_low.astype(jnp.float32), axis=1)
        gate_grad = jnp.einsum(
            "td,ktf->kdf", kept["normed"], pre_low, preferred_element_type=jnp.float32
        )
        normed_part = jnp.einsum(
            "ktf,kdf->td", pre_low, gates_full, preferred_element_type=jnp.float32
        )
        normed_grad = lax.psum_scatter(
            normed_part.astype(jnp.bfloat16), "mp", scatter_dimension=0, tiled=True
        ).astype(jnp.float32)
        unused_first, first_back = jax.vjp(rms_scale, kept["stream"], kept["gain_first"])
        stream_part, gain_one_grad = first_back(normed_grad)
        grad = mixed_grad + stream_part
        gate_parts.append(
            (
                sum_at_owner(gate_grad.astype(jnp.bfloat16), "dp", 1),
                sum_at_owner(bias_grad.astype(jnp.bfloat16), "dp", 1),
                sum_at_owner(out_grad.astype(jnp.bfloat16), "dp", 1),
            )
        )
        mlp_parts.append(
            (
                lax.psum_scatter(up_grad, ("dp", "mp"), scatter_dimension=0, tiled=True),
                lax.psum_scatter(down_grad, ("dp", "mp"), scatter_dimension=0, tiled=True),
                lax.psum_scatter(gain_one_grad, ("dp", "mp"), scatter_dimension=0, tiled=True),
                lax.psum_scatter(gain_two_grad, ("dp", "mp"), scatter_dimension=0, tiled=True),
            )
        )
    gate_parts = gate_parts[::-1]
    mlp_parts = mlp_parts[::-1]
    gate_stack = tuple((jnp.stack([entry[member] for entry in gate_parts]) for member in range(3)))
    mlp_stack = tuple((jnp.stack([entry[member] for entry in mlp_parts]) for member in range(4)))
    return (
        stream.astype(jnp.bfloat16),
        grad,
        gate_stack[0],
        gate_stack[1],
        gate_stack[2],
        mlp_stack[2],
        mlp_stack[3],
        mlp_stack[0],
        mlp_stack[1],
    )


def body(inputs, gate_weight, gate_bias, out_weight, gain_one, gain_two, up_weight, down_weight, cotangent):
    shards = (gate_weight, gate_bias, out_weight, gain_one, gain_two, up_weight, down_weight)
    if not fits(inputs, *shards):
        return general_body(inputs, *shards, cotangent)
    out, *kept = forward(inputs, *shards)
    return settle(out, *backward(cotangent, kept))


def solution(mesh):
    placed = (
        P(("dp", "mp"), None),
        P(None, None, "dp", "mp"),
        P(None, None, ("mp", "dp")),
        P(None, "mp", "dp"),
        P(None, ("dp", "mp")),
        P(None, ("dp", "mp")),
        P(None, ("dp", "mp"), None),
        P(None, ("dp", "mp"), None),
        P(("dp", "mp"), None),
    )
    return jax.shard_map(
        body,
        mesh=mesh,
        in_specs=placed,
        out_specs=(
            P(("dp", "mp"), None),
            P(("dp", "mp"), None),
            P(None, None, "dp", "mp"),
            P(None, None, ("mp", "dp")),
            P(None, "mp", "dp"),
            P(None, ("dp", "mp")),
            P(None, ("dp", "mp")),
            P(None, ("dp", "mp"), None),
            P(None, ("dp", "mp"), None),
        ),
        check_vma=False,
    )
```

```python
from functools import partial

import jax
import jax.numpy as jnp
from jax import lax
from jax.experimental import pallas as pl
from jax.experimental.pallas import tpu as pltpu
from jax.sharding import PartitionSpec as P

LENGTH = 1024


eps = 1e-06


def cut_along(x, dim, size):
    shape = x.shape
    blocks = x.reshape(*shape[:dim], size, shape[dim] // size, *shape[dim + 1 :])
    return jnp.moveaxis(blocks, dim, 0)


def sum_at_owner(x, axis, dim):
    size = lax.axis_size(axis)
    blocks = lax.all_to_all(cut_along(x, dim, size), axis, 0, 0, tiled=True)
    return jnp.sum(blocks.astype(jnp.float32), axis=0)


def rms_scale(values, gain):
    return values * lax.rsqrt(jnp.mean(values * values, axis=-1, keepdims=True) + eps) * gain


def link(earlier, later):
    return (earlier[0] * later[0], later[0] * earlier[1] + later[1])


def gate_terms(pre_acts, starts):
    sig_forget = jax.nn.sigmoid(pre_acts[0])
    sig_input = jax.nn.sigmoid(pre_acts[1])
    total = sig_forget + sig_input
    decay = jnp.where(starts, 0.0, sig_forget / total)
    return (decay, sig_input / total * pre_acts[2])


def dot_plain(left, right):
    return jnp.dot(left, right, preferred_element_type=jnp.float32)


def dot_first(left, right):
    return lax.dot_general(
        left, right, (((0,), (0,)), ((), ())), preferred_element_type=jnp.float32
    )


def dot_last(left, right):
    return lax.dot_general(
        left, right, (((1,), (1,)), ((), ())), preferred_element_type=jnp.float32
    )


GATHER_PLAN = (
    (0, 5, 10, 15, 1, 20, 6, 25, 2, 11, 30, 45, 7, 3, 16, 35, 12, 4),
    (),
    (46,),
    (21, 40),
    (8, 26, 50, 17, 9, 31, 55, 13, 47, 22, 36, 60, 27, 14, 41, 65, 18, 32, 51, 70, 19),
    (),
    (56, 75, 37, 23),
    (),
    (42, 28),
    (24,),
    (33,),
    (52, 29),
    (),
    (),
    (57, 48, 34),
    (),
    (61, 80, 38),
    (),
    (43, 66),
    (49, 39, 53, 71, 44),
    (58,),
    (76, 62, 54),
    (67, 81, 72, 59),
    (),
    (77,),
    (),
    (63,),
    (68, 82, 64),
    (69,),
    (),
    (73,),
    (),
    (78,),
    (83, 74),
    (),
    (),
    (79,),
    (84,),
    (),
)
SCATTER_PLAN = (
    (),
    (),
    (),
    (),
    (0,),
    (),
    (),
    (),
    (5,),
    (10, 15),
    (1,),
    (20,),
    (),
    (),
    (6,),
    (11,),
    (16,),
    (21, 2),
    (),
    (25, 7),
    (30,),
    (35,),
    (12,),
    (26, 17, 31),
    (36, 22),
    (3,),
    (8,),
    (13,),
    (),
    (40,),
    (27,),
    (18, 4),
    (),
    (45, 32, 9),
    (50, 55, 41),
    (),
    (37, 14, 23, 46, 28, 19, 51, 33, 56, 42, 24, 38, 29, 47, 34, 52, 39),
    (60,),
    (),
    (57,),
    (43,),
    (48,),
    (),
    (61, 53),
    (58,),
    (65, 44),
    (70,),
    (75,),
    (62, 49),
    (66, 54),
    (71, 76, 59),
    (80,),
    (63, 67, 81, 72, 64, 77, 68, 82, 73, 78, 83, 69, 74, 79, 84),
)


ALL = slice(None)
MESH = pl.DeviceIdType.MESH
BF = jnp.bfloat16
F32 = jnp.float32
SHIFT = 0.25
LOG_SHIFT = -1.3862943611198906
TOP = 87.0
GELU_A = 0.7978845608028654
GELU_B = 0.044715
ROWS = 256
STEPS = ROWS // 8


def first_of(mp, rows):
    return lax.div(jnp.minimum(lax.rem(mp * (LENGTH - rows), LENGTH), rows), ROWS)


Z_LAST = (("gate", 1, 0),)


def place():
    dp = lax.axis_index("dp")
    mp = lax.axis_index("mp")
    return (lax.div(dp, 2), lax.rem(dp, 2), lax.div(mp, 2), lax.rem(mp, 2))


def device(z, x, y, c):
    return (z * 2 + x, y * 2 + c)


def greet(wait=True):
    z, x, y, c = place()
    partners = [device(lax.rem(z + k, 4), x, y, c) for k in (1, 2, 3)]
    partners += [device(z, 1 - x, y, c), device(z, x, 1 - y, c)]
    partners += [device(z, x, y, 1 - c), device(z, x, 1 - y, 1 - c)]
    barrier = pltpu.get_barrier_semaphore()
    for partner in partners:
        pl.semaphore_signal(barrier, inc=1, device_id=partner, device_id_type=MESH)
    if wait:
        greeted()


def greeted():
    pl.semaphore_wait(pltpu.get_barrier_semaphore(), 7)


class Gather:
    def __init__(self, bufs, own, items, plan, send, recv):
        self.bufs = bufs
        self.own = own
        self.items = items
        self.send = send
        self.recv = recv
        self.at = place()
        self.sent = []
        self.plan = [list(row) for row in plan]

    def view(self, item, z, x, y, c, h):
        kind, l, part = item
        w4, up, dn, vec = self.bufs
        if kind == "vec":
            return vec.at[z, x, y, c, h]
        if kind == "gate":
            return w4.at[l, y, c, part, z, x, h]
        if kind == "up":
            return up.at[l, part, h, z, x, y, c]
        return dn.at[l, z, x, y, c, part, h]

    def go(self, n, slot, ref, target):
        cp = pltpu.make_async_remote_copy(
            src_ref=ref,
            dst_ref=ref,
            send_sem=self.send.at[n, slot],
            recv_sem=self.recv.at[n, slot],
            device_id=target,
            device_id_type=MESH,
        )
        cp.start()
        self.sent.append(cp)

    def landed(self, n, slot, ref, source):
        pltpu.make_async_remote_copy(
            src_ref=ref,
            dst_ref=ref,
            send_sem=self.send.at[n, slot],
            recv_sem=self.recv.at[n, slot],
            device_id=source,
            device_id_type=MESH,
        ).wait_recv()

    def stage(self, step, n, item):
        z, x, y, c = self.at
        v = lambda *where: self.view(item, *where)
        to_x = device(z, 1 - x, y, c)
        to_y = device(z, x, 1 - y, c)
        to_c = device(z, x, y, 1 - c)
        if step == 0:
            for cp in self.own.pop(item):
                cp.wait()
        if item in Z_LAST:
            self.stage_z_last(step, n, v, to_x, to_y, to_c)
        elif step == 0:
            for k in (1, 2, 3):
                self.go(n, k - 1, v(z, x, y, c, ALL), device(lax.rem(z + k, 4), x, y, c))
        elif step == 1:
            for k in (1, 2, 3):
                source = lax.rem(z + 4 - k, 4)
                self.landed(n, k - 1, v(source, x, y, c, ALL), device(source, x, y, c))
            self.go(n, 3, v(ALL, x, y, c, 0), to_x)
            self.go(n, 4, v(ALL, x, y, c, 1), to_y)
            self.go(n, 7, v(ALL, x, y, c, ALL), to_c)
        elif step == 2:
            self.landed(n, 3, v(ALL, 1 - x, y, c, 0), to_x)
            self.go(n, 5, v(ALL, ALL, y, c, 0), to_y)
            self.landed(n, 4, v(ALL, x, 1 - y, c, 1), to_y)
            self.go(n, 6, v(ALL, x, ALL, c, 1), to_x)
            self.go(n, 8, v(ALL, 1 - x, y, c, 0), to_c)
            self.go(n, 9, v(ALL, x, 1 - y, c, 1), to_c)
        elif step == 3:
            self.landed(n, 5, v(ALL, ALL, 1 - y, c, 0), to_y)
            self.go(n, 10, v(ALL, ALL, 1 - y, c, 0), to_c)
            self.landed(n, 6, v(ALL, 1 - x, ALL, c, 1), to_x)
            self.go(n, 11, v(ALL, 1 - x, ALL, c, 1), to_c)
        else:
            self.landed(n, 7, v(ALL, x, y, 1 - c, ALL), to_c)
            self.landed(n, 8, v(ALL, 1 - x, y, 1 - c, 0), to_c)
            self.landed(n, 9, v(ALL, x, 1 - y, 1 - c, 1), to_c)
            self.landed(n, 10, v(ALL, ALL, 1 - y, 1 - c, 0), to_c)
            self.landed(n, 11, v(ALL, 1 - x, ALL, 1 - c, 1), to_c)

    def stage_z_last(self, step, n, v, to_x, to_y, to_c):
        z, x, y, c = self.at
        if step == 0:
            self.go(n, 3, v(z, x, y, c, 0), to_x)
            self.go(n, 4, v(z, x, y, c, 1), to_y)
        elif step == 1:
            self.landed(n, 3, v(z, 1 - x, y, c, 0), to_x)
            self.go(n, 5, v(z, ALL, y, c, 0), to_y)
            self.landed(n, 4, v(z, x, 1 - y, c, 1), to_y)
            self.go(n, 6, v(z, x, ALL, c, 1), to_x)
        elif step == 2:
            self.landed(n, 5, v(z, ALL, 1 - y, c, 0), to_y)
            self.landed(n, 6, v(z, 1 - x, ALL, c, 1), to_x)
            for k in (1, 2, 3):
                self.go(n, k - 1, v(z, ALL, ALL, c, ALL), device(lax.rem(z + k, 4), x, y, c))
            self.go(n, 7, v(z, ALL, ALL, c, ALL), to_c)
        elif step == 3:
            for k in (1, 2, 3):
                source = lax.rem(z + 4 - k, 4)
                self.landed(n, k - 1, v(source, ALL, ALL, c, ALL), device(source, x, y, c))
                self.go(n, 7 + k, v(source, ALL, ALL, c, ALL), to_c)
        else:
            self.landed(n, 7, v(z, ALL, ALL, 1 - c, ALL), to_c)
            for k in (1, 2, 3):
                self.landed(n, 7 + k, v(lax.rem(z + 4 - k, 4), ALL, ALL, 1 - c, ALL), to_c)

    def go_on(self):
        for code in self.plan.pop(0):
            n, step = divmod(code, 5)
            self.stage(step, n, self.items[n])

    def finish(self):
        for cp in self.sent:
            cp.wait_send()


def dot(a, b):
    return jnp.dot(a, b, preferred_element_type=F32)


def dot_nt(a, b):
    return lax.dot_general(a, b, (((1,), (1,)), ((), ())), preferred_element_type=F32)


def dot_tn(a, b):
    return lax.dot_general(a, b, (((0,), (0,)), ((), ())), preferred_element_type=F32)


def spread(vec, l, first, size, total, per_mp):
    rows = vec[:, :, :, :, l].reshape(256, 128).astype(BF)
    j = lax.broadcasted_iota(jnp.int32, (128, total), 0)
    d = lax.broadcasted_iota(jnp.int32, (128, total), 1)
    pick = jnp.where(j == first + lax.rem(d, size), 1.0, 0.0).astype(BF)
    wide = dot(rows, pick)
    r = lax.div(lax.broadcasted_iota(jnp.int32, (256, total), 0), 8)
    d = lax.broadcasted_iota(jnp.int32, (256, total), 1)
    if per_mp:
        owner = lax.div(lax.rem(d, total // 4), size) * 4 + lax.div(d, total // 4)
    else:
        owner = lax.div(d, size)
    return jnp.sum(jnp.where(r == owner, wide, 0.0), axis=0, keepdims=True)


def combine(a, b, row, sign):
    for s in (1, 2, 4):
        keep = (row >= s) if sign > 0 else (row < 8 - s)
        by = s if sign > 0 else 8 - s
        am = jnp.where(keep, a, 0.0)
        b = b + am * pltpu.roll(b, by, 0)
        if s < 4:
            a = jnp.where(keep, a * pltpu.roll(a, by, 0), a)
        else:
            a = jnp.where(keep, a * pltpu.roll(a, by, 0), a)
    return a, b


def into_steps(v, turn, i):
    for n in range(4):
        turn[n, pl.ds(i * ROWS, ROWS), :] = v[:, n * 128 : n * 128 + 128]
    parts = []
    for n in range(4):
        rows = [turn[n, pl.ds(i * ROWS + j, 8, stride=STEPS), :] for j in range(STEPS)]
        parts.append(jnp.concatenate(rows, axis=0))
    return jnp.concatenate(parts, axis=1)


def unturn(v, turn, i):
    for n in range(4):
        for j in range(STEPS):
            turn[n, pl.ds(i * ROWS + j, 8, stride=STEPS), :] = v[j * 8 : j * 8 + 8, n * 128 : n * 128 + 128]
    return jnp.concatenate([turn[n, pl.ds(i * ROWS, ROWS), :] for n in range(4)], axis=1)


def fwd_kernel(
    x_in, gate_in, out_in, up_in, down_in, gain_one_in, gain_two_in, bias_in,
    out_hbm, w4_hbm, up_hbm, dn_hbm, gain_hbm, stream_hbm, mixed_hbm, keep_hbm, q_hbm, hid_hbm, ff_hbm, turned_hbm,
    w4, up, dn, vec, normed, stream, mixed, turned, turn, ends, enter, keep, states, c3, hid, ff, bias, gain, c_out, c_in,
    ag_send, ag_recv, own_sem, spill_sem, carry_send, carry_recv,
):
    z, x, y, c = place()
    mp = y * 2 + c
    rows_all = normed.shape[0]
    chunks = rows_all // ROWS
    fill = []

    def local(src, dst, sem):
        cp = pltpu.make_async_copy(src, dst, sem)
        cp.start()
        return cp

    own = {}
    n_own = 0

    def add_own(key, src, dst):
        nonlocal n_own
        own.setdefault(key, []).append(local(src, dst, own_sem.at[n_own]))
        n_own += 1

    x_copy = local(x_in, normed, own_sem.at[48])
    own[("vec", 0, 0)] = []
    vec[z, x, y, c] = jnp.zeros((2, 8, 128), F32)
    for l in range(2):
        ours = [gain_one_in[l : l + 1, :], gain_two_in[l : l + 1, :]] + [bias_in[k, l : l + 1, :] for k in range(3)]
        vec[z, x, y, c, l, 0:1, :] = jnp.concatenate([v.astype(F32) for v in ours], axis=1)
    for l in range(2):
        for k in range(3):
            add_own(("gate", l, k), gate_in.at[l, k], w4.at[l, y, c, k, z, x])
        add_own(("gate", l, 3), out_in.at[l], w4.at[l, y, c, 3, z, x])
        for pair in range(2):
            for h in range(2):
                columns = pl.ds((pair * 2 + h) * 512, 512)
                add_own(("up", l, pair), up_in.at[l, :, columns], up.at[l, pair, h, z, x, y, c])
            add_own(("down", l, pair), down_in.at[l, pair], dn.at[l, z, x, y, c, pair])
    greet()
    items = [("vec", 0, 0)]
    for l in range(2):
        items += [("gate", l, k) for k in range(4)]
        items += [(kind, l, pair) for kind in ("up", "down") for pair in range(2)]
    gather = Gather((w4, up, dn, vec), own, items, GATHER_PLAN, ag_send, ag_recv)
    go_on = gather.go_on

    n_spill = 0
    spills = {}

    def spill(key, src, dst):
        nonlocal n_spill
        spills[key] = local(src, dst, spill_sem.at[n_spill])
        n_spill += 1

    def settle(key):
        if key in spills:
            spills.pop(key).wait()


    def rms(src, dst, g):
        @pl.loop(0, chunks)
        def _(i):
            r = pl.ds(pl.multiple_of(i * ROWS, ROWS), ROWS)
            v = src[r, :]
            scale = lax.rsqrt(jnp.mean(v * v, axis=-1, keepdims=True) + eps)
            n = (v * scale * g).astype(BF)
            dst[r, :] = n
            turned[0, :, r] = n.T

    def gate_panel(l, p):
        w = [w4[l, p // 2, p % 2, k].reshape(512, 256) for k in range(3)]
        bs = [bias[l, k : k + 1, p * 256 : (p + 1) * 256] for k in range(3)]

        @pl.loop(0, chunks)
        def _(i):
            r = pl.ds(pl.multiple_of(i * ROWS, ROWS), ROWS)
            n = normed[r, :]
            f, inp, cand = [dot(n, w[k]) + bs[k] for k in range(3)]
            e_f = jnp.exp(jnp.minimum(-f, TOP) + LOG_SHIFT)
            e_i = jnp.exp(jnp.minimum(-inp, TOP) + LOG_SHIFT)
            a_f = e_f + SHIFT
            a_i = e_i + SHIFT
            total = a_f + a_i
            inv = pl.reciprocal(total, approx=True)
            inv = inv * (2.0 - total * inv)
            share = a_f * inv
            decay = a_i * inv
            drive = share * cand
            keep[p, r, :] = share
            c3[p, 0, r, :] = (decay * (e_f * inv)).astype(BF)
            c3[p, 1, r, :] = (share * (e_i * inv)).astype(BF)
            c3[p, 2, r, :] = cand.astype(BF)
            s = drive[0:8]
            a = decay[0:8]
            local_states = [s]
            for j in range(1, STEPS):
                t = slice(j * 8, j * 8 + 8)
                s = decay[t] * s + drive[t]
                a = a * decay[t]
                local_states.append(s)
            states[p, r, :] = jnp.concatenate(local_states, axis=0)
            columns = slice(p * 256, p * 256 + 256)
            ends[0, i, :, columns] = a
            ends[1, i, :, columns] = s

    row = lax.broadcasted_iota(jnp.int32, (8, 1024), 0)
    first_chunk = first_of(mp, rows_all)

    def carries(entering):
        for i in range(chunks):
            c0 = jnp.where(first_chunk == i, 0.0, entering)
            a, s = combine(ends[0, i], ends[1, i], row, 1)
            enter[i] = jnp.where(row == 0, c0, pltpu.roll(a, 1, 0) * c0 + pltpu.roll(s, 1, 0))
            entering = jnp.broadcast_to(a[7:8] * c0[7:8] + s[7:8], (8, 1024))
        return entering

    def carry_copy(l, there):
        return pltpu.make_async_remote_copy(
            src_ref=c_out.at[l],
            dst_ref=c_in.at[l],
            send_sem=carry_send.at[l],
            recv_sem=carry_recv.at[l],
            device_id=device(z, x, lax.div(there, 2), lax.rem(there, 2)),
            device_id_type=MESH,
        )

    def carry_out(l):
        c_out[l] = carries(jnp.zeros((8, 1024), F32))

        @pl.when(mp < 3)
        def _():
            carry_copy(l, jnp.minimum(mp + 1, 3)).start()

    def carry_into(l):
        @pl.when(mp > 0)
        def _():
            carry_copy(l, jnp.maximum(mp - 1, 0)).wait_recv()
            carries(c_in[l])

        @pl.when(mp < 3)
        def _():
            carry_copy(l, jnp.minimum(mp + 1, 3)).wait_send()

    def project(l):
        g = gain[l, 1:2, :]
        w = [w4[l, p // 2, p % 2, 3].reshape(512, 256) for p in range(4)]

        @pl.loop(0, chunks)
        def _(i):
            r = pl.ds(pl.multiple_of(i * ROWS, ROWS), ROWS)
            v = stream[r, :]
            for p in range(4):
                share = keep[p, r, :]
                s_local = states[p, r, :]
                cand = c3[p, 2, r, :].astype(F32)
                enters = enter[i, :, p * 256 : p * 256 + 256]
                before = enters
                weight = enters
                now, gap = [], []
                for j in range(STEPS):
                    t = slice(j * 8, j * 8 + 8)
                    weight = weight - share[t] * weight
                    s = s_local[t] + weight
                    gap.append(before - cand[t])
                    now.append(s)
                    before = s
                gap = jnp.concatenate(gap, axis=0)
                h = jnp.concatenate(now, axis=0).astype(BF)
                hid[p, r, :] = h
                c3[p, 0, r, :] = (gap * c3[p, 0, r, :].astype(F32)).astype(BF)
                c3[p, 1, r, :] = (-gap * c3[p, 1, r, :].astype(F32)).astype(BF)
                v = v + dot_nt(h, w[p])
            mixed[r, :] = v
            scale = lax.rsqrt(jnp.mean(v * v, axis=-1, keepdims=True) + eps)
            n = (v * scale * g).astype(BF)
            normed[r, :] = n
            turned[1, :, r] = n.T

    def feed_up(l, q):
        w_up = up[l, q // 2, q % 2].reshape(512, 512)

        @pl.loop(0, chunks)
        def _(i):
            r = pl.ds(pl.multiple_of(i * ROWS, ROWS), ROWS)
            u = dot(normed[r, :], w_up)
            sq = u * u
            t = jnp.tanh(u * (GELU_A + (GELU_A * GELU_B) * sq))
            gate = 0.5 + 0.5 * t
            act = (u * gate).astype(BF)
            slope = gate + (0.5 * u) * (1.0 - t * t) * (GELU_A + (3.0 * GELU_A * GELU_B) * sq)
            for half in range(2):
                side = slice(half * 256, half * 256 + 256)
                ff[q, half, r, :] = slope[:, side].astype(BF)
                ff[q, 2 + half, r, :] = act[:, side]

    def feed_down(l):
        w_down = dn[l].reshape(2048, 512)

        @pl.loop(0, chunks)
        def _(i):
            r = pl.ds(pl.multiple_of(i * ROWS, ROWS), ROWS)
            acts = [ff[q, 2 + half, r, :] for q in range(4) for half in range(2)]
            v = mixed[r, :] + dot(jnp.concatenate(acts, axis=1), w_down)
            if l == 0:
                stream[r, :] = v
            else:
                normed[r, :] = unturn(v, turn, i).astype(BF)

    go_on()
    for l in range(2):
        gain[l, 0:1, :] = spread(vec, l, 0, 16, 512, False)
        gain[l, 1:2, :] = spread(vec, l, 16, 16, 512, False)
        for k in range(3):
            bias[l, k : k + 1, :] = spread(vec, l, 32 + 32 * k, 32, 1024, True)
        go_on()
    x_copy.wait()

    @pl.loop(0, chunks)
    def _(i):
        r = pl.ds(pl.multiple_of(i * ROWS, ROWS), ROWS)
        stream[r, :] = into_steps(normed[r, :].astype(F32), turn, i)

    spill("gain", gain, gain_hbm)
    for l in range(2):
        settle(("first", 0))
        rms(stream, normed, gain[l, 0:1, :])
        spill(("first", l), turned.at[0], turned_hbm.at[l, 0])
        settle(("keep", 0))
        settle(("q", 0))
        spill(("stream", l), stream, stream_hbm.at[l])
        go_on()
        go_on()
        for p in range(4):
            gate_panel(l, p)
            go_on()
        spill(("keep", l), keep, keep_hbm.at[l])
        carry_out(l)
        settle(("hid", 0))
        settle(("mixed", 0))
        go_on()
        carry_into(l)
        settle(("second", 0))
        project(l)
        spill(("second", l), turned.at[1], turned_hbm.at[l, 1])
        spill(("q", l), c3.at[:, pl.ds(0, 2)], q_hbm.at[l])
        spill(("hid", l), hid, hid_hbm.at[l])
        spill(("w4", l), w4.at[l], w4_hbm.at[l])
        spill(("mixed", l), mixed, mixed_hbm.at[l])
        go_on()
        for q in range(4):
            settle(("ff", 0, q))
            go_on()
            feed_up(l, q)
            spill(("ff", l, q), ff.at[q], ff_hbm.at[l, q])
            go_on()
        spill(("up", l), up.at[l], up_hbm.at[l])
        settle(("stream", l))
        go_on()
        feed_down(l)
        spill(("dn", l), dn.at[l], dn_hbm.at[l])
        go_on()
    spill("result", normed, out_hbm)
    for key in list(spills):
        settle(key)
    gather.finish()


def forward(x, gate_weight, gate_bias, out_weight, gain_one, gain_two, up_weight, down_weight):
    rows = x.shape[0]
    any_space = pl.BlockSpec(memory_space=pl.ANY)
    args = (
        x,
        gate_weight.reshape(2, 3, 2, 32, 256),
        out_weight.transpose(0, 2, 1).reshape(2, 2, 32, 256),
        up_weight,
        down_weight.reshape(2, 2, 2, 16, 512),
        gain_one,
        gain_two,
        gate_bias.transpose(1, 0, 2),
    )
    s = jax.ShapeDtypeStruct
    w4 = (2, 2, 2, 4, 4, 2, 2, 32, 256)
    up = (2, 2, 2, 4, 2, 2, 2, 16, 512)
    dn = (2, 4, 2, 2, 2, 2, 2, 16, 512)
    dma = pltpu.SemaphoreType.DMA
    return pl.pallas_call(
        fwd_kernel,
        name="forward",
        out_shape=(
            s((rows, 512), BF), s(w4, BF), s(up, BF), s(dn, BF), s((2, 8, 512), F32), s((2, rows, 512), F32),
            s((2, rows, 512), F32), s((2, 4, rows, 256), F32), s((2, 4, 2, rows, 256), BF),
            s((2, 4, rows, 256), BF), s((2, 4, 4, rows, 256), BF), s((2, 2, 512, rows), BF),
        ),
        in_specs=[any_space] * 5 + [pl.BlockSpec(memory_space=pltpu.VMEM)] * 3,
        out_specs=(any_space,) * 12,
        scratch_shapes=[
            pltpu.VMEM(w4, BF), pltpu.VMEM(up, BF), pltpu.VMEM(dn, BF), pltpu.VMEM((4, 2, 2, 2, 2, 8, 128), F32),
            pltpu.VMEM((rows, 512), BF), pltpu.VMEM((rows, 512), F32), pltpu.VMEM((rows, 512), F32), pltpu.VMEM((2, 512, rows), BF), pltpu.VMEM((4, rows, 128), F32),
            pltpu.VMEM((2, 3, 8, 1024), F32), pltpu.VMEM((3, 8, 1024), F32),
            pltpu.VMEM((4, rows, 256), F32), pltpu.VMEM((4, rows, 256), F32), pltpu.VMEM((4, 3, rows, 256), BF),
            pltpu.VMEM((4, rows, 256), BF), pltpu.VMEM((4, 4, rows, 256), BF),
            pltpu.VMEM((2, 8, 1024), F32), pltpu.VMEM((2, 8, 512), F32),
            pltpu.VMEM((2, 8, 1024), F32), pltpu.VMEM((2, 8, 1024), F32),
            dma((17, 12)), dma((17, 12)), dma((49,)), dma((32,)), dma((2,)), dma((2,)),
        ],
        compiler_params=pltpu.CompilerParams(
            collective_id=0, has_side_effects=True, vmem_limit_bytes=62 * 2**20
        ),
    )(*args)


class Scatter:
    def __init__(self, grads, landing, plan, send, recv, give):
        self.grads = grads
        self.landing = landing
        self.send = send
        self.recv = recv
        self.give = give
        self.at = place()
        self.sent = {}
        self.items = []
        self.plan = [list(row) for row in plan]

    def own(self, item, z, x, y, c, h):
        kind, l, part = item
        w4, up, dn, vec = self.grads
        if kind == "vec":
            return vec.at[z, x, y, c, h]
        if kind == "gate":
            return w4.at[y, c, part, z, x, h]
        if kind == "up":
            return up.at[l, part, h, z, x, y, c]
        return dn.at[l, z, x, y, c, part, h]

    def land(self, item, stage, *where):
        kind, l, part = item
        ref = self.landing[("gate", "up", "down", "vec").index(kind)][stage]
        where = where if kind == "vec" else (l, part, *where)
        return ref.at[where] if where else ref

    def copy(self, n, slot, src, dst, target):
        return pltpu.make_async_remote_copy(
            src_ref=src,
            dst_ref=dst,
            send_sem=self.send.at[n, slot],
            recv_sem=self.recv.at[n, slot],
            device_id=target,
            device_id_type=MESH,
        )

    def go(self, n, slot, src, dst, target):
        cp = self.copy(n, slot, src, dst, target)
        cp.start()
        self.sent.setdefault(n, []).append(cp)

    def landed(self, n, slot, dst, source):
        self.copy(n, slot, dst, dst, source).wait_recv()

    def add(self, item, stage):
        z, x, y, c = self.at
        kind = item[0]

        def plus(there, *where):
            there[...] = there[...] + self.land(item, stage, *where)[...]

        @pl.loop(0, 4)
        def _(n):
            if stage == 0:
                for i in range(2):
                    for j in range(2):
                        for h in range(2):
                            if kind == "gate":
                                plus(self.own(item, n, j, i, c, h), i, n, j, h)
                            elif kind == "up":
                                plus(self.own(item, n, i, j, c, h), h, n, i, j)
                            else:
                                plus(self.own(item, n, i, j, c, h), n, i, j, h)
            elif stage == 1:
                for i in range(2):
                    plus(self.own(item, n, i, y, c, 0), n, i)
            elif stage == 2:
                for i in range(2):
                    plus(self.own(item, n, x, i, c, 1), *((i, n) if kind == "gate" else (n, i)))
            else:
                for h in range(2):
                    plus(self.own(item, n, x, y, c, h), h, n)

    def total(self, item, h):
        z, x, y, c = self.at
        v = self.own(item, z, x, y, c, h)[...].astype(F32)
        for j in range(3):
            v = v + self.land(item, 4, j, h)[...].astype(F32)
        return v

    def stage(self, step, n, item):
        z, x, y, c = self.at
        v = lambda *where: self.own(item, *where)
        to_x = device(z, 1 - x, y, c)
        to_y = device(z, x, 1 - y, c)
        to_c = device(z, x, y, 1 - c)
        land = lambda *w: self.land(item, *w)
        if step == 0:
            self.go(n, 0, v(ALL, ALL, ALL, 1 - c, ALL), land(0), to_c)
        elif step == 1:
            self.landed(n, 0, land(0), to_c)
            self.add(item, 0)
            self.go(n, 1, v(ALL, ALL, 1 - y, c, 0), land(1), to_y)
            self.go(n, 2, v(ALL, 1 - x, ALL, c, 1), land(2), to_x)
        elif step == 2:
            self.landed(n, 1, land(1), to_y)
            self.add(item, 1)
            self.go(n, 3, v(ALL, 1 - x, y, c, 0), land(3, 0), to_x)
            self.landed(n, 2, land(2), to_x)
            self.add(item, 2)
            self.go(n, 4, v(ALL, x, 1 - y, c, 1), land(3, 1), to_y)
        elif step == 3:
            self.landed(n, 3, land(3, 0), to_x)
            self.landed(n, 4, land(3, 1), to_y)
            self.add(item, 3)
            for k in (1, 2, 3):
                there = lax.rem(z + k, 4)
                self.go(n, 4 + k, v(there, x, y, c, ALL), land(4, k - 1), device(there, x, y, c))
        else:
            for k in (1, 2, 3):
                source = lax.rem(z + 4 - k, 4)
                self.landed(n, 4 + k, land(4, k - 1), device(source, x, y, c))
            self.give(item, self)

    def go_on(self):
        for code in self.plan.pop(0):
            n, step = divmod(code, 5)
            self.stage(step, n, self.items[n])

    def settle(self, numbers):
        for n in numbers:
            for cp in self.sent.pop(n):
                cp.wait_send()


def spread_back(g, first, size, total, per_mp):
    r = lax.broadcasted_iota(jnp.int32, (32, total), 0)
    d = lax.broadcasted_iota(jnp.int32, (32, total), 1)
    if per_mp:
        owner = lax.div(lax.rem(d, total // 4), size) * 4 + lax.div(d, total // 4)
    else:
        owner = lax.div(d, size)
    rows = jnp.where(r == owner, g, 0.0)
    d = lax.broadcasted_iota(jnp.int32, (total, 128), 0)
    j = lax.broadcasted_iota(jnp.int32, (total, 128), 1)
    pick = jnp.where(j == first + lax.rem(d, size), 1.0, 0.0).astype(BF)
    high = rows.astype(BF)
    rest = rows - high.astype(F32)
    middle = rest.astype(BF)
    low = (rest - middle.astype(F32)).astype(BF)
    return dot(high, pick) + dot(middle, pick) + dot(low, pick)


def bwd_kernel(
    ct_in, w4_in, up_in, dn_in, gain_in, stream_in, mixed_in, keep_in, q_in, hid_in, ff_in, turned_in,
    grad_hbm, gate_hbm, out_hbm, up_hbm, down_hbm, vec_hbm,
    w4, up, dn, gain, keep, pre, mixed, ff, grad, acc, low, low_t, act_t, up_low, sg, c_out, c_in,
    ends, enter, gains, biases, g_w4, g_up, g_dn, g_vec,
    lw0, lw1, lw2, lw3, lw4, lu0, lu1, lu2, lu3, lu4, ld0, ld1, ld2, ld3, ld4, lv0, lv1, lv2, lv3, lv4,
    f_w4, f_up, f_dn, f_vec,
    rs_send, rs_recv, load_sem, save_sem, carry_send, carry_recv,
):
    z, x, y, c = place()
    mp = y * 2 + c
    rows_all = low.shape[0]
    chunks = rows_all // ROWS
    loads = {}
    n_load = 0
    saves = []

    def load(key, src, dst):
        nonlocal n_load
        cp = pltpu.make_async_copy(src, dst, load_sem.at[n_load])
        cp.start()
        loads[key] = cp
        n_load += 1

    def ready(key):
        loads.pop(key).wait()

    def save(src, dst):
        cp = pltpu.make_async_copy(src, dst, save_sem.at[len(saves)])
        cp.start()
        saves.append(cp)

    def load_feed(l):
        load("dn", dn_in.at[l], dn)
        load("up", up_in.at[l], up)

    def load_chunk(l, q):
        load(("ff", q), ff_in.at[l, q], ff.at[q % 2])

    def load_gates(l):
        load("w4", w4_in.at[l], w4)
        load("keep", keep_in.at[l], keep)
        load("q", q_in.at[l], pre.at[:, pl.ds(0, 2)])

    load("ct", ct_in, low)
    load("gain", gain_in, gain)
    load_feed(1)
    load_chunk(1, 0)
    load("act_t", turned_in.at[1, 1], act_t.at[pl.ds(0, 512)])
    load("mixed", mixed_in.at[1], mixed)
    load_chunk(1, 1)
    load_gates(1)
    greet(wait=False)

    def give(item, scatter):
        kind, l, part = item
        if kind == "gate":
            for h in range(2):
                f_w4[l, part, h] = scatter.total(item, h)
            save(f_w4.at[l, part], gate_hbm.at[l, part] if part < 3 else out_hbm.at[l])
        elif kind == "up":
            for h in range(2):
                f_up[l, part, h] = scatter.total(item, h)
                save(f_up.at[l, part, h], up_hbm.at[l, :, pl.ds((part * 2 + h) * 512, 512)])
        elif kind == "down":
            for h in range(2):
                f_dn[l, part, h] = scatter.total(item, h)
            save(f_dn.at[l, part], down_hbm.at[l, part])
        else:
            for h in range(2):
                f_vec[h] = scatter.total(item, h)
            save(f_vec, vec_hbm)

    landing = (
        (lw0, lw1, lw2, lw3, lw4), (lu0, lu1, lu2, lu3, lu4), (ld0, ld1, ld2, ld3, ld4), (lv0, lv1, lv2, lv3, lv4),
    )
    scatter = Scatter((g_w4, g_up, g_dn, g_vec), landing, SCATTER_PLAN, rs_send, rs_recv, give)
    go_on = scatter.go_on

    def push(*item):
        scatter.items.append(item)

    def each(fn):
        @pl.loop(0, chunks)
        def _(i):
            fn(i, pl.ds(pl.multiple_of(i * ROWS, ROWS), ROWS))

    def feed(l, q):
        slot = q % 2
        w_down = dn[q].reshape(512, 512)
        w_up = up[q // 2, q % 2].reshape(512, 512)

        def part(i, r):
            act_grad = dot_nt(low[r, :], w_down)
            slope = jnp.concatenate([ff[slot, 0, r, :], ff[slot, 1, r, :]], axis=1).astype(F32)
            u = (act_grad * slope).astype(BF)
            up_low[r, :] = u
            back = dot_nt(u, w_up)
            acc[r, :] = back if q == 0 else acc[r, :] + back

        each(part)
        go_on()
        for half in range(2):
            g = dot(act_t[half * 256 : half * 256 + 256, :], up_low[...]).astype(BF)
            g_up[l, q // 2, q % 2, half * 2 : half * 2 + 2] = g.reshape(2, 2, 2, 2, 16, 512)
        for half in range(2):
            g = dot_tn(ff[slot, 2 + half], low[...]).astype(BF)
            g_dn[l, q, half] = g.reshape(2, 2, 2, 2, 16, 512)

    def rms_back(l, which, src, values_t):
        g = gain[l, which : which + 1, :]
        gains[l, which : which + 1, :] = jnp.zeros((1, 512), F32)

        def part(i, r):
            v = src[r, :]
            scale = lax.rsqrt(jnp.mean(v * v, axis=-1, keepdims=True) + eps)
            u = v * scale
            d = acc[r, :]
            gains[l, which : which + 1, :] += jnp.sum(d * u, axis=0, keepdims=True)
            dg = d * g
            new = grad[r, :] + scale * (dg - u * jnp.mean(dg * u, axis=-1, keepdims=True))
            grad[r, :] = new
            new = new.astype(BF)
            low[r, :] = new
            if values_t is not None:
                values_t[:, r] = new.T

        each(part)

    def out_back(p):
        g = dot(low_t[...], ff[0, p]).astype(BF)
        g_w4[p // 2, p % 2, 3] = g.reshape(4, 2, 2, 32, 256)

    def states_back(p):
        w = w4[p // 2, p % 2, 3].reshape(512, 256)

        def part(i, r):
            v = dot(low[r, :], w)
            share = keep[p, r, :]
            decay = 1.0 - share
            t = slice(ROWS - 8, ROWS)
            adjoint = v[t]
            parts = [adjoint]
            a = decay[t]
            passed = a * adjoint
            for j in range(STEPS - 2, -1, -1):
                t = slice(j * 8, j * 8 + 8)
                adjoint = v[t] + passed
                passed = decay[t] * adjoint
                a = a * decay[t]
                parts.append(adjoint)
            whole = jnp.concatenate(parts[::-1], axis=0)
            for n in range(2):
                sg[p * 2 + n, r, :] = whole[:, n * 128 : n * 128 + 128]
            columns = slice(p * 256, p * 256 + 256)
            ends[0, i, :, columns] = a
            ends[1, i, :, columns] = passed

        each(part)

    row = lax.broadcasted_iota(jnp.int32, (8, 1024), 0)
    first_chunk = first_of(mp, rows_all)

    def carries(entering):
        for i in range(chunks - 1, -1, -1):
            c0 = jnp.where(first_chunk == i + 1, 0.0, entering)
            a, v = combine(ends[0, i], ends[1, i], row, -1)
            enter[i] = jnp.where(row == 7, c0, pltpu.roll(a, 7, 0) * c0 + pltpu.roll(v, 7, 0))
            entering = jnp.broadcast_to(a[0:1] * c0[0:1] + v[0:1], (8, 1024))
        return entering

    def carry_copy(l, there):
        return pltpu.make_async_remote_copy(
            src_ref=c_out.at[l],
            dst_ref=c_in.at[l],
            send_sem=carry_send.at[l],
            recv_sem=carry_recv.at[l],
            device_id=device(z, x, lax.div(there, 2), lax.rem(there, 2)),
            device_id_type=MESH,
        )

    def carry_out(l):
        c_out[l] = carries(jnp.zeros((8, 1024), F32))

        @pl.when(mp > 0)
        def _():
            carry_copy(l, jnp.maximum(mp - 1, 0)).start()

    def carry_into(l):
        @pl.when(mp < 3)
        def _():
            carry_copy(l, jnp.minimum(mp + 1, 3)).wait_recv()
            carries(c_in[l])

        @pl.when(mp > 0)
        def _():
            carry_copy(l, jnp.maximum(mp - 1, 0)).wait_send()

    def pre_back(p):
        def part(i, r):
            share = keep[p, r, :]
            local = jnp.concatenate([sg[p * 2, r, :], sg[p * 2 + 1, r, :]], axis=1)
            weight = enter[i, :, p * 256 : p * 256 + 256]
            parts = []
            for j in range(STEPS - 1, -1, -1):
                t = slice(j * 8, j * 8 + 8)
                parts.append(local[t] + weight)
                if j:
                    weight = weight - share[t] * weight
            adjoint = jnp.concatenate(parts[::-1], axis=0)
            for k in range(3):
                v = share if k == 2 else pre[p, k, r, :].astype(F32)
                pre[p, k, r, :] = (adjoint * v).astype(BF)

        each(part)

    def normed_back(first):
        w = {(p, k): w4[p // 2, p % 2, k].reshape(512, 256) for p in (first, first + 1) for k in range(3)}

        def part(i, r):
            back = 0.0 if first == 0 else acc[r, :]
            for p, k in w:
                back = back + dot_nt(pre[p, k, r, :], w[p, k])
            acc[r, :] = back

        each(part)

    def gate_grads(l, k):
        for p in range(4):
            g = dot(act_t[...], pre[p, k])
            g_w4[p // 2, p % 2, k] = g[0:512].astype(BF).reshape(4, 2, 2, 32, 256)
            biases[l, k : k + 1, p * 256 : p * 256 + 256] = g[512:513]

    act_t[512:528, :] = jnp.ones((16, rows_all), BF)
    ready("ct")

    def widen(i, r):
        v = into_steps(low[r, :].astype(F32), sg, i)
        grad[r, :] = v
        low[r, :] = v.astype(BF)

    each(widen)
    ready("gain")
    for l in (1, 0):
        ready("act_t")
        go_on()
        ready("dn")
        ready("up")
        for q in range(4):
            ready(("ff", q))
            feed(l, q)
            if l == 1 and q == 0:
                greeted()
            if q < 2:
                load_chunk(l, q + 2)
            elif q == 2:
                load("hid", hid_in.at[l], ff.at[0])
            if q % 2 == 1:
                push("up", l, q // 2)
            go_on()
        push("down", l, 0)
        push("down", l, 1)
        go_on()
        load("act_t", turned_in.at[l, 0], act_t.at[pl.ds(0, 512)])
        ready("mixed")
        rms_back(l, 1, mixed, low_t)
        load("stream", stream_in.at[l], mixed)
        go_on()
        if l == 1:
            load_feed(0)
        else:
            go_on()
            scatter.settle(range(4, 8))
        ready("w4")
        ready("hid")
        for p in range(4):
            out_back(p)
        push("gate", l, 3)
        go_on()
        if l == 1:
            load_chunk(0, 0)
        ready("keep")
        for p in range(4):
            states_back(p)
            go_on()
        carry_out(l)
        go_on()
        ready("q")
        carry_into(l)
        for p in range(4):
            pre_back(p)
            if p % 2 == 1:
                go_on()
        ready("act_t")
        for k in range(3):
            gate_grads(l, k)
            push("gate", l, k)
            go_on()
        if l == 1:
            load("act_t", turned_in.at[0, 1], act_t.at[pl.ds(0, 512)])
        for first in (0, 2):
            normed_back(first)
            go_on()
        ready("stream")
        if l == 1:
            load_chunk(0, 1)
            load_gates(0)
        rms_back(l, 0, mixed, None)
        if l == 1:
            load("mixed", mixed_in.at[0], mixed)
        go_on()
        rows = spread_back(gains[l, 0:1, :], 0, 16, 512, False) + spread_back(gains[l, 1:2, :], 16, 16, 512, False)
        for k in range(3):
            rows = rows + spread_back(biases[l, k : k + 1, :], 32 + 32 * k, 32, 1024, True)
        for n in range(32):
            g_vec[n // 8, n // 4 % 2, n // 2 % 2, n % 2, l] = jnp.broadcast_to(rows[n : n + 1, :], (8, 128))
    push("vec", 0, 0)
    go_on()

    def finish(i, r):
        mixed[r, :] = unturn(grad[r, :], sg, i)

    each(finish)
    save(mixed, grad_hbm)
    go_on()
    scatter.settle([*range(4), *range(8, 17)])
    for cp in saves:
        cp.wait()


def backward(cotangent, kept):
    w4_all, up_all, dn_all, gain, stream, mixed, keep, q, hid, ff, turned = kept
    rows = cotangent.shape[0]
    any_space = pl.BlockSpec(memory_space=pl.ANY)
    s = jax.ShapeDtypeStruct
    dma = pltpu.SemaphoreType.DMA
    v = pltpu.VMEM
    args = (cotangent, w4_all, up_all, dn_all, gain, stream, mixed, keep, q, hid, ff, turned)
    grad, gates, out, up, down, vec = pl.pallas_call(
        bwd_kernel,
        name="backward",
        out_shape=(
            s((rows, 512), F32), s((2, 3, 2, 32, 256), F32), s((2, 2, 32, 256), F32), s((2, 16, 2048), F32),
            s((2, 2, 2, 16, 512), F32), s((2, 8, 128), F32),
        ),
        in_specs=[any_space] * len(args),
        out_specs=(any_space,) * 6,
        scratch_shapes=[
            v((2, 2, 4, 4, 2, 2, 32, 256), BF), v((2, 2, 4, 2, 2, 2, 16, 512), BF), v((4, 2, 2, 2, 2, 2, 16, 512), BF),
            v((2, 8, 512), F32), v((4, rows, 256), F32), v((4, 3, rows, 256), BF), v((rows, 512), F32),
            v((2, 4, rows, 256), BF), v((rows, 512), F32), v((rows, 512), F32), v((rows, 512), BF), v((512, rows), BF),
            v((528, rows), BF), v((rows, 512), BF), v((8, rows, 128), F32), v((2, 8, 1024), F32), v((2, 8, 1024), F32),
            v((2, 3, 8, 1024), F32), v((3, 8, 1024), F32), v((2, 8, 512), F32), v((2, 8, 1024), F32),
            v((2, 2, 4, 4, 2, 2, 32, 256), BF), v((2, 2, 2, 4, 2, 2, 2, 16, 512), BF), v((2, 4, 2, 2, 2, 2, 2, 16, 512), BF),
            v((4, 2, 2, 2, 2, 8, 128), F32),
            v((2, 4, 2, 4, 2, 2, 32, 256), BF), v((2, 4, 4, 2, 32, 256), BF), v((2, 4, 2, 4, 32, 256), BF),
            v((2, 4, 2, 4, 32, 256), BF), v((2, 4, 3, 2, 32, 256), BF),
            v((2, 2, 2, 4, 2, 2, 16, 512), BF), v((2, 2, 4, 2, 16, 512), BF), v((2, 2, 4, 2, 16, 512), BF),
            v((2, 2, 2, 4, 16, 512), BF), v((2, 2, 3, 2, 16, 512), BF),
            v((2, 2, 4, 2, 2, 2, 16, 512), BF), v((2, 2, 4, 2, 16, 512), BF), v((2, 2, 4, 2, 16, 512), BF),
            v((2, 2, 2, 4, 16, 512), BF), v((2, 2, 3, 2, 16, 512), BF),
            v((4, 2, 2, 2, 8, 128), F32), v((4, 2, 8, 128), F32), v((4, 2, 8, 128), F32), v((2, 4, 8, 128), F32),
            v((3, 2, 8, 128), F32),
            v((2, 4, 2, 32, 256), F32), v((2, 2, 2, 16, 512), F32), v((2, 2, 2, 16, 512), F32), v((2, 8, 128), F32),
            dma((17, 8)), dma((17, 8)), dma((32,)), dma((24,)), dma((2,)), dma((2,)),
        ],
        compiler_params=pltpu.CompilerParams(
            collective_id=1, has_side_effects=True, vmem_limit_bytes=63 * 2**20
        ),
    )(*args)
    return grad, gates, out, up, down, vec


def settle_kernel(*refs):
    vec, biases, gain_one, gain_two = refs[6], *refs[13:]
    for src, dst in zip(refs[:6], refs[7:13]):
        dst[...] = src[...]
    for l in range(2):
        gain_one[l : l + 1, :] = vec[l, 0:1, 0:16]
        gain_two[l : l + 1, :] = vec[l, 0:1, 16:32]
        for k in range(3):
            biases[k, l : l + 1, :] = vec[l, 0:1, 32 + 32 * k : 64 + 32 * k]


def settle(result, grad, gates, out, up, down, vec):
    rows = result.shape[0]
    s = jax.ShapeDtypeStruct
    args = (
        result, grad, gates.reshape(12, 32, 256), out.reshape(4, 32, 256), up, down.reshape(8, 16, 512),
    )
    whole = lambda *shape: pl.BlockSpec(shape, lambda i: (0,) * len(shape))
    blocks = [
        pl.BlockSpec((rows // 4, 512), lambda i: (i, 0)),
        pl.BlockSpec((rows // 4, 512), lambda i: (i, 0)),
        pl.BlockSpec((3, 32, 256), lambda i: (i, 0, 0)),
        pl.BlockSpec((1, 32, 256), lambda i: (i, 0, 0)),
        pl.BlockSpec((2, 16, 512), lambda i: (0, 0, i)),
        pl.BlockSpec((2, 16, 512), lambda i: (i, 0, 0)),
    ]
    result, grad, gates, out, up, down, biases, gain_one, gain_two = pl.pallas_call(
        settle_kernel,
        name="settle",
        grid=(4,),
        out_shape=tuple(s(v.shape, v.dtype) for v in args) + (s((3, 2, 32), F32), s((2, 16), F32), s((2, 16), F32)),
        in_specs=blocks + [whole(2, 8, 128)],
        out_specs=tuple(blocks) + (whole(3, 2, 32), whole(2, 16), whole(2, 16)),
    )(*args, vec)
    return (
        result,
        grad,
        gates.reshape(2, 3, 64, 256),
        biases.transpose(1, 0, 2),
        out.reshape(2, 64, 256).transpose(0, 2, 1),
        gain_one,
        gain_two,
        up,
        down.reshape(2, 64, 512),
    )


def fits(inputs, gate_weight, gate_bias, out_weight, gain_one, gain_two, up_weight, down_weight):
    rows = inputs.shape[0]
    shapes = (gate_weight.shape, gate_bias.shape, out_weight.shape, gain_one.shape, up_weight.shape, down_weight.shape)
    planned = ((2, 3, 64, 256), (2, 3, 32), (2, 256, 64), (2, 16), (2, 16, 2048), (2, 64, 512))
    axes = (lax.axis_size("dp"), lax.axis_size("mp"))
    return axes == (8, 4) and shapes == planned and rows == 768 and 4 * rows == 3 * LENGTH


def general_body(
    inputs,
    gate_weight,
    gate_bias,
    out_weight,
    norm_gain_one,
    norm_gain_two,
    up_weight,
    down_weight,
    cotangent,
):
    own_rows = inputs.shape[0]
    group = own_rows * lax.axis_size("mp")
    starts = (jnp.arange(group, dtype=jnp.int32) % LENGTH == 0)[:, None]
    layer_count = gate_weight.shape[0]
    width = gate_weight.shape[3]
    stream = inputs.astype(jnp.float32)
    saved = []
    held = []
    for layer_no in range(layer_count):
        gates_full, bias_full, out_full = (
            lax.all_gather(gate_weight[layer_no], "dp", axis=1, tiled=True),
            lax.all_gather(gate_bias[layer_no], "dp", axis=1, tiled=True),
            lax.all_gather(out_weight[layer_no], "dp", axis=1, tiled=True),
        )
        up_full, down_full, gain_first, gain_second = (
            lax.all_gather(up_weight[layer_no], ("dp", "mp"), axis=0, tiled=True),
            lax.all_gather(down_weight[layer_no], ("dp", "mp"), axis=0, tiled=True),
            lax.all_gather(norm_gain_one[layer_no], ("dp", "mp"), axis=0, tiled=True),
            lax.all_gather(norm_gain_two[layer_no], ("dp", "mp"), axis=0, tiled=True),
        )
        gain_first = gain_first.astype(jnp.float32)
        gain_second = gain_second.astype(jnp.float32)
        normed = rms_scale(stream, gain_first).astype(jnp.bfloat16)
        normed_all = lax.all_gather(normed, "mp", axis=0, tiled=True)
        pre_acts = (
            jnp.einsum("td,kdf->ktf", normed_all, gates_full, preferred_element_type=jnp.float32)
            + bias_full.astype(jnp.float32)[:, None, :]
        )
        decay, drive = gate_terms(pre_acts, starts)
        products, states = lax.associative_scan(link, (decay, drive), axis=0)
        hidden = states.astype(jnp.bfloat16)
        mixed = stream + lax.psum_scatter(
            dot_plain(hidden, out_full).astype(jnp.bfloat16), "mp", scatter_dimension=0, tiled=True
        ).astype(jnp.float32)
        second = rms_scale(mixed, gain_second).astype(jnp.bfloat16)
        up_acts = dot_plain(second, up_full)
        activated = jax.nn.gelu(up_acts).astype(jnp.bfloat16)
        saved.append(
            {
                "stream": stream,
                "gain_first": gain_first,
                "gain_second": gain_second,
                "normed": normed_all,
                "pre": pre_acts,
                "decay": decay,
                "states": states,
                "hidden": hidden,
                "mixed": mixed,
                "second": second,
                "up_acts": up_acts,
                "activated": activated,
            }
        )
        held.append((gates_full, out_full, up_full, down_full))
        stream = mixed + dot_plain(activated, down_full)
    grad = cotangent.astype(jnp.float32)
    gate_parts = []
    mlp_parts = []
    for layer_no in reversed(range(layer_count)):
        kept = saved[layer_no]
        gates_full, out_full, up_full, down_full = held[layer_no]
        grad_low = grad.astype(jnp.bfloat16)
        act_grad = dot_last(grad_low, down_full)
        down_grad = dot_first(kept["activated"], grad_low)
        unused_gelu, gelu_back = jax.vjp(jax.nn.gelu, kept["up_acts"])
        up_low = gelu_back(act_grad)[0].astype(jnp.bfloat16)
        up_grad = dot_first(kept["second"], up_low)
        second_grad = dot_last(up_low, up_full)
        unused_norm, norm_back = jax.vjp(rms_scale, kept["mixed"], kept["gain_second"])
        mixed_part, gain_two_grad = norm_back(second_grad)
        mixed_grad = grad + mixed_part
        mixed_low = mixed_grad.astype(jnp.bfloat16)
        mixed_all = lax.all_gather(mixed_low, "mp", axis=0, tiled=True)
        state_grad = dot_last(mixed_all, out_full)
        out_grad = dot_first(kept["hidden"], mixed_all)
        decay = kept["decay"]
        shifted = jnp.concatenate([decay[1:], jnp.ones((1, width), jnp.float32)], axis=0)
        back_products, back_partial = lax.associative_scan(
            link, (shifted[::-1], state_grad[::-1]), axis=0
        )
        adjoint = back_partial[::-1]
        previous = jnp.concatenate(
            [jnp.zeros((1, width), jnp.float32), kept["states"][:-1]], axis=0
        )
        unused_gate, gate_back = jax.vjp(partial(gate_terms, starts=starts), kept["pre"])
        pre_low = gate_back((adjoint * previous, adjoint))[0].astype(jnp.bfloat16)
        bias_grad = jnp.sum(pre_low.astype(jnp.float32), axis=1)
        gate_grad = jnp.einsum(
            "td,ktf->kdf", kept["normed"], pre_low, preferred_element_type=jnp.float32
        )
        normed_part = jnp.einsum(
            "ktf,kdf->td", pre_low, gates_full, preferred_element_type=jnp.float32
        )
        normed_grad = lax.psum_scatter(
            normed_part.astype(jnp.bfloat16), "mp", scatter_dimension=0, tiled=True
        ).astype(jnp.float32)
        unused_first, first_back = jax.vjp(rms_scale, kept["stream"], kept["gain_first"])
        stream_part, gain_one_grad = first_back(normed_grad)
        grad = mixed_grad + stream_part
        gate_parts.append(
            (
                sum_at_owner(gate_grad.astype(jnp.bfloat16), "dp", 1),
                sum_at_owner(bias_grad.astype(jnp.bfloat16), "dp", 1),
                sum_at_owner(out_grad.astype(jnp.bfloat16), "dp", 1),
            )
        )
        mlp_parts.append(
            (
                lax.psum_scatter(up_grad, ("dp", "mp"), scatter_dimension=0, tiled=True),
                lax.psum_scatter(down_grad, ("dp", "mp"), scatter_dimension=0, tiled=True),
                lax.psum_scatter(gain_one_grad, ("dp", "mp"), scatter_dimension=0, tiled=True),
                lax.psum_scatter(gain_two_grad, ("dp", "mp"), scatter_dimension=0, tiled=True),
            )
        )
    gate_parts = gate_parts[::-1]
    mlp_parts = mlp_parts[::-1]
    gate_stack = tuple((jnp.stack([entry[member] for entry in gate_parts]) for member in range(3)))
    mlp_stack = tuple((jnp.stack([entry[member] for entry in mlp_parts]) for member in range(4)))
    return (
        stream.astype(jnp.bfloat16),
        grad,
        gate_stack[0],
        gate_stack[1],
        gate_stack[2],
        mlp_stack[2],
        mlp_stack[3],
        mlp_stack[0],
        mlp_stack[1],
    )


def body(inputs, gate_weight, gate_bias, out_weight, gain_one, gain_two, up_weight, down_weight, cotangent):
    shards = (gate_weight, gate_bias, out_weight, gain_one, gain_two, up_weight, down_weight)
    if not fits(inputs, *shards):
        return general_body(inputs, *shards, cotangent)
    out, *kept = forward(inputs, *shards)
    return settle(out, *backward(cotangent, kept))


def solution(mesh):
    placed = (
        P(("dp", "mp"), None),
        P(None, None, "dp", "mp"),
        P(None, None, ("mp", "dp")),
        P(None, "mp", "dp"),
        P(None, ("dp", "mp")),
        P(None, ("dp", "mp")),
        P(None, ("dp", "mp"), None),
        P(None, ("dp", "mp"), None),
        P(("dp", "mp"), None),
    )
    return jax.shard_map(
        body,
        mesh=mesh,
        in_specs=placed,
        out_specs=(
            P(("dp", "mp"), None),
            P(("dp", "mp"), None),
            P(None, None, "dp", "mp"),
            P(None, None, ("mp", "dp")),
            P(None, "mp", "dp"),
            P(None, ("dp", "mp")),
            P(None, ("dp", "mp")),
            P(None, ("dp", "mp"), None),
            P(None, ("dp", "mp"), None),
        ),
        check_vma=False,
    )
```

```python
from functools import partial

import jax
import jax.numpy as jnp
from jax import lax
from jax.experimental import pallas as pl
from jax.experimental.pallas import tpu as pltpu
from jax.sharding import PartitionSpec as P

LENGTH = 1024


eps = 1e-06


def cut_along(x, dim, size):
    shape = x.shape
    blocks = x.reshape(*shape[:dim], size, shape[dim] // size, *shape[dim + 1 :])
    return jnp.moveaxis(blocks, dim, 0)


def sum_at_owner(x, axis, dim):
    size = lax.axis_size(axis)
    blocks = lax.all_to_all(cut_along(x, dim, size), axis, 0, 0, tiled=True)
    return jnp.sum(blocks.astype(jnp.float32), axis=0)


def rms_scale(values, gain):
    return values * lax.rsqrt(jnp.mean(values * values, axis=-1, keepdims=True) + eps) * gain


def link(earlier, later):
    return (earlier[0] * later[0], later[0] * earlier[1] + later[1])


def gate_terms(pre_acts, starts):
    sig_forget = jax.nn.sigmoid(pre_acts[0])
    sig_input = jax.nn.sigmoid(pre_acts[1])
    total = sig_forget + sig_input
    decay = jnp.where(starts, 0.0, sig_forget / total)
    return (decay, sig_input / total * pre_acts[2])


def dot_plain(left, right):
    return jnp.dot(left, right, preferred_element_type=jnp.float32)


def dot_first(left, right):
    return lax.dot_general(
        left, right, (((0,), (0,)), ((), ())), preferred_element_type=jnp.float32
    )


def dot_last(left, right):
    return lax.dot_general(
        left, right, (((1,), (1,)), ((), ())), preferred_element_type=jnp.float32
    )


GATHER_PLAN = (
    (0, 5, 10, 15, 1, 20, 6, 25, 2, 11, 30, 45, 7, 3, 16, 35, 12, 4),
    (),
    (46,),
    (21, 40),
    (8, 26, 50, 17, 9, 31, 55, 13, 47, 22, 36, 60, 27, 14, 41, 65, 18, 32, 51, 70, 19),
    (),
    (56, 75, 37, 23),
    (),
    (42, 28),
    (24,),
    (33,),
    (52, 29),
    (),
    (),
    (57, 48, 34),
    (),
    (61, 80, 38),
    (),
    (43, 66),
    (49, 39, 53, 71, 44),
    (58,),
    (76, 62, 54),
    (67, 81, 72, 59),
    (),
    (77,),
    (),
    (63,),
    (68, 82, 64),
    (69,),
    (),
    (73,),
    (),
    (78,),
    (83, 74),
    (),
    (),
    (79,),
    (84,),
    (),
)
SCATTER_PLAN = (
    (),
    (),
    (),
    (),
    (0,),
    (),
    (),
    (),
    (5,),
    (10, 15),
    (1,),
    (20,),
    (),
    (),
    (6,),
    (11,),
    (16,),
    (21, 2),
    (),
    (25, 7),
    (30,),
    (35,),
    (12,),
    (26, 17, 31),
    (36, 22),
    (3,),
    (8,),
    (13,),
    (),
    (40,),
    (27,),
    (18, 4),
    (),
    (45, 32, 9),
    (50, 55, 41),
    (),
    (37, 14, 23, 46, 28, 19, 51, 33, 56, 42, 24, 38, 29, 47, 34, 52, 39),
    (60,),
    (),
    (57,),
    (43,),
    (48,),
    (),
    (61, 53),
    (58,),
    (65, 44),
    (70,),
    (75,),
    (62, 49),
    (66, 54),
    (71, 76, 59),
    (80,),
    (63, 67, 81, 72, 64, 77, 68, 82, 73, 78, 83, 69, 74, 79, 84),
)


ALL = slice(None)
MESH = pl.DeviceIdType.MESH
BF = jnp.bfloat16
F32 = jnp.float32
SHIFT = 0.25
LOG_SHIFT = -1.3862943611198906
TOP = 87.0
GELU_A = 0.7978845608028654
GELU_B = 0.044715
ROWS = 256
STEPS = ROWS // 8


def first_of(mp, rows):
    return lax.div(jnp.minimum(lax.rem(mp * (LENGTH - rows), LENGTH), rows), ROWS)


Z_LAST = (("gate", 1, 0),)


def place():
    dp = lax.axis_index("dp")
    mp = lax.axis_index("mp")
    return (lax.div(dp, 2), lax.rem(dp, 2), lax.div(mp, 2), lax.rem(mp, 2))


def device(z, x, y, c):
    return (z * 2 + x, y * 2 + c)


def greet(wait=True):
    z, x, y, c = place()
    partners = [device(lax.rem(z + k, 4), x, y, c) for k in (1, 2, 3)]
    partners += [device(z, 1 - x, y, c), device(z, x, 1 - y, c)]
    partners += [device(z, x, y, 1 - c), device(z, x, 1 - y, 1 - c)]
    barrier = pltpu.get_barrier_semaphore()
    for partner in partners:
        pl.semaphore_signal(barrier, inc=1, device_id=partner, device_id_type=MESH)
    if wait:
        greeted()


def greeted():
    pl.semaphore_wait(pltpu.get_barrier_semaphore(), 7)


class Gather:
    def __init__(self, bufs, own, items, plan, send, recv):
        self.bufs = bufs
        self.own = own
        self.items = items
        self.send = send
        self.recv = recv
        self.at = place()
        self.sent = []
        self.plan = [list(row) for row in plan]

    def view(self, item, z, x, y, c, h):
        kind, l, part = item
        w4, up, dn, vec = self.bufs
        if kind == "vec":
            return vec.at[z, x, y, c, h]
        if kind == "gate":
            return w4.at[l, y, c, part, z, x, h]
        if kind == "up":
            return up.at[l, part, h, z, x, y, c]
        return dn.at[l, z, x, y, c, part, h]

    def go(self, n, slot, ref, target):
        cp = pltpu.make_async_remote_copy(
            src_ref=ref,
            dst_ref=ref,
            send_sem=self.send.at[n, slot],
            recv_sem=self.recv.at[n, slot],
            device_id=target,
            device_id_type=MESH,
        )
        cp.start()
        self.sent.append(cp)

    def landed(self, n, slot, ref, source):
        pltpu.make_async_remote_copy(
            src_ref=ref,
            dst_ref=ref,
            send_sem=self.send.at[n, slot],
            recv_sem=self.recv.at[n, slot],
            device_id=source,
            device_id_type=MESH,
        ).wait_recv()

    def stage(self, step, n, item):
        z, x, y, c = self.at
        v = lambda *where: self.view(item, *where)
        to_x = device(z, 1 - x, y, c)
        to_y = device(z, x, 1 - y, c)
        to_c = device(z, x, y, 1 - c)
        if step == 0:
            for cp in self.own.pop(item):
                cp.wait()
        if item in Z_LAST:
            self.stage_z_last(step, n, v, to_x, to_y, to_c)
        elif step == 0:
            for k in (1, 2, 3):
                self.go(n, k - 1, v(z, x, y, c, ALL), device(lax.rem(z + k, 4), x, y, c))
        elif step == 1:
            for k in (1, 2, 3):
                source = lax.rem(z + 4 - k, 4)
                self.landed(n, k - 1, v(source, x, y, c, ALL), device(source, x, y, c))
            self.go(n, 3, v(ALL, x, y, c, 0), to_x)
            self.go(n, 4, v(ALL, x, y, c, 1), to_y)
            self.go(n, 7, v(ALL, x, y, c, ALL), to_c)
        elif step == 2:
            self.landed(n, 3, v(ALL, 1 - x, y, c, 0), to_x)
            self.go(n, 5, v(ALL, ALL, y, c, 0), to_y)
            self.landed(n, 4, v(ALL, x, 1 - y, c, 1), to_y)
            self.go(n, 6, v(ALL, x, ALL, c, 1), to_x)
            self.go(n, 8, v(ALL, 1 - x, y, c, 0), to_c)
            self.go(n, 9, v(ALL, x, 1 - y, c, 1), to_c)
        elif step == 3:
            self.landed(n, 5, v(ALL, ALL, 1 - y, c, 0), to_y)
            self.go(n, 10, v(ALL, ALL, 1 - y, c, 0), to_c)
            self.landed(n, 6, v(ALL, 1 - x, ALL, c, 1), to_x)
            self.go(n, 11, v(ALL, 1 - x, ALL, c, 1), to_c)
        else:
            self.landed(n, 7, v(ALL, x, y, 1 - c, ALL), to_c)
            self.landed(n, 8, v(ALL, 1 - x, y, 1 - c, 0), to_c)
            self.landed(n, 9, v(ALL, x, 1 - y, 1 - c, 1), to_c)
            self.landed(n, 10, v(ALL, ALL, 1 - y, 1 - c, 0), to_c)
            self.landed(n, 11, v(ALL, 1 - x, ALL, 1 - c, 1), to_c)

    def stage_z_last(self, step, n, v, to_x, to_y, to_c):
        z, x, y, c = self.at
        if step == 0:
            self.go(n, 3, v(z, x, y, c, 0), to_x)
            self.go(n, 4, v(z, x, y, c, 1), to_y)
        elif step == 1:
            self.landed(n, 3, v(z, 1 - x, y, c, 0), to_x)
            self.go(n, 5, v(z, ALL, y, c, 0), to_y)
            self.landed(n, 4, v(z, x, 1 - y, c, 1), to_y)
            self.go(n, 6, v(z, x, ALL, c, 1), to_x)
        elif step == 2:
            self.landed(n, 5, v(z, ALL, 1 - y, c, 0), to_y)
            self.landed(n, 6, v(z, 1 - x, ALL, c, 1), to_x)
            for k in (1, 2, 3):
                self.go(n, k - 1, v(z, ALL, ALL, c, ALL), device(lax.rem(z + k, 4), x, y, c))
            self.go(n, 7, v(z, ALL, ALL, c, ALL), to_c)
        elif step == 3:
            for k in (1, 2, 3):
                source = lax.rem(z + 4 - k, 4)
                self.landed(n, k - 1, v(source, ALL, ALL, c, ALL), device(source, x, y, c))
                self.go(n, 7 + k, v(source, ALL, ALL, c, ALL), to_c)
        else:
            self.landed(n, 7, v(z, ALL, ALL, 1 - c, ALL), to_c)
            for k in (1, 2, 3):
                self.landed(n, 7 + k, v(lax.rem(z + 4 - k, 4), ALL, ALL, 1 - c, ALL), to_c)

    def go_on(self):
        for code in self.plan.pop(0):
            n, step = divmod(code, 5)
            self.stage(step, n, self.items[n])

    def finish(self):
        for cp in self.sent:
            cp.wait_send()


def dot(a, b):
    return jnp.dot(a, b, preferred_element_type=F32)


def dot_nt(a, b):
    return lax.dot_general(a, b, (((1,), (1,)), ((), ())), preferred_element_type=F32)


def dot_tn(a, b):
    return lax.dot_general(a, b, (((0,), (0,)), ((), ())), preferred_element_type=F32)


def spread(vec, l, first, size, total, per_mp):
    rows = vec[:, :, :, :, l].reshape(256, 128).astype(BF)
    j = lax.broadcasted_iota(jnp.int32, (128, total), 0)
    d = lax.broadcasted_iota(jnp.int32, (128, total), 1)
    pick = jnp.where(j == first + lax.rem(d, size), 1.0, 0.0).astype(BF)
    wide = dot(rows, pick)
    r = lax.div(lax.broadcasted_iota(jnp.int32, (256, total), 0), 8)
    d = lax.broadcasted_iota(jnp.int32, (256, total), 1)
    if per_mp:
        owner = lax.div(lax.rem(d, total // 4), size) * 4 + lax.div(d, total // 4)
    else:
        owner = lax.div(d, size)
    return jnp.sum(jnp.where(r == owner, wide, 0.0), axis=0, keepdims=True)


def combine(a, b, row, sign):
    for s in (1, 2, 4):
        keep = (row >= s) if sign > 0 else (row < 8 - s)
        by = s if sign > 0 else 8 - s
        am = jnp.where(keep, a, 0.0)
        b = b + am * pltpu.roll(b, by, 0)
        if s < 4:
            a = jnp.where(keep, a * pltpu.roll(a, by, 0), a)
        else:
            a = jnp.where(keep, a * pltpu.roll(a, by, 0), a)
    return a, b


def into_steps(v, turn, i):
    for n in range(4):
        turn[n, pl.ds(i * ROWS, ROWS), :] = v[:, n * 128 : n * 128 + 128]
    parts = []
    for n in range(4):
        rows = [turn[n, pl.ds(i * ROWS + j, 8, stride=STEPS), :] for j in range(STEPS)]
        parts.append(jnp.concatenate(rows, axis=0))
    return jnp.concatenate(parts, axis=1)


def unturn(v, turn, i):
    for n in range(4):
        for j in range(STEPS):
            turn[n, pl.ds(i * ROWS + j, 8, stride=STEPS), :] = v[j * 8 : j * 8 + 8, n * 128 : n * 128 + 128]
    return jnp.concatenate([turn[n, pl.ds(i * ROWS, ROWS), :] for n in range(4)], axis=1)


def fwd_kernel(
    x_in, gate_in, out_in, up_in, down_in, gain_one_in, gain_two_in, bias_in,
    out_hbm, w4_hbm, up_hbm, dn_hbm, gain_hbm, stream_hbm, mixed_hbm, keep_hbm, q_hbm, hid_hbm, ff_hbm, turned_hbm,
    w4, up, dn, vec, normed, stream, mixed, turned, turn, ends, enter, keep, states, c3, hid, ff, bias, gain, c_out, c_in,
    ag_send, ag_recv, own_sem, spill_sem, carry_send, carry_recv,
):
    z, x, y, c = place()
    mp = y * 2 + c
    rows_all = normed.shape[0]
    chunks = rows_all // ROWS
    fill = []

    def local(src, dst, sem):
        cp = pltpu.make_async_copy(src, dst, sem)
        cp.start()
        return cp

    own = {}
    n_own = 0

    def add_own(key, src, dst):
        nonlocal n_own
        own.setdefault(key, []).append(local(src, dst, own_sem.at[n_own]))
        n_own += 1

    x_copy = local(x_in, normed, own_sem.at[48])
    own[("vec", 0, 0)] = []
    vec[z, x, y, c] = jnp.zeros((2, 8, 128), F32)
    for l in range(2):
        ours = [gain_one_in[l : l + 1, :], gain_two_in[l : l + 1, :]] + [bias_in[k, l : l + 1, :] for k in range(3)]
        vec[z, x, y, c, l, 0:1, :] = jnp.concatenate([v.astype(F32) for v in ours], axis=1)
    for l in range(2):
        for k in range(3):
            add_own(("gate", l, k), gate_in.at[l, k], w4.at[l, y, c, k, z, x])
        add_own(("gate", l, 3), out_in.at[l], w4.at[l, y, c, 3, z, x])
        for pair in range(2):
            for h in range(2):
                columns = pl.ds((pair * 2 + h) * 512, 512)
                add_own(("up", l, pair), up_in.at[l, :, columns], up.at[l, pair, h, z, x, y, c])
            add_own(("down", l, pair), down_in.at[l, pair], dn.at[l, z, x, y, c, pair])
    greet()
    items = [("vec", 0, 0)]
    for l in range(2):
        items += [("gate", l, k) for k in range(4)]
        items += [(kind, l, pair) for kind in ("up", "down") for pair in range(2)]
    gather = Gather((w4, up, dn, vec), own, items, GATHER_PLAN, ag_send, ag_recv)
    go_on = gather.go_on

    n_spill = 0
    spills = {}

    def spill(key, src, dst):
        nonlocal n_spill
        spills[key] = local(src, dst, spill_sem.at[n_spill])
        n_spill += 1

    def settle(key):
        if key in spills:
            spills.pop(key).wait()


    def rms(src, dst, g):
        @pl.loop(0, chunks)
        def _(i):
            r = pl.ds(pl.multiple_of(i * ROWS, ROWS), ROWS)
            v = src[r, :]
            scale = lax.rsqrt(jnp.mean(v * v, axis=-1, keepdims=True) + eps)
            n = (v * scale * g).astype(BF)
            dst[r, :] = n
            turned[0, :, r] = n.T

    def gate_panel(l, p):
        w = [w4[l, p // 2, p % 2, k].reshape(512, 256) for k in range(3)]
        bs = [bias[l, k : k + 1, p * 256 : (p + 1) * 256] for k in range(3)]

        @pl.loop(0, chunks)
        def _(i):
            r = pl.ds(pl.multiple_of(i * ROWS, ROWS), ROWS)
            n = normed[r, :]
            f, inp, cand = [dot(n, w[k]) + bs[k] for k in range(3)]
            e_f = jnp.exp(jnp.minimum(-f, TOP) + LOG_SHIFT)
            e_i = jnp.exp(jnp.minimum(-inp, TOP) + LOG_SHIFT)
            a_f = e_f + SHIFT
            a_i = e_i + SHIFT
            total = a_f + a_i
            inv = pl.reciprocal(total, approx=True)
            inv = inv * (2.0 - total * inv)
            share = a_f * inv
            decay = a_i * inv
            drive = share * cand
            keep[p, r, :] = share
            c3[p, 0, r, :] = (decay * (e_f * inv)).astype(BF)
            c3[p, 1, r, :] = (share * (e_i * inv)).astype(BF)
            c3[p, 2, r, :] = cand.astype(BF)
            s = drive[0:8]
            a = decay[0:8]
            local_states = [s]
            for j in range(1, STEPS):
                t = slice(j * 8, j * 8 + 8)
                s = decay[t] * s + drive[t]
                a = a * decay[t]
                local_states.append(s)
            states[p, r, :] = jnp.concatenate(local_states, axis=0)
            columns = slice(p * 256, p * 256 + 256)
            ends[0, i, :, columns] = a
            ends[1, i, :, columns] = s

    row = lax.broadcasted_iota(jnp.int32, (8, 1024), 0)
    first_chunk = first_of(mp, rows_all)

    def carries(entering):
        for i in range(chunks):
            c0 = jnp.where(first_chunk == i, 0.0, entering)
            a, s = combine(ends[0, i], ends[1, i], row, 1)
            enter[i] = jnp.where(row == 0, c0, pltpu.roll(a, 1, 0) * c0 + pltpu.roll(s, 1, 0))
            entering = jnp.broadcast_to(a[7:8] * c0[7:8] + s[7:8], (8, 1024))
        return entering

    def carry_copy(l, there):
        return pltpu.make_async_remote_copy(
            src_ref=c_out.at[l],
            dst_ref=c_in.at[l],
            send_sem=carry_send.at[l],
            recv_sem=carry_recv.at[l],
            device_id=device(z, x, lax.div(there, 2), lax.rem(there, 2)),
            device_id_type=MESH,
        )

    def carry_out(l):
        c_out[l] = carries(jnp.zeros((8, 1024), F32))

        @pl.when(mp < 3)
        def _():
            carry_copy(l, jnp.minimum(mp + 1, 3)).start()

    def carry_into(l):
        @pl.when(mp > 0)
        def _():
            carry_copy(l, jnp.maximum(mp - 1, 0)).wait_recv()
            carries(c_in[l])

        @pl.when(mp < 3)
        def _():
            carry_copy(l, jnp.minimum(mp + 1, 3)).wait_send()

    def project(l):
        g = gain[l, 1:2, :]
        w = [w4[l, p // 2, p % 2, 3].reshape(512, 256) for p in range(4)]

        @pl.loop(0, chunks)
        def _(i):
            r = pl.ds(pl.multiple_of(i * ROWS, ROWS), ROWS)
            v = stream[r, :]
            for p in range(4):
                share = keep[p, r, :]
                s_local = states[p, r, :]
                cand = c3[p, 2, r, :].astype(F32)
                enters = enter[i, :, p * 256 : p * 256 + 256]
                before = enters
                weight = enters
                now, gap = [], []
                for j in range(STEPS):
                    t = slice(j * 8, j * 8 + 8)
                    weight = weight - share[t] * weight
                    s = s_local[t] + weight
                    gap.append(before - cand[t])
                    now.append(s)
                    before = s
                gap = jnp.concatenate(gap, axis=0)
                h = jnp.concatenate(now, axis=0).astype(BF)
                hid[p, r, :] = h
                c3[p, 0, r, :] = (gap * c3[p, 0, r, :].astype(F32)).astype(BF)
                c3[p, 1, r, :] = (-gap * c3[p, 1, r, :].astype(F32)).astype(BF)
                v = v + dot_nt(h, w[p])
            mixed[r, :] = v
            scale = lax.rsqrt(jnp.mean(v * v, axis=-1, keepdims=True) + eps)
            n = (v * scale * g).astype(BF)
            normed[r, :] = n
            turned[1, :, r] = n.T

    def feed_up(l, q):
        w_up = up[l, q // 2, q % 2].reshape(512, 512)

        @pl.loop(0, chunks)
        def _(i):
            r = pl.ds(pl.multiple_of(i * ROWS, ROWS), ROWS)
            u = dot(normed[r, :], w_up)
            sq = u * u
            t = jnp.tanh(u * (GELU_A + (GELU_A * GELU_B) * sq))
            gate = 0.5 + 0.5 * t
            act = (u * gate).astype(BF)
            slope = gate + (0.5 * u) * (1.0 - t * t) * (GELU_A + (3.0 * GELU_A * GELU_B) * sq)
            for half in range(2):
                side = slice(half * 256, half * 256 + 256)
                ff[q, half, r, :] = slope[:, side].astype(BF)
                ff[q, 2 + half, r, :] = act[:, side]

    def feed_down(l):
        w_down = dn[l].reshape(2048, 512)

        @pl.loop(0, chunks)
        def _(i):
            r = pl.ds(pl.multiple_of(i * ROWS, ROWS), ROWS)
            acts = [ff[q, 2 + half, r, :] for q in range(4) for half in range(2)]
            v = mixed[r, :] + dot(jnp.concatenate(acts, axis=1), w_down)
            if l == 0:
                stream[r, :] = v
            else:
                normed[r, :] = unturn(v, turn, i).astype(BF)

    go_on()
    for l in range(2):
        gain[l, 0:1, :] = spread(vec, l, 0, 16, 512, False)
        gain[l, 1:2, :] = spread(vec, l, 16, 16, 512, False)
        for k in range(3):
            bias[l, k : k + 1, :] = spread(vec, l, 32 + 32 * k, 32, 1024, True)
        go_on()
    x_copy.wait()

    @pl.loop(0, chunks)
    def _(i):
        r = pl.ds(pl.multiple_of(i * ROWS, ROWS), ROWS)
        stream[r, :] = into_steps(normed[r, :].astype(F32), turn, i)

    spill("gain", gain, gain_hbm)
    for l in range(2):
        settle(("first", 0))
        rms(stream, normed, gain[l, 0:1, :])
        spill(("first", l), turned.at[0], turned_hbm.at[l, 0])
        settle(("keep", 0))
        settle(("q", 0))
        spill(("stream", l), stream, stream_hbm.at[l])
        go_on()
        go_on()
        for p in range(4):
            gate_panel(l, p)
            go_on()
        spill(("keep", l), keep, keep_hbm.at[l])
        carry_out(l)
        settle(("hid", 0))
        settle(("mixed", 0))
        go_on()
        carry_into(l)
        settle(("second", 0))
        project(l)
        spill(("second", l), turned.at[1], turned_hbm.at[l, 1])
        spill(("q", l), c3.at[:, pl.ds(0, 2)], q_hbm.at[l])
        spill(("hid", l), hid, hid_hbm.at[l])
        spill(("w4", l), w4.at[l], w4_hbm.at[l])
        spill(("mixed", l), mixed, mixed_hbm.at[l])
        go_on()
        for q in range(4):
            settle(("ff", 0, q))
            go_on()
            feed_up(l, q)
            spill(("ff", l, q), ff.at[q], ff_hbm.at[l, q])
            go_on()
        spill(("up", l), up.at[l], up_hbm.at[l])
        settle(("stream", l))
        go_on()
        spill(("dn", l), dn.at[l], dn_hbm.at[l])
        feed_down(l)
        go_on()
    spill("result", normed, out_hbm)
    for key in list(spills):
        settle(key)
    gather.finish()


def forward(x, gate_weight, gate_bias, out_weight, gain_one, gain_two, up_weight, down_weight):
    rows = x.shape[0]
    any_space = pl.BlockSpec(memory_space=pl.ANY)
    args = (
        x,
        gate_weight.reshape(2, 3, 2, 32, 256),
        out_weight.transpose(0, 2, 1).reshape(2, 2, 32, 256),
        up_weight,
        down_weight.reshape(2, 2, 2, 16, 512),
        gain_one,
        gain_two,
        gate_bias.transpose(1, 0, 2),
    )
    s = jax.ShapeDtypeStruct
    w4 = (2, 2, 2, 4, 4, 2, 2, 32, 256)
    up = (2, 2, 2, 4, 2, 2, 2, 16, 512)
    dn = (2, 4, 2, 2, 2, 2, 2, 16, 512)
    dma = pltpu.SemaphoreType.DMA
    return pl.pallas_call(
        fwd_kernel,
        name="forward",
        out_shape=(
            s((rows, 512), BF), s(w4, BF), s(up, BF), s(dn, BF), s((2, 8, 512), F32), s((2, rows, 512), F32),
            s((2, rows, 512), F32), s((2, 4, rows, 256), F32), s((2, 4, 2, rows, 256), BF),
            s((2, 4, rows, 256), BF), s((2, 4, 4, rows, 256), BF), s((2, 2, 512, rows), BF),
        ),
        in_specs=[any_space] * 5 + [pl.BlockSpec(memory_space=pltpu.VMEM)] * 3,
        out_specs=(any_space,) * 12,
        scratch_shapes=[
            pltpu.VMEM(w4, BF), pltpu.VMEM(up, BF), pltpu.VMEM(dn, BF), pltpu.VMEM((4, 2, 2, 2, 2, 8, 128), F32),
            pltpu.VMEM((rows, 512), BF), pltpu.VMEM((rows, 512), F32), pltpu.VMEM((rows, 512), F32), pltpu.VMEM((2, 512, rows), BF), pltpu.VMEM((4, rows, 128), F32),
            pltpu.VMEM((2, 3, 8, 1024), F32), pltpu.VMEM((3, 8, 1024), F32),
            pltpu.VMEM((4, rows, 256), F32), pltpu.VMEM((4, rows, 256), F32), pltpu.VMEM((4, 3, rows, 256), BF),
            pltpu.VMEM((4, rows, 256), BF), pltpu.VMEM((4, 4, rows, 256), BF),
            pltpu.VMEM((2, 8, 1024), F32), pltpu.VMEM((2, 8, 512), F32),
            pltpu.VMEM((2, 8, 1024), F32), pltpu.VMEM((2, 8, 1024), F32),
            dma((17, 12)), dma((17, 12)), dma((49,)), dma((32,)), dma((2,)), dma((2,)),
        ],
        compiler_params=pltpu.CompilerParams(
            collective_id=0, has_side_effects=True, vmem_limit_bytes=62 * 2**20
        ),
    )(*args)


class Scatter:
    def __init__(self, grads, landing, plan, send, recv, give):
        self.grads = grads
        self.landing = landing
        self.send = send
        self.recv = recv
        self.give = give
        self.at = place()
        self.sent = {}
        self.items = []
        self.plan = [list(row) for row in plan]

    def own(self, item, z, x, y, c, h):
        kind, l, part = item
        w4, up, dn, vec = self.grads
        if kind == "vec":
            return vec.at[z, x, y, c, h]
        if kind == "gate":
            return w4.at[y, c, part, z, x, h]
        if kind == "up":
            return up.at[l, part, h, z, x, y, c]
        return dn.at[l, z, x, y, c, part, h]

    def land(self, item, stage, *where):
        kind, l, part = item
        ref = self.landing[("gate", "up", "down", "vec").index(kind)][stage]
        where = where if kind == "vec" else (l, part, *where)
        return ref.at[where] if where else ref

    def copy(self, n, slot, src, dst, target):
        return pltpu.make_async_remote_copy(
            src_ref=src,
            dst_ref=dst,
            send_sem=self.send.at[n, slot],
            recv_sem=self.recv.at[n, slot],
            device_id=target,
            device_id_type=MESH,
        )

    def go(self, n, slot, src, dst, target):
        cp = self.copy(n, slot, src, dst, target)
        cp.start()
        self.sent.setdefault(n, []).append(cp)

    def landed(self, n, slot, dst, source):
        self.copy(n, slot, dst, dst, source).wait_recv()

    def add(self, item, stage):
        z, x, y, c = self.at
        kind = item[0]

        def plus(there, *where):
            there[...] = there[...] + self.land(item, stage, *where)[...]

        @pl.loop(0, 4)
        def _(n):
            if stage == 0:
                for i in range(2):
                    for j in range(2):
                        for h in range(2):
                            if kind == "gate":
                                plus(self.own(item, n, j, i, c, h), i, n, j, h)
                            elif kind == "up":
                                plus(self.own(item, n, i, j, c, h), h, n, i, j)
                            else:
                                plus(self.own(item, n, i, j, c, h), n, i, j, h)
            elif stage == 1:
                for i in range(2):
                    plus(self.own(item, n, i, y, c, 0), n, i)
            elif stage == 2:
                for i in range(2):
                    plus(self.own(item, n, x, i, c, 1), *((i, n) if kind == "gate" else (n, i)))
            else:
                for h in range(2):
                    plus(self.own(item, n, x, y, c, h), h, n)

    def total(self, item, h):
        z, x, y, c = self.at
        v = self.own(item, z, x, y, c, h)[...].astype(F32)
        for j in range(3):
            v = v + self.land(item, 4, j, h)[...].astype(F32)
        return v

    def stage(self, step, n, item):
        z, x, y, c = self.at
        v = lambda *where: self.own(item, *where)
        to_x = device(z, 1 - x, y, c)
        to_y = device(z, x, 1 - y, c)
        to_c = device(z, x, y, 1 - c)
        land = lambda *w: self.land(item, *w)
        if step == 0:
            self.go(n, 0, v(ALL, ALL, ALL, 1 - c, ALL), land(0), to_c)
        elif step == 1:
            self.landed(n, 0, land(0), to_c)
            self.add(item, 0)
            self.go(n, 1, v(ALL, ALL, 1 - y, c, 0), land(1), to_y)
            self.go(n, 2, v(ALL, 1 - x, ALL, c, 1), land(2), to_x)
        elif step == 2:
            self.landed(n, 1, land(1), to_y)
            self.add(item, 1)
            self.go(n, 3, v(ALL, 1 - x, y, c, 0), land(3, 0), to_x)
            self.landed(n, 2, land(2), to_x)
            self.add(item, 2)
            self.go(n, 4, v(ALL, x, 1 - y, c, 1), land(3, 1), to_y)
        elif step == 3:
            self.landed(n, 3, land(3, 0), to_x)
            self.landed(n, 4, land(3, 1), to_y)
            self.add(item, 3)
            for k in (1, 2, 3):
                there = lax.rem(z + k, 4)
                self.go(n, 4 + k, v(there, x, y, c, ALL), land(4, k - 1), device(there, x, y, c))
        else:
            for k in (1, 2, 3):
                source = lax.rem(z + 4 - k, 4)
                self.landed(n, 4 + k, land(4, k - 1), device(source, x, y, c))
            self.give(item, self)

    def go_on(self):
        for code in self.plan.pop(0):
            n, step = divmod(code, 5)
            self.stage(step, n, self.items[n])

    def settle(self, numbers):
        for n in numbers:
            for cp in self.sent.pop(n):
                cp.wait_send()


def spread_back(g, first, size, total, per_mp):
    r = lax.broadcasted_iota(jnp.int32, (32, total), 0)
    d = lax.broadcasted_iota(jnp.int32, (32, total), 1)
    if per_mp:
        owner = lax.div(lax.rem(d, total // 4), size) * 4 + lax.div(d, total // 4)
    else:
        owner = lax.div(d, size)
    rows = jnp.where(r == owner, g, 0.0)
    d = lax.broadcasted_iota(jnp.int32, (total, 128), 0)
    j = lax.broadcasted_iota(jnp.int32, (total, 128), 1)
    pick = jnp.where(j == first + lax.rem(d, size), 1.0, 0.0).astype(BF)
    high = rows.astype(BF)
    rest = rows - high.astype(F32)
    middle = rest.astype(BF)
    low = (rest - middle.astype(F32)).astype(BF)
    return dot(high, pick) + dot(middle, pick) + dot(low, pick)


def bwd_kernel(
    ct_in, w4_in, up_in, dn_in, gain_in, stream_in, mixed_in, keep_in, q_in, hid_in, ff_in, turned_in,
    grad_hbm, gate_hbm, out_hbm, up_hbm, down_hbm, vec_hbm,
    w4, up, dn, gain, keep, pre, mixed, ff, grad, acc, low, low_t, act_t, up_low, sg, c_out, c_in,
    ends, enter, gains, biases, g_w4, g_up, g_dn, g_vec,
    lw0, lw1, lw2, lw3, lw4, lu0, lu1, lu2, lu3, lu4, ld0, ld1, ld2, ld3, ld4, lv0, lv1, lv2, lv3, lv4,
    f_w4, f_up, f_dn, f_vec,
    rs_send, rs_recv, load_sem, save_sem, carry_send, carry_recv,
):
    z, x, y, c = place()
    mp = y * 2 + c
    rows_all = low.shape[0]
    chunks = rows_all // ROWS
    loads = {}
    n_load = 0
    saves = []

    def load(key, src, dst):
        nonlocal n_load
        cp = pltpu.make_async_copy(src, dst, load_sem.at[n_load])
        cp.start()
        loads[key] = cp
        n_load += 1

    def ready(key):
        loads.pop(key).wait()

    def save(src, dst):
        cp = pltpu.make_async_copy(src, dst, save_sem.at[len(saves)])
        cp.start()
        saves.append(cp)

    def load_feed(l):
        load("dn", dn_in.at[l], dn)
        load("up", up_in.at[l], up)

    def load_chunk(l, q):
        load(("ff", q), ff_in.at[l, q], ff.at[q % 2])

    def load_gates(l):
        load("w4", w4_in.at[l], w4)
        load("keep", keep_in.at[l], keep)
        load("q", q_in.at[l], pre.at[:, pl.ds(0, 2)])

    load("ct", ct_in, low)
    load("gain", gain_in, gain)
    load_feed(1)
    load_chunk(1, 0)
    load("act_t", turned_in.at[1, 1], act_t.at[pl.ds(0, 512)])
    load("mixed", mixed_in.at[1], mixed)
    load_chunk(1, 1)
    load_gates(1)
    greet(wait=False)

    def give(item, scatter):
        kind, l, part = item
        if kind == "gate":
            for h in range(2):
                f_w4[l, part, h] = scatter.total(item, h)
            save(f_w4.at[l, part], gate_hbm.at[l, part] if part < 3 else out_hbm.at[l])
        elif kind == "up":
            for h in range(2):
                f_up[l, part, h] = scatter.total(item, h)
                save(f_up.at[l, part, h], up_hbm.at[l, :, pl.ds((part * 2 + h) * 512, 512)])
        elif kind == "down":
            for h in range(2):
                f_dn[l, part, h] = scatter.total(item, h)
            save(f_dn.at[l, part], down_hbm.at[l, part])
        else:
            for h in range(2):
                f_vec[h] = scatter.total(item, h)
            save(f_vec, vec_hbm)

    landing = (
        (lw0, lw1, lw2, lw3, lw4), (lu0, lu1, lu2, lu3, lu4), (ld0, ld1, ld2, ld3, ld4), (lv0, lv1, lv2, lv3, lv4),
    )
    scatter = Scatter((g_w4, g_up, g_dn, g_vec), landing, SCATTER_PLAN, rs_send, rs_recv, give)
    go_on = scatter.go_on

    def push(*item):
        scatter.items.append(item)

    def each(fn):
        @pl.loop(0, chunks)
        def _(i):
            fn(i, pl.ds(pl.multiple_of(i * ROWS, ROWS), ROWS))

    def feed(l, q):
        slot = q % 2
        w_down = dn[q].reshape(512, 512)
        w_up = up[q // 2, q % 2].reshape(512, 512)

        def part(i, r):
            act_grad = dot_nt(low[r, :], w_down)
            slope = jnp.concatenate([ff[slot, 0, r, :], ff[slot, 1, r, :]], axis=1).astype(F32)
            u = (act_grad * slope).astype(BF)
            up_low[r, :] = u
            back = dot_nt(u, w_up)
            acc[r, :] = back if q == 0 else acc[r, :] + back

        each(part)
        go_on()
        for half in range(2):
            g = dot(act_t[half * 256 : half * 256 + 256, :], up_low[...]).astype(BF)
            g_up[l, q // 2, q % 2, half * 2 : half * 2 + 2] = g.reshape(2, 2, 2, 2, 16, 512)
        for half in range(2):
            g = dot_tn(ff[slot, 2 + half], low[...]).astype(BF)
            g_dn[l, q, half] = g.reshape(2, 2, 2, 2, 16, 512)

    def rms_back(l, which, src, values_t):
        g = gain[l, which : which + 1, :]
        gains[l, which : which + 1, :] = jnp.zeros((1, 512), F32)

        def part(i, r):
            v = src[r, :]
            scale = lax.rsqrt(jnp.mean(v * v, axis=-1, keepdims=True) + eps)
            u = v * scale
            d = acc[r, :]
            gains[l, which : which + 1, :] += jnp.sum(d * u, axis=0, keepdims=True)
            dg = d * g
            new = grad[r, :] + scale * (dg - u * jnp.mean(dg * u, axis=-1, keepdims=True))
            grad[r, :] = new
            new = new.astype(BF)
            low[r, :] = new
            if values_t is not None:
                values_t[:, r] = new.T

        each(part)

    def out_back(p):
        g = dot(low_t[...], ff[0, p]).astype(BF)
        g_w4[p // 2, p % 2, 3] = g.reshape(4, 2, 2, 32, 256)

    def states_back(p):
        w = w4[p // 2, p % 2, 3].reshape(512, 256)

        def part(i, r):
            v = dot(low[r, :], w)
            share = keep[p, r, :]
            decay = 1.0 - share
            t = slice(ROWS - 8, ROWS)
            adjoint = v[t]
            parts = [adjoint]
            a = decay[t]
            passed = a * adjoint
            for j in range(STEPS - 2, -1, -1):
                t = slice(j * 8, j * 8 + 8)
                adjoint = v[t] + passed
                passed = decay[t] * adjoint
                a = a * decay[t]
                parts.append(adjoint)
            whole = jnp.concatenate(parts[::-1], axis=0)
            for n in range(2):
                sg[p * 2 + n, r, :] = whole[:, n * 128 : n * 128 + 128]
            columns = slice(p * 256, p * 256 + 256)
            ends[0, i, :, columns] = a
            ends[1, i, :, columns] = passed

        each(part)

    row = lax.broadcasted_iota(jnp.int32, (8, 1024), 0)
    first_chunk = first_of(mp, rows_all)

    def carries(entering):
        for i in range(chunks - 1, -1, -1):
            c0 = jnp.where(first_chunk == i + 1, 0.0, entering)
            a, v = combine(ends[0, i], ends[1, i], row, -1)
            enter[i] = jnp.where(row == 7, c0, pltpu.roll(a, 7, 0) * c0 + pltpu.roll(v, 7, 0))
            entering = jnp.broadcast_to(a[0:1] * c0[0:1] + v[0:1], (8, 1024))
        return entering

    def carry_copy(l, there):
        return pltpu.make_async_remote_copy(
            src_ref=c_out.at[l],
            dst_ref=c_in.at[l],
            send_sem=carry_send.at[l],
            recv_sem=carry_recv.at[l],
            device_id=device(z, x, lax.div(there, 2), lax.rem(there, 2)),
            device_id_type=MESH,
        )

    def carry_out(l):
        c_out[l] = carries(jnp.zeros((8, 1024), F32))

        @pl.when(mp > 0)
        def _():
            carry_copy(l, jnp.maximum(mp - 1, 0)).start()

    def carry_into(l):
        @pl.when(mp < 3)
        def _():
            carry_copy(l, jnp.minimum(mp + 1, 3)).wait_recv()
            carries(c_in[l])

        @pl.when(mp > 0)
        def _():
            carry_copy(l, jnp.maximum(mp - 1, 0)).wait_send()

    def pre_back(p):
        def part(i, r):
            share = keep[p, r, :]
            local = jnp.concatenate([sg[p * 2, r, :], sg[p * 2 + 1, r, :]], axis=1)
            weight = enter[i, :, p * 256 : p * 256 + 256]
            parts = []
            for j in range(STEPS - 1, -1, -1):
                t = slice(j * 8, j * 8 + 8)
                parts.append(local[t] + weight)
                if j:
                    weight = weight - share[t] * weight
            adjoint = jnp.concatenate(parts[::-1], axis=0)
            for k in range(3):
                v = share if k == 2 else pre[p, k, r, :].astype(F32)
                pre[p, k, r, :] = (adjoint * v).astype(BF)

        each(part)

    def normed_back(first):
        w = {(p, k): w4[p // 2, p % 2, k].reshape(512, 256) for p in (first, first + 1) for k in range(3)}

        def part(i, r):
            back = 0.0 if first == 0 else acc[r, :]
            for p, k in w:
                back = back + dot_nt(pre[p, k, r, :], w[p, k])
            acc[r, :] = back

        each(part)

    def gate_grads(l, k):
        for p in range(4):
            g = dot(act_t[...], pre[p, k])
            g_w4[p // 2, p % 2, k] = g[0:512].astype(BF).reshape(4, 2, 2, 32, 256)
            biases[l, k : k + 1, p * 256 : p * 256 + 256] = g[512:513]

    act_t[512:528, :] = jnp.ones((16, rows_all), BF)
    ready("ct")

    def widen(i, r):
        v = into_steps(low[r, :].astype(F32), sg, i)
        grad[r, :] = v
        low[r, :] = v.astype(BF)

    each(widen)
    ready("gain")
    for l in (1, 0):
        ready("act_t")
        go_on()
        ready("dn")
        ready("up")
        for q in range(4):
            ready(("ff", q))
            feed(l, q)
            if l == 1 and q == 0:
                greeted()
            if q < 2:
                load_chunk(l, q + 2)
            elif q == 2:
                load("hid", hid_in.at[l], ff.at[0])
            if q % 2 == 1:
                push("up", l, q // 2)
            go_on()
        push("down", l, 0)
        push("down", l, 1)
        go_on()
        load("act_t", turned_in.at[l, 0], act_t.at[pl.ds(0, 512)])
        ready("mixed")
        rms_back(l, 1, mixed, low_t)
        load("stream", stream_in.at[l], mixed)
        go_on()
        if l == 1:
            load_feed(0)
        else:
            go_on()
            scatter.settle(range(4, 8))
        ready("w4")
        ready("hid")
        for p in range(4):
            out_back(p)
        push("gate", l, 3)
        go_on()
        if l == 1:
            load_chunk(0, 0)
        ready("keep")
        for p in range(4):
            states_back(p)
            go_on()
        carry_out(l)
        go_on()
        ready("q")
        carry_into(l)
        for p in range(4):
            pre_back(p)
            if p % 2 == 1:
                go_on()
        ready("act_t")
        for k in range(3):
            gate_grads(l, k)
            push("gate", l, k)
            go_on()
        if l == 1:
            load("act_t", turned_in.at[0, 1], act_t.at[pl.ds(0, 512)])
        for first in (0, 2):
            normed_back(first)
            go_on()
        ready("stream")
        if l == 1:
            load_chunk(0, 1)
            load_gates(0)
        rms_back(l, 0, mixed, None)
        if l == 1:
            load("mixed", mixed_in.at[0], mixed)
        go_on()
        rows = spread_back(gains[l, 0:1, :], 0, 16, 512, False) + spread_back(gains[l, 1:2, :], 16, 16, 512, False)
        for k in range(3):
            rows = rows + spread_back(biases[l, k : k + 1, :], 32 + 32 * k, 32, 1024, True)
        for n in range(32):
            g_vec[n // 8, n // 4 % 2, n // 2 % 2, n % 2, l] = jnp.broadcast_to(rows[n : n + 1, :], (8, 128))
    push("vec", 0, 0)
    go_on()

    def finish(i, r):
        mixed[r, :] = unturn(grad[r, :], sg, i)

    each(finish)
    save(mixed, grad_hbm)
    go_on()
    scatter.settle([*range(4), *range(8, 17)])
    for cp in saves:
        cp.wait()


def backward(cotangent, kept):
    w4_all, up_all, dn_all, gain, stream, mixed, keep, q, hid, ff, turned = kept
    rows = cotangent.shape[0]
    any_space = pl.BlockSpec(memory_space=pl.ANY)
    s = jax.ShapeDtypeStruct
    dma = pltpu.SemaphoreType.DMA
    v = pltpu.VMEM
    args = (cotangent, w4_all, up_all, dn_all, gain, stream, mixed, keep, q, hid, ff, turned)
    grad, gates, out, up, down, vec = pl.pallas_call(
        bwd_kernel,
        name="backward",
        out_shape=(
            s((rows, 512), F32), s((2, 3, 2, 32, 256), F32), s((2, 2, 32, 256), F32), s((2, 16, 2048), F32),
            s((2, 2, 2, 16, 512), F32), s((2, 8, 128), F32),
        ),
        in_specs=[any_space] * len(args),
        out_specs=(any_space,) * 6,
        scratch_shapes=[
            v((2, 2, 4, 4, 2, 2, 32, 256), BF), v((2, 2, 4, 2, 2, 2, 16, 512), BF), v((4, 2, 2, 2, 2, 2, 16, 512), BF),
            v((2, 8, 512), F32), v((4, rows, 256), F32), v((4, 3, rows, 256), BF), v((rows, 512), F32),
            v((2, 4, rows, 256), BF), v((rows, 512), F32), v((rows, 512), F32), v((rows, 512), BF), v((512, rows), BF),
            v((528, rows), BF), v((rows, 512), BF), v((8, rows, 128), F32), v((2, 8, 1024), F32), v((2, 8, 1024), F32),
            v((2, 3, 8, 1024), F32), v((3, 8, 1024), F32), v((2, 8, 512), F32), v((2, 8, 1024), F32),
            v((2, 2, 4, 4, 2, 2, 32, 256), BF), v((2, 2, 2, 4, 2, 2, 2, 16, 512), BF), v((2, 4, 2, 2, 2, 2, 2, 16, 512), BF),
            v((4, 2, 2, 2, 2, 8, 128), F32),
            v((2, 4, 2, 4, 2, 2, 32, 256), BF), v((2, 4, 4, 2, 32, 256), BF), v((2, 4, 2, 4, 32, 256), BF),
            v((2, 4, 2, 4, 32, 256), BF), v((2, 4, 3, 2, 32, 256), BF),
            v((2, 2, 2, 4, 2, 2, 16, 512), BF), v((2, 2, 4, 2, 16, 512), BF), v((2, 2, 4, 2, 16, 512), BF),
            v((2, 2, 2, 4, 16, 512), BF), v((2, 2, 3, 2, 16, 512), BF),
            v((2, 2, 4, 2, 2, 2, 16, 512), BF), v((2, 2, 4, 2, 16, 512), BF), v((2, 2, 4, 2, 16, 512), BF),
            v((2, 2, 2, 4, 16, 512), BF), v((2, 2, 3, 2, 16, 512), BF),
            v((4, 2, 2, 2, 8, 128), F32), v((4, 2, 8, 128), F32), v((4, 2, 8, 128), F32), v((2, 4, 8, 128), F32),
            v((3, 2, 8, 128), F32),
            v((2, 4, 2, 32, 256), F32), v((2, 2, 2, 16, 512), F32), v((2, 2, 2, 16, 512), F32), v((2, 8, 128), F32),
            dma((17, 8)), dma((17, 8)), dma((32,)), dma((24,)), dma((2,)), dma((2,)),
        ],
        compiler_params=pltpu.CompilerParams(
            collective_id=1, has_side_effects=True, vmem_limit_bytes=63 * 2**20
        ),
    )(*args)
    return grad, gates, out, up, down, vec


def settle_kernel(*refs):
    vec, biases, gain_one, gain_two = refs[6], *refs[13:]
    for src, dst in zip(refs[:6], refs[7:13]):
        dst[...] = src[...]
    for l in range(2):
        gain_one[l : l + 1, :] = vec[l, 0:1, 0:16]
        gain_two[l : l + 1, :] = vec[l, 0:1, 16:32]
        for k in range(3):
            biases[k, l : l + 1, :] = vec[l, 0:1, 32 + 32 * k : 64 + 32 * k]


def settle(result, grad, gates, out, up, down, vec):
    rows = result.shape[0]
    s = jax.ShapeDtypeStruct
    args = (
        result, grad, gates.reshape(12, 32, 256), out.reshape(4, 32, 256), up, down.reshape(8, 16, 512),
    )
    whole = lambda *shape: pl.BlockSpec(shape, lambda i: (0,) * len(shape))
    blocks = [
        pl.BlockSpec((rows // 2, 512), lambda i: (i, 0)),
        pl.BlockSpec((rows // 2, 512), lambda i: (i, 0)),
        pl.BlockSpec((6, 32, 256), lambda i: (i, 0, 0)),
        pl.BlockSpec((2, 32, 256), lambda i: (i, 0, 0)),
        pl.BlockSpec((2, 16, 1024), lambda i: (0, 0, i)),
        pl.BlockSpec((4, 16, 512), lambda i: (i, 0, 0)),
    ]
    result, grad, gates, out, up, down, biases, gain_one, gain_two = pl.pallas_call(
        settle_kernel,
        name="settle",
        grid=(2,),
        out_shape=tuple(s(v.shape, v.dtype) for v in args) + (s((3, 2, 32), F32), s((2, 16), F32), s((2, 16), F32)),
        in_specs=blocks + [whole(2, 8, 128)],
        out_specs=tuple(blocks) + (whole(3, 2, 32), whole(2, 16), whole(2, 16)),
    )(*args, vec)
    return (
        result,
        grad,
        gates.reshape(2, 3, 64, 256),
        biases.transpose(1, 0, 2),
        out.reshape(2, 64, 256).transpose(0, 2, 1),
        gain_one,
        gain_two,
        up,
        down.reshape(2, 64, 512),
    )


def fits(inputs, gate_weight, gate_bias, out_weight, gain_one, gain_two, up_weight, down_weight):
    rows = inputs.shape[0]
    shapes = (gate_weight.shape, gate_bias.shape, out_weight.shape, gain_one.shape, up_weight.shape, down_weight.shape)
    planned = ((2, 3, 64, 256), (2, 3, 32), (2, 256, 64), (2, 16), (2, 16, 2048), (2, 64, 512))
    axes = (lax.axis_size("dp"), lax.axis_size("mp"))
    return axes == (8, 4) and shapes == planned and rows == 768 and 4 * rows == 3 * LENGTH


def general_body(
    inputs,
    gate_weight,
    gate_bias,
    out_weight,
    norm_gain_one,
    norm_gain_two,
    up_weight,
    down_weight,
    cotangent,
):
    own_rows = inputs.shape[0]
    group = own_rows * lax.axis_size("mp")
    starts = (jnp.arange(group, dtype=jnp.int32) % LENGTH == 0)[:, None]
    layer_count = gate_weight.shape[0]
    width = gate_weight.shape[3]
    stream = inputs.astype(jnp.float32)
    saved = []
    held = []
    for layer_no in range(layer_count):
        gates_full, bias_full, out_full = (
            lax.all_gather(gate_weight[layer_no], "dp", axis=1, tiled=True),
            lax.all_gather(gate_bias[layer_no], "dp", axis=1, tiled=True),
            lax.all_gather(out_weight[layer_no], "dp", axis=1, tiled=True),
        )
        up_full, down_full, gain_first, gain_second = (
            lax.all_gather(up_weight[layer_no], ("dp", "mp"), axis=0, tiled=True),
            lax.all_gather(down_weight[layer_no], ("dp", "mp"), axis=0, tiled=True),
            lax.all_gather(norm_gain_one[layer_no], ("dp", "mp"), axis=0, tiled=True),
            lax.all_gather(norm_gain_two[layer_no], ("dp", "mp"), axis=0, tiled=True),
        )
        gain_first = gain_first.astype(jnp.float32)
        gain_second = gain_second.astype(jnp.float32)
        normed = rms_scale(stream, gain_first).astype(jnp.bfloat16)
        normed_all = lax.all_gather(normed, "mp", axis=0, tiled=True)
        pre_acts = (
            jnp.einsum("td,kdf->ktf", normed_all, gates_full, preferred_element_type=jnp.float32)
            + bias_full.astype(jnp.float32)[:, None, :]
        )
        decay, drive = gate_terms(pre_acts, starts)
        products, states = lax.associative_scan(link, (decay, drive), axis=0)
        hidden = states.astype(jnp.bfloat16)
        mixed = stream + lax.psum_scatter(
            dot_plain(hidden, out_full).astype(jnp.bfloat16), "mp", scatter_dimension=0, tiled=True
        ).astype(jnp.float32)
        second = rms_scale(mixed, gain_second).astype(jnp.bfloat16)
        up_acts = dot_plain(second, up_full)
        activated = jax.nn.gelu(up_acts).astype(jnp.bfloat16)
        saved.append(
            {
                "stream": stream,
                "gain_first": gain_first,
                "gain_second": gain_second,
                "normed": normed_all,
                "pre": pre_acts,
                "decay": decay,
                "states": states,
                "hidden": hidden,
                "mixed": mixed,
                "second": second,
                "up_acts": up_acts,
                "activated": activated,
            }
        )
        held.append((gates_full, out_full, up_full, down_full))
        stream = mixed + dot_plain(activated, down_full)
    grad = cotangent.astype(jnp.float32)
    gate_parts = []
    mlp_parts = []
    for layer_no in reversed(range(layer_count)):
        kept = saved[layer_no]
        gates_full, out_full, up_full, down_full = held[layer_no]
        grad_low = grad.astype(jnp.bfloat16)
        act_grad = dot_last(grad_low, down_full)
        down_grad = dot_first(kept["activated"], grad_low)
        unused_gelu, gelu_back = jax.vjp(jax.nn.gelu, kept["up_acts"])
        up_low = gelu_back(act_grad)[0].astype(jnp.bfloat16)
        up_grad = dot_first(kept["second"], up_low)
        second_grad = dot_last(up_low, up_full)
        unused_norm, norm_back = jax.vjp(rms_scale, kept["mixed"], kept["gain_second"])
        mixed_part, gain_two_grad = norm_back(second_grad)
        mixed_grad = grad + mixed_part
        mixed_low = mixed_grad.astype(jnp.bfloat16)
        mixed_all = lax.all_gather(mixed_low, "mp", axis=0, tiled=True)
        state_grad = dot_last(mixed_all, out_full)
        out_grad = dot_first(kept["hidden"], mixed_all)
        decay = kept["decay"]
        shifted = jnp.concatenate([decay[1:], jnp.ones((1, width), jnp.float32)], axis=0)
        back_products, back_partial = lax.associative_scan(
            link, (shifted[::-1], state_grad[::-1]), axis=0
        )
        adjoint = back_partial[::-1]
        previous = jnp.concatenate(
            [jnp.zeros((1, width), jnp.float32), kept["states"][:-1]], axis=0
        )
        unused_gate, gate_back = jax.vjp(partial(gate_terms, starts=starts), kept["pre"])
        pre_low = gate_back((adjoint * previous, adjoint))[0].astype(jnp.bfloat16)
        bias_grad = jnp.sum(pre_low.astype(jnp.float32), axis=1)
        gate_grad = jnp.einsum(
            "td,ktf->kdf", kept["normed"], pre_low, preferred_element_type=jnp.float32
        )
        normed_part = jnp.einsum(
            "ktf,kdf->td", pre_low, gates_full, preferred_element_type=jnp.float32
        )
        normed_grad = lax.psum_scatter(
            normed_part.astype(jnp.bfloat16), "mp", scatter_dimension=0, tiled=True
        ).astype(jnp.float32)
        unused_first, first_back = jax.vjp(rms_scale, kept["stream"], kept["gain_first"])
        stream_part, gain_one_grad = first_back(normed_grad)
        grad = mixed_grad + stream_part
        gate_parts.append(
            (
                sum_at_owner(gate_grad.astype(jnp.bfloat16), "dp", 1),
                sum_at_owner(bias_grad.astype(jnp.bfloat16), "dp", 1),
                sum_at_owner(out_grad.astype(jnp.bfloat16), "dp", 1),
            )
        )
        mlp_parts.append(
            (
                lax.psum_scatter(up_grad, ("dp", "mp"), scatter_dimension=0, tiled=True),
                lax.psum_scatter(down_grad, ("dp", "mp"), scatter_dimension=0, tiled=True),
                lax.psum_scatter(gain_one_grad, ("dp", "mp"), scatter_dimension=0, tiled=True),
                lax.psum_scatter(gain_two_grad, ("dp", "mp"), scatter_dimension=0, tiled=True),
            )
        )
    gate_parts = gate_parts[::-1]
    mlp_parts = mlp_parts[::-1]
    gate_stack = tuple((jnp.stack([entry[member] for entry in gate_parts]) for member in range(3)))
    mlp_stack = tuple((jnp.stack([entry[member] for entry in mlp_parts]) for member in range(4)))
    return (
        stream.astype(jnp.bfloat16),
        grad,
        gate_stack[0],
        gate_stack[1],
        gate_stack[2],
        mlp_stack[2],
        mlp_stack[3],
        mlp_stack[0],
        mlp_stack[1],
    )


def body(inputs, gate_weight, gate_bias, out_weight, gain_one, gain_two, up_weight, down_weight, cotangent):
    shards = (gate_weight, gate_bias, out_weight, gain_one, gain_two, up_weight, down_weight)
    if not fits(inputs, *shards):
        return general_body(inputs, *shards, cotangent)
    out, *kept = forward(inputs, *shards)
    return settle(out, *backward(cotangent, kept))


def solution(mesh):
    placed = (
        P(("dp", "mp"), None),
        P(None, None, "dp", "mp"),
        P(None, None, ("mp", "dp")),
        P(None, "mp", "dp"),
        P(None, ("dp", "mp")),
        P(None, ("dp", "mp")),
        P(None, ("dp", "mp"), None),
        P(None, ("dp", "mp"), None),
        P(("dp", "mp"), None),
    )
    return jax.shard_map(
        body,
        mesh=mesh,
        in_specs=placed,
        out_specs=(
            P(("dp", "mp"), None),
            P(("dp", "mp"), None),
            P(None, None, "dp", "mp"),
            P(None, None, ("mp", "dp")),
            P(None, "mp", "dp"),
            P(None, ("dp", "mp")),
            P(None, ("dp", "mp")),
            P(None, ("dp", "mp"), None),
            P(None, ("dp", "mp"), None),
        ),
        check_vma=False,
    )
```
